32 devices in a mesh: groups: 2 (over y), dp: 4 (over z), section: 2 (over x), mp: 2 (over core).
Axes of the slice: x: 2, y: 2, z: 4, core: 2. Of those that a mesh axis runs over, the one named last changes fastest.
Arguments:
- hidden_in: bfloat16 [2, 8, 128, 2560], P('section', ('groups', 'dp'), None, 'mp'), parts along dimension 1, may hold values from -6 to 6
- attn_out: bfloat16 [2, 8, 128, 2560], P('section', ('groups', 'dp'), None, 'mp'), parts along dimension 1, may hold values from -5 to 5
- queries: bfloat16 [2, 8, 128, 2560], P('section', ('groups', 'dp'), None, 'mp'), parts along dimension 1, may hold values from -72 to 72
- keys: bfloat16 [2, 8, 128, 512], P('section', ('groups', 'dp'), None, 'mp'), parts along dimension 1, may hold values from -5 to 5
- value_weight: bfloat16 [2, 2560, 512], P('section', 'mp'), may hold values from -0.125 to 0.125
- out_weight: bfloat16 [2, 2560, 2560], P('section', 'mp', 'dp'), may hold values from -0.125 to 0.125
- lengths: int32 [8], P(('groups', 'dp')), parts along dimension 0, may hold values from 32 to 128, as said below
Outputs:
- heat: float32 [2, 8, 128], P('section', ('groups', 'dp')), parts along dimension 1
- weight_relevance: float32 [4, 2560, 512], P(('groups', 'section'), ('mp', 'dp')), parts along dimension 0
The draws below stay inside these ranges and needn't reach their ends.
There are 2 independent parts, one for each index of `groups`. The reference program is written for one: setup_inputs(seed, part) draws one part's arguments, and reference() takes and returns one part's arrays. A program takes and returns all parts, laid end to end along the dimension named above; an argument that names none is the same for every part. Nothing has to cross between parts.
Inputs may be any that keep to these rules, and one draw needn't show every extreme that they name: `lengths`: the valid length of each reference sequence; positions at or past it are padding.
All inputs are finite; a program needn't handle non-finite values.
Results may differ from the reference program's by a relative error of at most 0.035.
Values may be sent and summed in bfloat16 or wider, within the bound.
No kernel may reach another device: no remote copies, remote signals or barrier semaphores. Data moves between devices by JAX's collectives and lax.ppermute only.
A program may use at most 64 MiB of HBM per device.

```python
import math
import jax
import jax.numpy as jnp
from jax import lax

DW = 2560
HD = 128
QH = 20
KVH = 4
L = 128
SECTIONS = 2
SEQS = 4


def queries_keys(key):
    folded = jax.random.fold_in(key, 31)
    key_query, key_key = jax.random.split(folded, 2)
    group_size = QH // KVH
    keys_base = jnp.clip(jax.random.normal(key_key, (SECTIONS, SEQS, L, KVH, HD), jnp.float32), -4.0, 4.0)
    query_base = jnp.clip(jax.random.normal(key_query, (SECTIONS, SEQS, L, KVH, group_size, HD), jnp.float32), -4.0, 4.0)
    return (query_base.reshape(SECTIONS, SEQS, L, QH * HD), keys_base.reshape(SECTIONS, SEQS, L, KVH * HD))


def draw_queries(key, part):
    return queries_keys(key)[0].astype(jnp.bfloat16)


def draw_keys(key, part):
    return queries_keys(key)[1].astype(jnp.bfloat16)


def draw_lengths(key, part):
    key_length, key_spot = jax.random.split(jax.random.fold_in(key, 11))
    length_draw = jax.random.randint(key_length, (SEQS,), L // 4, L + 1)
    spot_order = jax.random.permutation(key_spot, SEQS)
    length_draw = jnp.where(spot_order == 0, L, length_draw)
    return jnp.where(spot_order == 1, L // 4, length_draw).astype(jnp.int32)


def level_of(key, shape, shards, least, high):
    gain = 1.0
    for axis_at, blocks in shards:
        heights = jax.random.uniform(jax.random.fold_in(jax.random.fold_in(key, 6), axis_at), (blocks,), jnp.float32, least / len(shards), high / len(shards))
        gain = gain * jnp.repeat(jnp.exp(heights), shape[axis_at] // blocks).reshape((-1,) + (1,) * (len(shape) - 1 - axis_at))
    return gain


def normal_values(rng, extent, spread, reach, pieces=(), kind=jnp.bfloat16):
    values = jax.random.normal(rng, extent, jnp.float32) * spread
    if len(pieces) > 0:
        values = level_of(rng, extent, pieces, -0.22, 0.18) * values
    return jnp.clip(values, min=-reach, max=reach).astype(kind)


def setup_inputs(seed: int = 0, part: int = 0) -> dict:
    splits = jax.random.split(jax.random.key(seed), 8)
    part_keys = jax.random.split(jax.random.fold_in(splits[7], part), 8)
    hidden_in = normal_values(part_keys[0], (SECTIONS, SEQS, L, DW), 1.0, 6.0, ((0, 2), (1, 4), (3, 2)))
    attn_out = normal_values(part_keys[1], (SECTIONS, SEQS, L, DW), 0.7, 5.0, ((0, 2), (1, 4), (3, 2)))
    queries = draw_queries(jax.random.fold_in(jax.random.fold_in(splits[7], part), 71), part)
    keys = draw_keys(jax.random.fold_in(jax.random.fold_in(splits[7], part), 71), part)
    value_weight = normal_values(splits[4], (SECTIONS, DW, KVH * HD), DW ** -0.5, 0.125, ((0, 2), (1, 2)))
    out_weight = normal_values(splits[5], (SECTIONS, QH * HD, DW), (QH * HD) ** -0.5, 0.125, ((0, 2), (1, 2), (2, 4)))
    lengths = draw_lengths(jax.random.fold_in(jax.random.fold_in(splits[7], part), 71), part)
    return dict(hidden_in=hidden_in, attn_out=attn_out, queries=queries, keys=keys, value_weight=value_weight, out_weight=out_weight, lengths=lengths)


EPS = 0.25

def stabilize(entries):
    return jnp.where(entries >= 0, entries + EPS, entries - EPS)

def section_rule(inputs, branch, query_rows, key_rows, length, incoming, value_rows, out_rows):
    group_size = QH // KVH
    seq_len = inputs.shape[0]
    inputs_f = inputs.astype(jnp.float32)
    branch_f = branch.astype(jnp.float32)
    totals = inputs_f + branch_f
    values_bf = lax.optimization_barrier(jnp.dot(inputs, value_rows, preferred_element_type=jnp.float32).astype(jnp.bfloat16))
    values_f = values_bf.astype(jnp.float32)
    query_heads = query_rows.astype(jnp.float32).reshape(seq_len, KVH, group_size, HD)
    key_heads = key_rows.astype(jnp.float32).reshape(seq_len, KVH, HD)
    scores = jnp.einsum('tgjd,sgd->gjts', query_heads, key_heads) / math.sqrt(HD)
    position = jnp.arange(seq_len, dtype=jnp.int32)
    allowed = (position[None, :] <= position[:, None]) & (position[None, :] < length)
    scores = jnp.where(allowed, scores, -1000000000.0)
    row_top = lax.optimization_barrier(jnp.max(scores, axis=-1, keepdims=True))
    weights = jnp.exp(scores - row_top)
    prob_rows = (weights / lax.optimization_barrier(jnp.sum(weights, axis=-1, keepdims=True))).astype(jnp.bfloat16)
    prob_f = prob_rows.astype(jnp.float32)
    mixed_heads = jnp.einsum('gjts,sgd->tgjd', prob_f, values_f.reshape(seq_len, KVH, HD)).reshape(seq_len, QH * HD)
    sens_total = incoming.astype(jnp.float32) / stabilize(totals)
    kept = inputs_f * sens_total
    sens_branch = (branch_f * sens_total / stabilize(branch_f)).astype(jnp.bfloat16)
    back_mixed = jnp.dot(sens_branch, out_rows.T, preferred_element_type=jnp.float32)
    sens_mixed = (mixed_heads * back_mixed / stabilize(mixed_heads)).astype(jnp.bfloat16)
    back_values = jnp.einsum('gjts,tgjd->sgd', prob_f, sens_mixed.astype(jnp.float32).reshape(seq_len, KVH, group_size, HD)).reshape(seq_len, KVH * HD)
    sens_values = (values_f * back_values / stabilize(values_f)).astype(jnp.bfloat16)
    back_inputs = jnp.dot(sens_values, value_rows.T, preferred_element_type=jnp.float32)
    outgoing = (kept + inputs_f * back_inputs).astype(jnp.bfloat16)
    return (outgoing, sens_values)

def reference(hidden_in, attn_out, queries, keys, value_weight, out_weight, lengths):
    vmapped = jax.vmap(section_rule, in_axes=(0, 0, 0, 0, 0, 0, None, None))
    position = jnp.arange(L, dtype=jnp.int32)
    valid_rows = (position[None, :] < lengths[:, None]).astype(jnp.float32)
    total_last = hidden_in[SECTIONS - 1].astype(jnp.float32) + attn_out[SECTIONS - 1].astype(jnp.float32)
    incoming = (total_last * valid_rows[:, :, None]).astype(jnp.bfloat16)
    heat_list = [None] * SECTIONS
    weight_list = [None] * SECTIONS
    for section_pos in range(SECTIONS - 1, -1, -1):
        outgoing, sens_values = vmapped(hidden_in[section_pos], attn_out[section_pos], queries[section_pos], keys[section_pos], lengths, incoming, value_weight[section_pos], out_weight[section_pos])
        heat_list[section_pos] = lax.optimization_barrier(jnp.sum(outgoing.astype(jnp.float32), axis=-1)) / DW
        summed = jnp.einsum('btc,btk->ck', hidden_in[section_pos].astype(jnp.float32), sens_values.astype(jnp.float32))
        weight_list[section_pos] = value_weight[section_pos].astype(jnp.float32) * summed
        incoming = outgoing
    return (jnp.stack(heat_list), jnp.stack(weight_list))
```

```python
import math

import jax
import jax.numpy as jnp
from jax import lax
from jax.sharding import PartitionSpec as P

DW = 2560
HD = 128
QH = 20
KVH = 4
EPS = 0.25
F32 = jnp.float32
BF16 = jnp.bfloat16


def stabilize(entries):
    return jnp.where(entries >= 0, entries + EPS, entries - EPS)


def cycled(shard, axis, by):
    peers = lax.axis_size(axis)
    return lax.ppermute(shard, axis, [(i, (i + by) % peers) for i in range(peers)])


def shifted(shard, axis, by):
    peers = lax.axis_size(axis)
    return lax.ppermute(
        shard, axis, [(i, i + by) for i in range(peers) if 0 <= i + by < peers]
    )


def from_next_section(shard, flip=False):
    sections = lax.axis_size("section")
    cores = lax.axis_size("mp")
    pairs = []
    for s in range(1, sections):
        for c in range(cores):
            d = (c + 1) % cores if flip else c
            pairs.append((s * cores + c, (s - 1) * cores + d))
    return lax.ppermute(shard, ("section", "mp"), pairs)


def gather_blocks(mine, axis):
    peers = lax.axis_size(axis)
    pos = lax.axis_index(axis)
    low = pos < peers // 2
    longer = jnp.where(low, peers - 1 - pos, pos)
    up, down = [mine], [mine]
    for _ in range(1, peers):
        up.append(shifted(up[-1], axis, 1))
        down.append(shifted(down[-1], axis, -1))
    slots = []
    for j in range(1, peers):
        block = jnp.where(low, down[j], up[j])
        owner = jnp.where(low, pos + j, pos - j)
        for k in range(1, min(j, (peers - 1) // 2) + 1):
            here = j - longer == k
            block = jnp.where(here, jnp.where(low, up[k], down[k]), block)
            owner = jnp.where(here, jnp.where(low, pos - k, pos + k), owner)
        slots.append((block, owner))
    return slots


def on_device(hidden_in, attn_out, queries, keys, value_weight, out_weight, lengths):
    inputs = hidden_in[0, 0]
    branch = attn_out[0, 0]
    query_rows = queries[0, 0]
    key_rows = keys[0, 0]
    value_rows = value_weight[0]
    out_block = out_weight[0]
    seq_len, half_width = inputs.shape
    group_size = QH // KVH
    local_kv = key_rows.shape[1] // HD
    kv_width = local_kv * HD
    sections = lax.axis_size("section")
    section_pos = lax.axis_index("section")
    groups = lax.axis_size("groups")
    group_pos = lax.axis_index("groups")
    peers = lax.axis_size("dp")
    dp_pos = lax.axis_index("dp")
    core_pos = lax.axis_index("mp")
    head_rows, block_width = out_block.shape

    share = head_rows // groups
    carried = lax.dynamic_slice_in_dim(out_block, group_pos * share, share, 0)
    slots = [(out_block, dp_pos)]
    for block, owner in gather_blocks(carried, "dp"):
        rows = [block] + [cycled(block, "groups", k) for k in range(1, groups)]
        whole = jnp.zeros((head_rows, block_width), BF16)
        if groups == 2:
            first = jnp.where(group_pos == 0, rows[0], rows[1])
            second = jnp.where(group_pos == 0, rows[1], rows[0])
            whole = jnp.concatenate([first, second], 0)
        else:
            for k in range(groups):
                at = lax.rem(group_pos - k + groups, groups) * share
                whole = lax.dynamic_update_slice_in_dim(whole, rows[k], at, 0)
        slots.append((whole, owner))

    behind_inputs = from_next_section(inputs).astype(F32)
    behind_values = from_next_section(value_rows)

    inputs_f = inputs.astype(F32)
    branch_f = branch.astype(F32)
    totals = inputs_f + branch_f
    inv_totals = 1.0 / stabilize(totals)
    kept_gain = inputs_f * inv_totals
    branch_gain = branch_f * inv_totals / stabilize(branch_f)

    value_part = jnp.dot(inputs, value_rows, preferred_element_type=F32)
    part_mine = lax.dynamic_slice_in_dim(value_part, core_pos * kv_width, kv_width, 1)
    part_other = lax.dynamic_slice_in_dim(value_part, (1 - core_pos) * kv_width, kv_width, 1)
    values_f = part_mine + cycled(part_other.astype(BF16), "mp", 1).astype(F32)
    values_bf = values_f.astype(BF16)
    values_r = values_bf.astype(F32)
    value_gain = values_r / stabilize(values_r)

    query_heads = query_rows.reshape(seq_len, local_kv, group_size, HD)
    key_heads = key_rows.reshape(seq_len, local_kv, HD)
    scores = jnp.einsum(
        "tgjd,sgd->gjts", query_heads, key_heads, preferred_element_type=F32
    ) / math.sqrt(HD)
    position = lax.iota(jnp.int32, seq_len)
    allowed = (position[None, :] <= position[:, None]) & (position[None, :] < lengths[0])
    scores = jnp.where(allowed, scores, -1000000000.0)
    row_top = jnp.max(scores, axis=-1, keepdims=True)
    weights = jnp.exp(scores - row_top)
    prob_rows = (weights / jnp.sum(weights, axis=-1, keepdims=True)).astype(BF16)
    mixed = jnp.einsum(
        "gjts,sgd->tgjd",
        prob_rows,
        values_bf.reshape(seq_len, local_kv, HD),
        preferred_element_type=F32,
    ).reshape(seq_len, local_kv * group_size * HD)
    mixed_gain = mixed / stabilize(mixed)

    valid_rows = (position < lengths[0]).astype(F32)
    current = (totals * valid_rows[:, None]).astype(BF16).astype(F32)
    sens_values = jnp.zeros((seq_len, kv_width), BF16)
    kept_sum = jnp.zeros((seq_len,), F32)
    for turn in range(sections):
        last_turn = turn + 1 == sections
        active = section_pos == sections - 1 - turn
        kept = current * kept_gain
        if not last_turn:
            behind_kept = from_next_section(kept.astype(BF16))
        sens_branch = (current * branch_gain).astype(BF16)
        sens_other = cycled(sens_branch, "mp", 1)
        first = jnp.where(core_pos == 0, sens_branch, sens_other)
        second = jnp.where(core_pos == 0, sens_other, sens_branch)
        sens_full = jnp.concatenate([first, second], 1)
        back_mixed = jnp.zeros((seq_len, head_rows), F32)
        for block, owner in slots:
            part = lax.dynamic_slice_in_dim(sens_full, owner * block_width, block_width, 1)
            back_mixed += lax.dot_general(
                part, block, (((1,), (1,)), ((), ())), preferred_element_type=F32
            )
        sens_mixed = (mixed_gain * back_mixed).astype(BF16)
        back_values = jnp.einsum(
            "gjts,tgjd->sgd",
            prob_rows,
            sens_mixed.reshape(seq_len, local_kv, group_size, HD),
            preferred_element_type=F32,
        ).reshape(seq_len, kv_width)
        found = (value_gain * back_values).astype(BF16)
        sens_values = jnp.where(active, found, sens_values)
        kept_sum = jnp.where(active, jnp.sum(kept, axis=1), kept_sum)
        if not last_turn:
            straight = from_next_section(found)
            crossed = from_next_section(found, flip=True)
            first = jnp.where(core_pos == 0, straight, crossed)
            second = jnp.where(core_pos == 0, crossed, straight)
            behind_sens = jnp.concatenate([first, second], 1)
            back_inputs = lax.dot_general(
                behind_sens, behind_values, (((1,), (1,)), ((), ())), preferred_element_type=F32
            )
            arrived = behind_kept.astype(F32) + behind_inputs * back_inputs
            current = jnp.where(active, current, arrived)

    heat_part = kept_sum + jnp.sum(sens_values.astype(F32) * values_f, axis=1)
    heat_rows = (heat_part + cycled(heat_part, "mp", 1)) / DW

    block_rows = half_width // peers
    own_inputs, own_sens = [], []
    for k in range(peers):
        to = lax.rem(dp_pos + k, peers)
        piece = lax.dynamic_slice_in_dim(inputs, to * block_rows, block_rows, 1)
        own_inputs.append(cycled(piece, "dp", k) if k else piece)
        own_sens.append(cycled(sens_values, "dp", k) if k else sens_values)
    all_inputs = jnp.concatenate(own_inputs, 0)
    mine = jnp.concatenate(own_sens, 0)
    other = cycled(mine, "mp", 1)
    first = jnp.where(core_pos == 0, mine, other)
    second = jnp.where(core_pos == 0, other, mine)
    all_sens = jnp.concatenate([first, second], 1)
    summed = lax.dot_general(
        all_inputs, all_sens, (((0,), (0,)), ((), ())), preferred_element_type=F32
    )
    value_block = lax.dynamic_slice_in_dim(value_rows, dp_pos * block_rows, block_rows, 0)
    relevance_rows = value_block.astype(F32) * summed
    return (heat_rows[None, None, :], relevance_rows[None])


def solution(mesh):
    placed = (
        P("section", ("groups", "dp"), None, "mp"),
        P("section", ("groups", "dp"), None, "mp"),
        P("section", ("groups", "dp"), None, "mp"),
        P("section", ("groups", "dp"), None, "mp"),
        P("section", "mp", None),
        P("section", "mp", "dp"),
        P(("groups", "dp")),
    )
    return jax.shard_map(
        on_device,
        mesh=mesh,
        in_specs=placed,
        out_specs=(
            P("section", ("groups", "dp"), None),
            P(("groups", "section"), ("mp", "dp"), None),
        ),
        check_vma=False,
    )
```

```python
import itertools
import math

import jax
import jax.numpy as jnp
from jax import lax
from jax.sharding import PartitionSpec as P

DW = 2560
HD = 128
QH = 20
KVH = 4
EPS = 0.25
F32 = jnp.float32
BF16 = jnp.bfloat16


def stabilize(entries):
    return jnp.where(entries >= 0, entries + EPS, entries - EPS)


def cycled(shard, axis, by):
    peers = lax.axis_size(axis)
    return lax.ppermute(shard, axis, [(i, (i + by) % peers) for i in range(peers)])


def shifted(shard, axis, by):
    peers = lax.axis_size(axis)
    return lax.ppermute(
        shard, axis, [(i, i + by) for i in range(peers) if 0 <= i + by < peers]
    )


def moved(shard, axes, target):
    sizes = [lax.axis_size(axis) for axis in axes]
    places = list(itertools.product(*[range(size) for size in sizes]))
    index = {place: i for i, place in enumerate(places)}
    pairs = [(index[place], index[target(*place)]) for place in places if target(*place) is not None]
    return lax.ppermute(shard, axes, pairs)


def from_next_section(shard, flip=False):
    cores = lax.axis_size("mp")
    return moved(
        shard, ("section", "mp"), lambda s, c: (s - 1, (c + flip) % cores) if s > 0 else None
    )


def chain_hop(shard, by, step):
    sections, peers = lax.axis_size("section"), lax.axis_size("dp")

    def target(i, s):
        inside = 0 <= i + by < peers and 0 <= i - by * (step - 1) < peers
        return (i + by, s) if inside and s < sections - 1 else None

    return moved(shard, ("dp", "section"), target)


def swapped_groups(shard):
    sections, groups = lax.axis_size("section"), lax.axis_size("groups")
    return moved(
        shard,
        ("groups", "section"),
        lambda g, s: ((g + 1) % groups, s) if s < sections - 1 else None,
    )


def gather_blocks(mine, chunks):
    peers = lax.axis_size("dp")
    pos = lax.axis_index("dp")
    low = pos < peers // 2
    longer = jnp.where(low, peers - 1 - pos, pos)
    pieces = jnp.split(mine, chunks, axis=0)
    up = [[piece] for piece in pieces]
    down = [[piece] for piece in pieces]
    swaps = [[] for _ in pieces]
    slots = []
    for j in range(1, peers):
        own_rows, other_rows = [], []
        for q in range(chunks):
            send_up, send_down = up[q][-1], down[q][-1]
            if len(swaps[q]) > 1:
                send_up, send_down, swaps[q][-2] = lax.optimization_barrier(
                    (send_up, send_down, swaps[q][-2])
                )
            up[q].append(chain_hop(send_up, 1, j))
            down[q].append(chain_hop(send_down, -1, j))
            block = jnp.where(low, down[q][j], up[q][j])
            for k in range(1, min(j, (peers - 1) // 2) + 1):
                block = jnp.where(j - longer == k, jnp.where(low, up[q][k], down[q][k]), block)
            own_rows.append(block)
            swaps[q].append(swapped_groups(block))
        owner = jnp.where(low, pos + j, pos - j)
        for k in range(1, min(j, (peers - 1) // 2) + 1):
            owner = jnp.where(j - longer == k, jnp.where(low, pos - k, pos + k), owner)
        slots.append([own_rows, None, owner])
    for j in range(peers - 1):
        slots[j][1] = [swaps[q][j] for q in range(chunks)]
    return slots


def spread_product(sens_branch, out_block):
    axes = ("dp", "section", "mp")
    peers, cores = lax.axis_size("dp"), lax.axis_size("mp")
    last = lax.axis_size("section") - 1
    pos, core = lax.axis_index("dp"), lax.axis_index("mp")
    seq_len = sens_branch.shape[0]
    width = out_block.shape[1]
    per_core = peers // cores
    arrived = []
    for k in range(peers):
        to = lax.rem(pos + k, peers)
        part = lax.dynamic_slice_in_dim(sens_branch, lax.rem(to, per_core) * width, width, 1)
        if k:
            part = moved(
                part,
                axes,
                lambda i, s, c: ((i + k) % peers, s, c)
                if s == last and c == (i + k) % peers // per_core
                else None,
            )
        arrived.append(part)
    mine = jnp.concatenate(arrived, 0)
    theirs = moved(
        mine,
        axes,
        lambda i, s, c: (i, s, 1 - c) if s == last and c == i // per_core else None,
    )
    operand = jnp.where(core == pos // per_core, mine, theirs)
    product = lax.dot_general(
        operand, out_block, (((1,), (1,)), ((), ())), preferred_element_type=F32
    )
    total = product[:seq_len]
    for k in range(1, peers):
        back = product[k * seq_len : (k + 1) * seq_len].astype(BF16)
        back = moved(back, axes, lambda i, s, c: ((i - k) % peers, s, c) if s == last else None)
        total = total + back.astype(F32)
    return total


def on_device(hidden_in, attn_out, queries, keys, value_weight, out_weight, lengths):
    inputs = hidden_in[0, 0]
    branch = attn_out[0, 0]
    query_rows = queries[0, 0]
    key_rows = keys[0, 0]
    value_rows = value_weight[0]
    out_block = out_weight[0]
    seq_len, half_width = inputs.shape
    group_size = QH // KVH
    local_kv = key_rows.shape[1] // HD
    kv_width = local_kv * HD
    sections = lax.axis_size("section")
    section_pos = lax.axis_index("section")
    groups = lax.axis_size("groups")
    group_pos = lax.axis_index("groups")
    peers = lax.axis_size("dp")
    dp_pos = lax.axis_index("dp")
    core_pos = lax.axis_index("mp")
    head_rows, block_width = out_block.shape

    share = head_rows // groups
    own_rows = lax.dynamic_slice_in_dim(out_block, group_pos * share, share, 0)
    other_rows = lax.dynamic_slice_in_dim(out_block, (1 - group_pos) * share, share, 0)
    slots = [[[own_rows], [other_rows], dp_pos]] + gather_blocks(own_rows, 2)

    behind_inputs = from_next_section(inputs).astype(F32)
    behind_values = from_next_section(value_rows)

    inputs_f = inputs.astype(F32)
    branch_f = branch.astype(F32)
    totals = inputs_f + branch_f
    inv_totals = 1.0 / stabilize(totals)
    kept_gain = inputs_f * inv_totals
    branch_gain = branch_f * inv_totals / stabilize(branch_f)

    value_part = jnp.dot(inputs, value_rows, preferred_element_type=F32)
    part_mine = lax.dynamic_slice_in_dim(value_part, core_pos * kv_width, kv_width, 1)
    part_other = lax.dynamic_slice_in_dim(value_part, (1 - core_pos) * kv_width, kv_width, 1)
    values_f = part_mine + cycled(part_other.astype(BF16), "mp", 1).astype(F32)
    values_bf = values_f.astype(BF16)
    values_r = values_bf.astype(F32)
    value_gain = values_r / stabilize(values_r)

    query_heads = query_rows.reshape(seq_len, local_kv, group_size, HD)
    key_heads = key_rows.reshape(seq_len, local_kv, HD)
    scores = jnp.einsum(
        "tgjd,sgd->gjts", query_heads, key_heads, preferred_element_type=F32
    ) / math.sqrt(HD)
    position = lax.iota(jnp.int32, seq_len)
    allowed = (position[None, :] <= position[:, None]) & (position[None, :] < lengths[0])
    scores = jnp.where(allowed, scores, -1000000000.0)
    row_top = jnp.max(scores, axis=-1, keepdims=True)
    weights = jnp.exp(scores - row_top)
    prob_rows = (weights / jnp.sum(weights, axis=-1, keepdims=True)).astype(BF16)
    mixed = jnp.einsum(
        "gjts,sgd->tgjd",
        prob_rows,
        values_bf.reshape(seq_len, local_kv, HD),
        preferred_element_type=F32,
    ).reshape(seq_len, local_kv * group_size * HD)
    mixed_gain = mixed / stabilize(mixed)

    valid_rows = (position < lengths[0]).astype(F32)
    current = (totals * valid_rows[:, None]).astype(BF16).astype(F32)
    sens_values = jnp.zeros((seq_len, kv_width), BF16)
    kept_sum = jnp.zeros((seq_len,), F32)
    for turn in range(sections):
        last_turn = turn + 1 == sections
        active = section_pos == sections - 1 - turn
        kept = current * kept_gain
        if not last_turn:
            behind_kept = from_next_section(kept.astype(BF16))
        sens_branch = (current * branch_gain).astype(BF16)
        if turn == 0:
            back_mixed = spread_product(sens_branch, out_block)
        else:
            sens_other = cycled(sens_branch, "mp", 1)
            first = jnp.where(core_pos == 0, sens_branch, sens_other)
            second = jnp.where(core_pos == 0, sens_other, sens_branch)
            sens_full = jnp.concatenate([first, second], 1)
            halves = [jnp.zeros((seq_len, share), F32) for _ in range(2)]
            for *blocks, owner in slots:
                part = lax.dynamic_slice_in_dim(sens_full, owner * block_width, block_width, 1)
                for side in range(2):
                    halves[side] += lax.dot_general(
                        part,
                        jnp.concatenate(blocks[side], 0),
                        (((1,), (1,)), ((), ())),
                        preferred_element_type=F32,
                    )
            first = jnp.where(group_pos == 0, halves[0], halves[1])
            second = jnp.where(group_pos == 0, halves[1], halves[0])
            back_mixed = jnp.concatenate([first, second], 1)
        sens_mixed = (mixed_gain * back_mixed).astype(BF16)
        back_values = jnp.einsum(
            "gjts,tgjd->sgd",
            prob_rows,
            sens_mixed.reshape(seq_len, local_kv, group_size, HD),
            preferred_element_type=F32,
        ).reshape(seq_len, kv_width)
        found = (value_gain * back_values).astype(BF16)
        sens_values = jnp.where(active, found, sens_values)
        kept_sum = jnp.where(active, jnp.sum(kept, axis=1), kept_sum)
        if not last_turn:
            straight = from_next_section(found)
            crossed = from_next_section(found, flip=True)
            first = jnp.where(core_pos == 0, straight, crossed)
            second = jnp.where(core_pos == 0, crossed, straight)
            behind_sens = jnp.concatenate([first, second], 1)
            back_inputs = lax.dot_general(
                behind_sens, behind_values, (((1,), (1,)), ((), ())), preferred_element_type=F32
            )
            arrived = behind_kept.astype(F32) + behind_inputs * back_inputs
            current = jnp.where(active, current, arrived)

    heat_part = kept_sum + jnp.sum(sens_values.astype(F32) * values_f, axis=1)
    heat_rows = (heat_part + cycled(heat_part, "mp", 1)) / DW

    block_rows = half_width // peers
    own_inputs, own_sens = [], []
    for k in range(peers):
        to = lax.rem(dp_pos + k, peers)
        piece = lax.dynamic_slice_in_dim(inputs, to * block_rows, block_rows, 1)
        own_inputs.append(cycled(piece, "dp", k) if k else piece)
        own_sens.append(cycled(sens_values, "dp", k) if k else sens_values)
    all_inputs = jnp.concatenate(own_inputs, 0)
    mine = jnp.concatenate(own_sens, 0)
    other = cycled(mine, "mp", 1)
    first = jnp.where(core_pos == 0, mine, other)
    second = jnp.where(core_pos == 0, other, mine)
    all_sens = jnp.concatenate([first, second], 1)
    summed = lax.dot_general(
        all_inputs, all_sens, (((0,), (0,)), ((), ())), preferred_element_type=F32
    )
    value_block = lax.dynamic_slice_in_dim(value_rows, dp_pos * block_rows, block_rows, 0)
    relevance_rows = value_block.astype(F32) * summed
    return (heat_rows[None, None, :], relevance_rows[None])


def solution(mesh):
    placed = (
        P("section", ("groups", "dp"), None, "mp"),
        P("section", ("groups", "dp"), None, "mp"),
        P("section", ("groups", "dp"), None, "mp"),
        P("section", ("groups", "dp"), None, "mp"),
        P("section", "mp", None),
        P("section", "mp", "dp"),
        P(("groups", "dp")),
    )
    return jax.shard_map(
        on_device,
        mesh=mesh,
        in_specs=placed,
        out_specs=(
            P("section", ("groups", "dp"), None),
            P(("groups", "section"), ("mp", "dp"), None),
        ),
        check_vma=False,
    )
```

```python
import itertools
import math

import jax
import jax.numpy as jnp
from jax import lax
from jax.sharding import PartitionSpec as P

DW = 2560
HD = 128
QH = 20
KVH = 4
EPS = 0.25
F32 = jnp.float32
BF16 = jnp.bfloat16


def stabilize(entries):
    return jnp.where(entries >= 0, entries + EPS, entries - EPS)


def moved(shard, axes, target):
    sizes = [lax.axis_size(axis) for axis in axes]
    places = list(itertools.product(*[range(size) for size in sizes]))
    index = {place: i for i, place in enumerate(places)}
    pairs = [(index[place], index[target(*place)]) for place in places if target(*place) is not None]
    return lax.ppermute(shard, axes, pairs)


def along_dp(shard, by):
    peers = lax.axis_size("dp")
    return moved(shard, ("dp",), lambda i: ((i + by) % peers,)) if by else shard


def other_core(shard):
    return moved(shard, ("mp",), lambda c: (1 - c,))


def other_group(shard):
    return moved(shard, ("groups",), lambda g: (1 - g,))


def pair_partner(shard):
    return moved(shard, ("dp",), lambda i: (i ^ 1,))


def from_next_section(shard, flip_pair=0, flip_core=0):
    return moved(
        shard,
        ("dp", "section", "mp"),
        lambda i, s, c: (i ^ flip_pair, s - 1, c ^ flip_core) if s > 0 else None,
    )


def ordered(first_is_mine, mine, theirs, axis):
    return jnp.concatenate(
        [jnp.where(first_is_mine, mine, theirs), jnp.where(first_is_mine, theirs, mine)], axis
    )


def part_of(array, index, width, axis):
    return lax.dynamic_slice_in_dim(array, index * width, width, axis)


def on_device(hidden_in, attn_out, queries, keys, value_weight, out_weight, lengths):
    inputs = hidden_in[0, 0]
    branch = attn_out[0, 0]
    query_rows = queries[0, 0]
    key_rows = keys[0, 0]
    value_rows = value_weight[0]
    out_block = out_weight[0]
    seq_len, half_width = inputs.shape
    group_size = QH // KVH
    kv_width = key_rows.shape[1]
    head_width = group_size * HD
    sections = lax.axis_size("section")
    section_pos = lax.axis_index("section")
    group_pos = lax.axis_index("groups")
    peers = lax.axis_size("dp")
    dp_pos = lax.axis_index("dp")
    core_pos = lax.axis_index("mp")
    block_width = out_block.shape[1]
    side = dp_pos % 2
    even = side == 0
    quarter = head_width // 2

    own_quarters = [part_of(out_block, 2 * side + group_pos, quarter, 0)]
    other_quarters = [part_of(out_block, 2 * side + 1 - group_pos, quarter, 0)]
    sent = [
        part_of(out_block, 2 * ((dp_pos + k) % 2) + group_pos, quarter, 0) for k in range(1, peers)
    ]
    for k in range(1, peers):
        own_quarters.append(along_dp(sent[k - 1], k))
        other_quarters.append(other_group(own_quarters[k]))
    own_rows = jnp.concatenate(own_quarters, 1)
    other_rows = jnp.concatenate(other_quarters, 1)

    inputs_f = inputs.astype(F32)
    branch_f = branch.astype(F32)
    totals = inputs_f + branch_f
    inv_totals = 1.0 / stabilize(totals)
    kept_gain = inputs_f * inv_totals
    branch_gain = branch_f * inv_totals / stabilize(branch_f)
    position = lax.iota(jnp.int32, seq_len)
    valid_rows = (position < lengths[0]).astype(F32)
    current = (totals * valid_rows[:, None]).astype(BF16).astype(F32)
    sens_branch = (current * branch_gain).astype(BF16)

    def both_cores(mine):
        return ordered(core_pos == 0, mine, other_core(mine), 1)

    def both_sequences(mine):
        return ordered(even, mine, pair_partner(mine), 0)

    sens_full = both_cores(both_sequences(sens_branch))

    behind_inputs = from_next_section(inputs).astype(F32)
    behind_values = from_next_section(value_rows)
    behind_values = ordered(core_pos == 0, behind_values, other_core(behind_values), 0)
    bent_full = both_cores(both_sequences((branch_gain * behind_inputs).astype(BF16)))

    value_part = jnp.dot(inputs, value_rows, preferred_element_type=F32)
    part_mine = part_of(value_part, core_pos, kv_width, 1)
    part_other = part_of(value_part, 1 - core_pos, kv_width, 1)
    values_own = part_mine + other_core(part_other.astype(BF16)).astype(F32)
    own_len = jnp.broadcast_to(lengths[0].astype(BF16), (8, HD))
    sent_values = jnp.concatenate(
        [part_of(values_own, 1 - side, HD, 1).astype(BF16), own_len], 0
    )
    got_values = pair_partner(sent_values)
    kept_values = jnp.concatenate([part_of(values_own, side, HD, 1).astype(BF16), own_len], 0)
    pair_values = jnp.stack(
        [jnp.where(even, kept_values, got_values), jnp.where(even, got_values, kept_values)]
    )
    pair_lengths = pair_values[:, seq_len, 0].astype(jnp.int32)
    pair_values = pair_values[:, :seq_len]
    values_r = pair_values.astype(F32)
    value_gain = values_r / stabilize(values_r)

    sent_heads = jnp.concatenate(
        [part_of(query_rows, 1 - side, head_width, 1), part_of(key_rows, 1 - side, HD, 1)], 1
    )
    kept_heads = jnp.concatenate(
        [part_of(query_rows, side, head_width, 1), part_of(key_rows, side, HD, 1)], 1
    )
    got_heads = pair_partner(sent_heads)
    heads = jnp.stack(
        [jnp.where(even, kept_heads, got_heads), jnp.where(even, got_heads, kept_heads)]
    )
    query_heads = heads[:, :, :head_width].reshape(2, seq_len, group_size, HD)
    key_heads = heads[:, :, head_width:]
    scores = jnp.einsum(
        "btjd,bsd->bjts", query_heads, key_heads, preferred_element_type=F32
    ) / math.sqrt(HD)
    allowed = (position[None, None, :] <= position[None, :, None]) & (
        position[None, None, :] < pair_lengths[:, None, None]
    )
    scores = jnp.where(allowed[:, None], scores, -1000000000.0)
    row_top = jnp.max(scores, axis=-1, keepdims=True)
    weights = jnp.exp(scores - row_top)
    prob_rows = (weights / jnp.sum(weights, axis=-1, keepdims=True)).astype(BF16)
    mixed = jnp.einsum(
        "bjts,bsd->btjd", prob_rows, pair_values, preferred_element_type=F32
    ).reshape(2 * seq_len, head_width)
    mixed_gain = mixed / stabilize(mixed)

    sens_values = jnp.zeros((2 * seq_len, HD), BF16)
    kept_sum = jnp.zeros((seq_len,), F32)
    for turn in range(sections):
        active = section_pos == sections - 1 - turn
        kept = current * kept_gain
        if turn + 1 < sections:
            behind_kept = from_next_section(kept.astype(BF16)).astype(F32)
            flat_full = both_cores(both_sequences((branch_gain * behind_kept).astype(BF16)))
        halves = [jnp.zeros((2 * seq_len, quarter), F32) for _ in range(2)]
        turned = jnp.concatenate(
            [part_of(sens_full, (dp_pos - k) % peers, block_width, 1) for k in range(peers)], 1
        )
        for half, rows in enumerate((own_rows, other_rows)):
            halves[half] = lax.dot_general(
                turned, rows, (((1,), (1,)), ((), ())), preferred_element_type=F32
            )
        back_mixed = ordered(group_pos == 0, halves[0], halves[1], 1)
        sens_mixed = (mixed_gain * back_mixed).astype(BF16)
        back_values = jnp.einsum(
            "bjts,btjd->bsd",
            prob_rows,
            sens_mixed.reshape(2, seq_len, group_size, HD),
            preferred_element_type=F32,
        )
        found = (value_gain * back_values).astype(BF16).reshape(2 * seq_len, HD)
        sens_values = jnp.where(active, found, sens_values)
        kept_sum = jnp.where(active, jnp.sum(kept, axis=1), kept_sum)
        if turn + 1 < sections:
            pieces = [[from_next_section(found, i, j) for j in range(2)] for i in range(2)]
            columns = [ordered(even, pieces[0][j], pieces[1][j], 1) for j in range(2)]
            behind_sens = ordered(core_pos == 0, columns[0], columns[1], 1)
            back_inputs = lax.dot_general(
                behind_sens, behind_values, (((1,), (1,)), ((), ())), preferred_element_type=F32
            )
            sens_full = (flat_full.astype(F32) + bent_full.astype(F32) * back_inputs).astype(BF16)
            mine = part_of(part_of(back_inputs, side, seq_len, 0), core_pos, half_width, 1)
            current = jnp.where(active, current, behind_kept + behind_inputs * mine)

    from_values = jnp.sum(
        (sens_values.astype(F32) * values_r.reshape(2 * seq_len, HD)).reshape(2, seq_len, HD), axis=2
    )
    kept_part = jnp.where(even, from_values[0], from_values[1])
    sent_part = jnp.where(even, from_values[1], from_values[0])
    heat_part = kept_sum + kept_part + pair_partner(sent_part)
    heat_rows = (heat_part + other_core(heat_part)) / DW

    block_rows = half_width // peers
    got_inputs = [
        along_dp(part_of(inputs, (dp_pos + k) % peers, block_rows, 1), k) for k in range(peers)
    ]
    all_inputs = []
    for j in range(0, peers, 2):
        after, before = got_inputs[j + 1], got_inputs[(j - 1) % peers]
        all_inputs.append(jnp.where(even, got_inputs[j], after))
        all_inputs.append(jnp.where(even, before, got_inputs[j]))
    all_inputs = jnp.concatenate(all_inputs, 0)
    got_sens = [along_dp(sens_values, k) for k in range(peers)]
    same_side = jnp.concatenate([got_sens[j] for j in range(0, peers, 2)], 0)
    other_side = jnp.concatenate(
        [jnp.where(even, got_sens[(j - 1) % peers], got_sens[j + 1]) for j in range(0, peers, 2)], 0
    )
    core_sens = ordered(even, same_side, other_side, 1)
    all_sens = both_cores(core_sens)
    summed = lax.dot_general(
        all_inputs, all_sens, (((0,), (0,)), ((), ())), preferred_element_type=F32
    )
    value_block = part_of(value_rows, dp_pos, block_rows, 0)
    relevance_rows = value_block.astype(F32) * summed
    return (heat_rows[None, None, :], relevance_rows[None])


def solution(mesh):
    placed = (
        P("section", ("groups", "dp"), None, "mp"),
        P("section", ("groups", "dp"), None, "mp"),
        P("section", ("groups", "dp"), None, "mp"),
        P("section", ("groups", "dp"), None, "mp"),
        P("section", "mp", None),
        P("section", "mp", "dp"),
        P(("groups", "dp")),
    )
    return jax.shard_map(
        on_device,
        mesh=mesh,
        in_specs=placed,
        out_specs=(
            P("section", ("groups", "dp"), None),
            P(("groups", "section"), ("mp", "dp"), None),
        ),
        check_vma=False,
    )
```

```python
import functools
import itertools
import math

import jax
import jax.numpy as jnp
from jax import lax
from jax.experimental import pallas as pl
from jax.experimental.pallas import tpu as pltpu
from jax.sharding import PartitionSpec as P

DW = 2560
HD = 128
QH = 20
KVH = 4
EPS = 0.25
F32 = jnp.float32
BF16 = jnp.bfloat16


def stabilize(entries):
    return jnp.where(entries >= 0, entries + EPS, entries - EPS)


VMEM = pl.BlockSpec(memory_space=pltpu.VMEM)
SMEM = pl.BlockSpec(memory_space=pltpu.SMEM)
ANY = pl.BlockSpec(memory_space=pl.ANY)


def by_columns(left, right):
    return lax.dot_general(left, right, (((1,), (1,)), ((), ())), preferred_element_type=F32)


def kernel_call(body, shapes, in_specs, scratch=(), flops=0, nbytes=0, limit=24):
    return pl.pallas_call(
        body,
        out_shape=shapes,
        in_specs=in_specs,
        out_specs=jax.tree.map(lambda _: VMEM, shapes),
        scratch_shapes=scratch,
        compiler_params=pltpu.CompilerParams(vmem_limit_bytes=limit * 2**20),
        cost_estimate=pl.CostEstimate(flops=flops, bytes_accessed=nbytes, transcendentals=0),
    )


def attention_kernel(length, queries, keys, values, probs_t, mixed_gain, value_gain):
    seq_len = queries.shape[0]
    kv_heads = keys.shape[1] // HD
    group_size = queries.shape[1] // HD // kv_heads
    row = lax.broadcasted_iota(jnp.int32, (seq_len, seq_len), 0)
    column = lax.broadcasted_iota(jnp.int32, (seq_len, seq_len), 1)
    allowed = (column <= row) & (column < length[0])
    values_bf = values[...].astype(BF16)
    values_r = values_bf.astype(F32)
    value_gain[...] = values_r / stabilize(values_r)
    for g in range(kv_heads):
        key_head = keys[:, g * HD : (g + 1) * HD]
        value_head = values_bf[:, g * HD : (g + 1) * HD]
        for h in range(g * group_size, (g + 1) * group_size):
            scores = by_columns(queries[:, h * HD : (h + 1) * HD], key_head) / math.sqrt(HD)
            scores = jnp.where(allowed, scores, -1000000000.0)
            weights = jnp.exp(scores - jnp.max(scores, axis=1, keepdims=True))
            probs = weights / jnp.sum(weights, axis=1, keepdims=True)
            probs_t[h] = probs.T.astype(BF16)
            mixed = jnp.dot(probs.astype(BF16), value_head, preferred_element_type=F32)
            mixed_gain[:, h * HD : (h + 1) * HD] = mixed / stabilize(mixed)


def attend(length, queries, keys, values):
    seq_len, width = queries.shape
    shapes = (
        jax.ShapeDtypeStruct((width // HD, seq_len, seq_len), BF16),
        jax.ShapeDtypeStruct((seq_len, width), F32),
        jax.ShapeDtypeStruct(values.shape, F32),
    )
    call = kernel_call(
        attention_kernel, shapes, [SMEM, VMEM, VMEM, VMEM], flops=10**8, nbytes=3 * 10**6
    )
    return call(length, queries, keys, values)


def head_step(back_mixed, probs_t, mixed_gain, value_gain, found):
    heads = probs_t.shape[0]
    kv_heads = value_gain.shape[1] // HD
    group_size = heads // kv_heads
    for g in range(kv_heads):
        total = jnp.zeros((probs_t.shape[1], HD), F32)
        for h in range(g * group_size, (g + 1) * group_size):
            at = slice(h * HD, (h + 1) * HD)
            sens_mixed = (mixed_gain[:, at] * back_mixed[:, at]).astype(BF16)
            total += jnp.dot(probs_t[h], sens_mixed, preferred_element_type=F32)
        at = slice(g * HD, (g + 1) * HD)
        found[:, at] = (value_gain[:, at] * total).astype(BF16)


def sum_heads_kernel(count, product, *refs):
    backs, (probs_t, mixed_gain, value_gain, found, total) = refs[:count], refs[count:]
    back_mixed = product[...]
    for back in backs:
        back_mixed += back[...].astype(F32)
    total[...] = back_mixed
    head_step(total, probs_t, mixed_gain, value_gain, found)


def sum_heads(product, backs, probs_t, mixed_gain, value_gain):
    call = kernel_call(
        functools.partial(sum_heads_kernel, len(backs)),
        jax.ShapeDtypeStruct(value_gain.shape, BF16),
        [VMEM] * (4 + len(backs)),
        [pltpu.VMEM(product.shape, F32)],
        flops=5 * 10**7,
        nbytes=3 * 10**6,
    )
    return call(product, *backs, probs_t, mixed_gain, value_gain)


def sensitivity_kernel(length, inputs, branch, *refs):
    current, sens = refs if len(refs) == 2 else (None, refs[0])
    inputs_f = inputs[...].astype(F32)
    branch_f = branch[...].astype(F32)
    totals = inputs_f + branch_f
    if current is None:
        row = lax.broadcasted_iota(jnp.int32, totals.shape, 0)
        entering = jnp.where(row < length[0], totals, 0.0).astype(BF16).astype(F32)
    else:
        entering = current[...].astype(F32)
    sens[...] = (branch_f * (entering / stabilize(totals)) / stabilize(branch_f)).astype(BF16)


def sensitivity(length, inputs, branch, *current):
    call = kernel_call(
        sensitivity_kernel,
        jax.ShapeDtypeStruct(inputs.shape, BF16),
        [SMEM] + [VMEM] * (2 + len(current)),
        flops=10**7,
        nbytes=10**6,
    )
    return call(length, inputs, branch, *current)


def outgoing_kernel(place, inputs, branch, sens_own, sens_other, value_rows, outgoing):
    core, length = place[0], place[1]
    width = sens_own.shape[1]
    inputs_f = inputs[...].astype(F32)
    totals = inputs_f + branch[...].astype(F32)
    row = lax.broadcasted_iota(jnp.int32, totals.shape, 0)
    entering = jnp.where(row < length, totals, 0.0).astype(BF16).astype(F32)
    own = value_rows[:, pl.ds(pl.multiple_of(core * width, 128), width)]
    other = value_rows[:, pl.ds(pl.multiple_of((1 - core) * width, 128), width)]
    back_inputs = by_columns(sens_own[...], own) + by_columns(sens_other[...], other)
    kept = inputs_f * (entering / stabilize(totals))
    outgoing[...] = (kept + inputs_f * back_inputs).astype(BF16)


def last_outgoing(place, inputs, branch, sens_own, sens_other, value_rows):
    call = kernel_call(
        outgoing_kernel,
        jax.ShapeDtypeStruct(inputs.shape, BF16),
        [SMEM] + [VMEM] * 5,
        flops=2 * 10**8,
        nbytes=2 * 10**6,
    )
    return call(place, inputs, branch, sens_own, sens_other, value_rows)


def product_kernel(use_mine, mine, theirs, block, own, *backs):
    seq_len = own.shape[0]

    def multiply(operand):
        product = by_columns(operand[...], block[...])
        own[...] = product[:seq_len]
        for k, back in enumerate(backs):
            back[...] = product[(k + 1) * seq_len : (k + 2) * seq_len].astype(BF16)

    @pl.when(use_mine[0] == 1)
    def _():
        multiply(mine)

    @pl.when(use_mine[0] == 0)
    def _():
        multiply(theirs)


def spread_products(use_mine, mine, theirs, block, seq_len):
    count = mine.shape[0] // seq_len
    width = block.shape[0]
    shapes = (jax.ShapeDtypeStruct((seq_len, width), F32),) + tuple(
        jax.ShapeDtypeStruct((seq_len, width), BF16) for _ in range(count - 1)
    )
    call = kernel_call(
        product_kernel, shapes, [SMEM, VMEM, VMEM, VMEM], flops=10**9, nbytes=5 * 10**6, limit=32
    )
    return call(use_mine, mine, theirs, block)


def main_kernel(layout, place, sens_own, sens_other, out_block, *refs):
    count = len(layout)
    pieces = refs[:count]
    probs_t, mixed_gain, value_gain, found, halves, total, block, sem = refs[count : count + 8]
    held, sems = refs[count + 8 :][:count], refs[count + 8 + count]
    pos, core, group = place[0], place[1], place[2]
    width = out_block.shape[1]
    per_core = sens_own.shape[1] // width
    copies = [pltpu.make_async_copy(out_block, block, sem)]
    copies += [pltpu.make_async_copy(pieces[i], held[i], sems.at[i]) for i in range(count)]
    for copy in copies:
        copy.start()
    halves[core] = sens_own[...]
    halves[1 - core] = sens_other[...]

    def part(slot):
        owner = pos ^ slot
        start = pl.multiple_of(lax.rem(owner, per_core) * width, 128)
        return halves[owner // per_core, :, pl.ds(start, width)]

    copies[0].wait()
    total[...] = by_columns(part(0), block[...])
    for i, (slot, side, start) in enumerate(layout):
        copies[i + 1].wait()
        rows = held[i].shape[0]
        at = (group if side == 0 else 1 - group) * (total.shape[1] // 2) + start
        total[:, pl.ds(pl.multiple_of(at, 128), rows)] += by_columns(part(slot), held[i][...])
    head_step(total, probs_t, mixed_gain, value_gain, found)


def main_step(place, sens_own, sens_other, out_block, slots, probs_t, mixed_gain, value_gain):
    layout, pieces = [], []
    for k, sides in enumerate(slots):
        for side in range(2):
            start = 0
            for piece in sides[side]:
                layout.append((k + 1, side, start))
                pieces.append(piece)
                start += piece.shape[0]
    seq_len, half_width = sens_own.shape
    call = kernel_call(
        functools.partial(main_kernel, tuple(layout)),
        jax.ShapeDtypeStruct(value_gain.shape, BF16),
        [SMEM, VMEM, VMEM, ANY] + [ANY] * len(pieces) + [VMEM] * 3,
        [
            pltpu.VMEM((2, seq_len, half_width), BF16),
            pltpu.VMEM(mixed_gain.shape, F32),
            pltpu.VMEM(out_block.shape, BF16),
            pltpu.SemaphoreType.DMA,
        ]
        + [pltpu.VMEM(piece.shape, BF16) for piece in pieces]
        + [pltpu.SemaphoreType.DMA((len(pieces),))],
        flops=10**9,
        nbytes=8 * 10**6,
        limit=32,
    )
    return call(place, sens_own, sens_other, out_block, *pieces, probs_t, mixed_gain, value_gain)


def moved(shard, axes, target):
    sizes = [lax.axis_size(axis) for axis in axes]
    places = list(itertools.product(*[range(size) for size in sizes]))
    index = {place: i for i, place in enumerate(places)}
    pairs = [(index[place], index[target(*place)]) for place in places if target(*place) is not None]
    return lax.ppermute(shard, axes, pairs)


def along_dp(shard, by):
    peers = lax.axis_size("dp")
    return moved(shard, ("dp",), lambda i: ((i + by) % peers,)) if by else shard


def other_core(shard):
    return moved(shard, ("mp",), lambda c: (1 - c,))


def from_next_section(shard):
    return moved(shard, ("section",), lambda s: (s - 1,) if s > 0 else None)


def ordered(first_is_mine, mine, theirs, axis):
    return jnp.concatenate(
        [jnp.where(first_is_mine, mine, theirs), jnp.where(first_is_mine, theirs, mine)], axis
    )


def part_of(array, index, width, axis):
    return lax.dynamic_slice_in_dim(array, index * width, width, axis)


def once(array, *others):
    return lax.optimization_barrier((array,) + others)[0]


def early_move(shard, axes, target):
    last = lax.axis_size("section") - 1
    at = axes.index("section")
    return moved(shard, axes, lambda *place: target(*place) if place[at] < last else None)


def between(shard, pairs):
    return early_move(shard, ("dp", "section"), lambda i, s: (pairs[i], s) if i in pairs else None)


def swap_groups(shard):
    return early_move(shard, ("groups", "section"), lambda g, s: (1 - g, s))


MIDDLE = {1: 2, 2: 1}
OUTWARD = {1: 0, 2: 3}


def start_gather(mine, *others):
    peers = lax.axis_size("dp")
    pos = lax.axis_index("dp")
    if peers != 4:
        return [between(mine, {i: i ^ k for i in range(peers)}) for k in range(1, peers)]
    pair = between(mine, {i: i ^ 1 for i in range(peers)})
    near = between(mine, MIDDLE)
    pair, near, *_ = lax.optimization_barrier((pair, near, *others))
    crossed = between(pair, MIDDLE)
    relayed = between(near, OUTWARD)
    pair_swapped = swap_groups(pair)
    second = jnp.where((pos == 1) | (pos == 2), crossed, relayed)
    return [pair, pair_swapped, second, near]


def finish_gather(started):
    peers = lax.axis_size("dp")
    pos = lax.axis_index("dp")
    if peers != 4:
        return [([block], [swap_groups(block)]) for block in started]
    pair, pair_swapped, second, near = started
    cut = [second.shape[0] * 3 // 5]
    third = [
        jnp.where((pos == 1) | (pos == 2), direct, between(far, OUTWARD))
        for direct, far in zip(jnp.split(near, cut), jnp.split(second, cut))
    ]
    return [
        ([pair], [pair_swapped]),
        ([second], [swap_groups(second)]),
        (third, [swap_groups(piece) for piece in third]),
    ]


def spread_product(sens_branch, out_block):
    axes = ("dp", "section", "mp")
    peers, cores = lax.axis_size("dp"), lax.axis_size("mp")
    last = lax.axis_size("section") - 1
    pos, core = lax.axis_index("dp"), lax.axis_index("mp")
    seq_len = sens_branch.shape[0]
    width = out_block.shape[1]
    per_core = peers // cores
    arrived = []
    for k in range(peers):
        to = lax.rem(pos + k, peers)
        part = part_of(sens_branch, lax.rem(to, per_core), width, 1)
        if k:
            part = moved(
                part,
                axes,
                lambda i, s, c: ((i + k) % peers, s, c)
                if s == last and c == (i + k) % peers // per_core
                else None,
            )
        arrived.append(part)
    mine = jnp.concatenate(arrived, 0)
    theirs = moved(
        mine,
        axes,
        lambda i, s, c: (i, s, 1 - c) if s == last and c == i // per_core else None,
    )
    if width % 128 == 0:
        use_mine = (core == pos // per_core).astype(jnp.int32)[None]
        own, *sent = spread_products(use_mine, mine, theirs, out_block, seq_len)
    else:
        product = by_columns(jnp.where(core == pos // per_core, mine, theirs), out_block)
        own, *sent = jnp.split(product, peers, axis=0)
    backs = [
        moved(
            sent[k - 1].astype(BF16),
            axes,
            lambda i, s, c: ((i - k) % peers, s, c) if s == last else None,
        )
        for k in range(1, peers)
    ]
    return own, backs


def on_device(hidden_in, attn_out, queries, keys, value_weight, out_weight, lengths):
    inputs = hidden_in[0, 0]
    branch = attn_out[0, 0]
    query_rows = queries[0, 0]
    key_rows = keys[0, 0]
    value_rows = value_weight[0]
    out_block = out_weight[0]
    seq_len, half_width = inputs.shape
    kv_width = key_rows.shape[1]
    sections = lax.axis_size("section")
    section_pos = lax.axis_index("section")
    group_pos = lax.axis_index("groups")
    peers = lax.axis_size("dp")
    dp_pos = lax.axis_index("dp")
    core_pos = lax.axis_index("mp")
    head_rows, block_width = out_block.shape
    is_last = section_pos == sections - 1

    totals = inputs.astype(F32) + branch.astype(F32)
    valid_rows = (lax.iota(jnp.int32, seq_len) < lengths[0]).astype(F32)
    current = (totals * valid_rows[:, None]).astype(BF16)

    def kept_of(entering):
        return inputs.astype(F32) * (entering.astype(F32) / stabilize(totals))

    def core_exchange(mine, take):
        return moved(
            mine, ("section", "mp"), lambda s, c: (s, 1 - c) if take(s == sections - 1) else None
        )

    def attention(take):
        value_part = jnp.dot(inputs, value_rows, preferred_element_type=F32)
        part_mine = part_of(value_part, core_pos, kv_width, 1)
        part_other = part_of(value_part, 1 - core_pos, kv_width, 1)
        values_f = part_mine + core_exchange(part_other.astype(BF16), take).astype(F32)
        return values_f, attend(lengths, query_rows, key_rows, values_f)

    block_rows = half_width // peers

    def inputs_of_all(rows, take):
        pieces = []
        for k in range(peers):
            piece = part_of(rows, lax.rem(dp_pos + k, peers), block_rows, 1)
            if k:
                piece = moved(
                    piece,
                    ("dp", "section"),
                    lambda i, s: ((i + k) % peers, s) if take(s == sections - 1) else None,
                )
            pieces.append(piece)
        return jnp.concatenate(pieces, 0)

    def last_section():
        values_f, rest = attention(lambda last: last)
        sens_branch = sensitivity(lengths, inputs, branch)
        own, backs = spread_product(sens_branch, out_block)
        all_inputs = inputs_of_all(inputs, lambda last: last)
        started = [jnp.zeros(leaf.shape, leaf.dtype) for leaf in early_shapes[-1]]
        own, all_inputs, *started = lax.optimization_barrier((own, all_inputs, *started))
        if peers > 4:
            for back in backs:
                own = own + back.astype(F32)
            backs = []
        found = sum_heads(own, backs, *rest)
        other = core_exchange(found, lambda last: last)
        place = jnp.stack([core_pos, lengths[0]])
        outgoing = last_outgoing(place, inputs, branch, found, other, value_rows)
        return values_f, rest, found, outgoing, all_inputs, started

    def early_section():
        mine = part_of(out_block, group_pos, head_rows // 2, 0)
        all_inputs = inputs_of_all(inputs, lambda last: not last)
        values_f, rest = attention(lambda last: not last)
        started = start_gather(mine, values_f, *rest, all_inputs)
        found = jnp.zeros((seq_len, kv_width), BF16)
        outgoing = jnp.zeros((seq_len, half_width), BF16)
        return values_f, rest, found, outgoing, all_inputs, started

    early_shapes = jax.eval_shape(early_section)
    values_f, rest, sens_values, outgoing, all_inputs, started = lax.cond(
        is_last, last_section, early_section
    )
    arrived = from_next_section(outgoing)
    slots = finish_gather(started)

    for turn in range(1, sections):
        active = section_pos == sections - 1 - turn
        current = jnp.where(active, arrived, current)
        sens_branch = sensitivity(lengths, inputs, branch, current)
        sens_other = core_exchange(sens_branch, lambda last: not last)
        if block_width % 128 == 0:
            place = jnp.stack([dp_pos, core_pos, group_pos])
            found = main_step(place, sens_branch, sens_other, out_block, slots, *rest)
        else:
            share = head_rows // 2
            own_rows = part_of(out_block, group_pos, share, 0)
            other_rows = part_of(out_block, 1 - group_pos, share, 0)
            sens_full = ordered(core_pos == 0, sens_branch, sens_other, 1)
            halves = [jnp.zeros((seq_len, share), F32) for _ in range(2)]
            for k, blocks in enumerate([([own_rows], [other_rows])] + slots):
                part = part_of(sens_full, dp_pos ^ k, block_width, 1)
                for side in range(2):
                    halves[side] += jnp.concatenate(
                        [by_columns(part, piece) for piece in blocks[side]], 1
                    )
            found = sum_heads(ordered(group_pos == 0, halves[0], halves[1], 1), [], *rest)
        sens_values = jnp.where(active, found, sens_values)
        if turn + 1 < sections:
            sens_all = ordered(
                core_pos == 0, found, core_exchange(found, lambda last: not last), 1
            )
            back_inputs = by_columns(sens_all, value_rows)
            outgoing = kept_of(current) + inputs.astype(F32) * back_inputs
            arrived = from_next_section(outgoing.astype(BF16))

    heat_part = jnp.sum(kept_of(current), axis=1)
    heat_part += jnp.sum(sens_values.astype(F32) * values_f, axis=1)
    heat_rows = (heat_part + other_core(heat_part)) / DW

    mine = jnp.concatenate([along_dp(sens_values, k) for k in range(peers)], 0)
    all_sens = ordered(core_pos == 0, mine, other_core(mine), 1)
    summed = lax.dot_general(
        all_inputs, all_sens, (((0,), (0,)), ((), ())), preferred_element_type=F32
    )
    value_block = part_of(value_rows, dp_pos, block_rows, 0)
    relevance_rows = value_block.astype(F32) * summed
    return (heat_rows[None, None, :], relevance_rows[None])


def solution(mesh):
    placed = (
        P("section", ("groups", "dp"), None, "mp"),
        P("section", ("groups", "dp"), None, "mp"),
        P("section", ("groups", "dp"), None, "mp"),
        P("section", ("groups", "dp"), None, "mp"),
        P("section", "mp", None),
        P("section", "mp", "dp"),
        P(("groups", "dp")),
    )
    return jax.shard_map(
        on_device,
        mesh=mesh,
        in_specs=placed,
        out_specs=(
            P("section", ("groups", "dp"), None),
            P(("groups", "section"), ("mp", "dp"), None),
        ),
        check_vma=False,
    )
```

```python
import functools
import itertools
import math

import jax
import jax.numpy as jnp
from jax import lax
from jax.experimental import pallas as pl
from jax.experimental.pallas import tpu as pltpu
from jax.sharding import PartitionSpec as P

DW = 2560
HD = 128
QH = 20
KVH = 4
EPS = 0.25
F32 = jnp.float32
BF16 = jnp.bfloat16


def stabilize(entries):
    return jnp.where(entries >= 0, entries + EPS, entries - EPS)


VMEM = pl.BlockSpec(memory_space=pltpu.VMEM)
SMEM = pl.BlockSpec(memory_space=pltpu.SMEM)


def by_columns(left, right):
    return lax.dot_general(left, right, (((1,), (1,)), ((), ())), preferred_element_type=F32)


def kernel_call(body, shapes, in_specs, scratch=(), flops=0, nbytes=0, limit=24):
    return pl.pallas_call(
        body,
        out_shape=shapes,
        in_specs=in_specs,
        out_specs=jax.tree.map(lambda _: VMEM, shapes),
        scratch_shapes=scratch,
        compiler_params=pltpu.CompilerParams(vmem_limit_bytes=limit * 2**20),
        cost_estimate=pl.CostEstimate(flops=flops, bytes_accessed=nbytes, transcendentals=0),
    )


def attention_kernel(length, queries, keys, values, probs_t, mixed_gain, value_gain):
    seq_len = queries.shape[0]
    kv_heads = keys.shape[1] // HD
    group_size = queries.shape[1] // HD // kv_heads
    row = lax.broadcasted_iota(jnp.int32, (seq_len, seq_len), 0)
    column = lax.broadcasted_iota(jnp.int32, (seq_len, seq_len), 1)
    allowed = (column <= row) & (column < length[0])
    values_bf = values[...].astype(BF16)
    values_r = values_bf.astype(F32)
    value_gain[...] = values_r / stabilize(values_r)
    for g in range(kv_heads):
        key_head = keys[:, g * HD : (g + 1) * HD]
        value_head = values_bf[:, g * HD : (g + 1) * HD]
        for h in range(g * group_size, (g + 1) * group_size):
            scores = by_columns(queries[:, h * HD : (h + 1) * HD], key_head) / math.sqrt(HD)
            scores = jnp.where(allowed, scores, -1000000000.0)
            weights = jnp.exp(scores - jnp.max(scores, axis=1, keepdims=True))
            probs = weights / jnp.sum(weights, axis=1, keepdims=True)
            probs_t[h] = probs.T.astype(BF16)
            mixed = jnp.dot(probs.astype(BF16), value_head, preferred_element_type=F32)
            mixed_gain[:, h * HD : (h + 1) * HD] = mixed / stabilize(mixed)


def attend(length, queries, keys, values):
    seq_len, width = queries.shape
    shapes = (
        jax.ShapeDtypeStruct((width // HD, seq_len, seq_len), BF16),
        jax.ShapeDtypeStruct((seq_len, width), F32),
        jax.ShapeDtypeStruct(values.shape, F32),
    )
    call = kernel_call(
        attention_kernel, shapes, [SMEM, VMEM, VMEM, VMEM], flops=10**8, nbytes=3 * 10**6
    )
    return call(length, queries, keys, values)


def head_step(back_mixed, probs_t, mixed_gain, value_gain, found):
    heads = probs_t.shape[0]
    kv_heads = value_gain.shape[1] // HD
    group_size = heads // kv_heads
    for g in range(kv_heads):
        total = jnp.zeros((probs_t.shape[1], HD), F32)
        for h in range(g * group_size, (g + 1) * group_size):
            at = slice(h * HD, (h + 1) * HD)
            sens_mixed = (mixed_gain[:, at] * back_mixed[:, at]).astype(BF16)
            total += jnp.dot(probs_t[h], sens_mixed, preferred_element_type=F32)
        at = slice(g * HD, (g + 1) * HD)
        found[:, at] = (value_gain[:, at] * total).astype(BF16)


def sum_heads_kernel(count, product, *refs):
    backs, (probs_t, mixed_gain, value_gain, found, total) = refs[:count], refs[count:]
    back_mixed = product[...]
    for back in backs:
        back_mixed += back[...].astype(F32)
    total[...] = back_mixed
    head_step(total, probs_t, mixed_gain, value_gain, found)


def sum_heads(product, backs, probs_t, mixed_gain, value_gain):
    call = kernel_call(
        functools.partial(sum_heads_kernel, len(backs)),
        jax.ShapeDtypeStruct(value_gain.shape, BF16),
        [VMEM] * (4 + len(backs)),
        [pltpu.VMEM(product.shape, F32)],
        flops=5 * 10**7,
        nbytes=3 * 10**6,
    )
    return call(product, *backs, probs_t, mixed_gain, value_gain)


def sensitivity_kernel(length, inputs, branch, *refs):
    current, sens = refs if len(refs) == 2 else (None, refs[0])
    inputs_f = inputs[...].astype(F32)
    branch_f = branch[...].astype(F32)
    totals = inputs_f + branch_f
    if current is None:
        row = lax.broadcasted_iota(jnp.int32, totals.shape, 0)
        entering = jnp.where(row < length[0], totals, 0.0).astype(BF16).astype(F32)
    else:
        entering = current[...].astype(F32)
    sens[...] = (branch_f * (entering / stabilize(totals)) / stabilize(branch_f)).astype(BF16)


def sensitivity(length, inputs, branch, *current):
    call = kernel_call(
        sensitivity_kernel,
        jax.ShapeDtypeStruct(inputs.shape, BF16),
        [SMEM] + [VMEM] * (2 + len(current)),
        flops=10**7,
        nbytes=10**6,
    )
    return call(length, inputs, branch, *current)


def outgoing_kernel(place, inputs, branch, sens_own, sens_other, value_rows, outgoing):
    core, length = place[0], place[1]
    width = sens_own.shape[1]
    inputs_f = inputs[...].astype(F32)
    totals = inputs_f + branch[...].astype(F32)
    row = lax.broadcasted_iota(jnp.int32, totals.shape, 0)
    entering = jnp.where(row < length, totals, 0.0).astype(BF16).astype(F32)
    own = value_rows[:, pl.ds(pl.multiple_of(core * width, 128), width)]
    other = value_rows[:, pl.ds(pl.multiple_of((1 - core) * width, 128), width)]
    back_inputs = by_columns(sens_own[...], own) + by_columns(sens_other[...], other)
    kept = inputs_f * (entering / stabilize(totals))
    outgoing[...] = (kept + inputs_f * back_inputs).astype(BF16)


def last_outgoing(place, inputs, branch, sens_own, sens_other, value_rows):
    call = kernel_call(
        outgoing_kernel,
        jax.ShapeDtypeStruct(inputs.shape, BF16),
        [SMEM] + [VMEM] * 5,
        flops=2 * 10**8,
        nbytes=2 * 10**6,
    )
    return call(place, inputs, branch, sens_own, sens_other, value_rows)


def product_kernel(use_mine, mine, theirs, block, own, *backs):
    seq_len = own.shape[0]

    def multiply(operand):
        product = by_columns(operand[...], block[...])
        own[...] = product[:seq_len]
        for k, back in enumerate(backs):
            back[...] = product[(k + 1) * seq_len : (k + 2) * seq_len].astype(BF16)

    @pl.when(use_mine[0] == 1)
    def _():
        multiply(mine)

    @pl.when(use_mine[0] == 0)
    def _():
        multiply(theirs)


def spread_products(use_mine, mine, theirs, block, seq_len):
    count = mine.shape[0] // seq_len
    width = block.shape[0]
    shapes = (jax.ShapeDtypeStruct((seq_len, width), F32),) + tuple(
        jax.ShapeDtypeStruct((seq_len, width), BF16) for _ in range(count - 1)
    )
    call = kernel_call(
        product_kernel, shapes, [SMEM, VMEM, VMEM, VMEM], flops=10**9, nbytes=5 * 10**6, limit=32
    )
    return call(use_mine, mine, theirs, block)


def main_kernel(layout, place, sens_own, sens_other, out_block, *refs):
    count = len(layout)
    pieces = refs[:count]
    before, probs_t, mixed_gain, value_gain, found, halves, total = refs[count:]
    pos, core, group, active = place[0], place[1], place[2], place[3]
    width = out_block.shape[1]
    per_core = sens_own.shape[1] // width
    halves[core] = sens_own[...]
    halves[1 - core] = sens_other[...]

    def part(slot):
        owner = pos ^ slot
        start = pl.multiple_of(lax.rem(owner, per_core) * width, 128)
        return halves[owner // per_core, :, pl.ds(start, width)]

    total[...] = by_columns(part(0), out_block[...])
    for piece, (slot, side, start) in zip(pieces, layout):
        at = (group if side == 0 else 1 - group) * (total.shape[1] // 2) + start
        at = pl.ds(pl.multiple_of(at, 128), piece.shape[0])
        total[:, at] += by_columns(part(slot), piece[...])
    head_step(total, probs_t, mixed_gain, value_gain, found)

    @pl.when(active == 0)
    def _():
        found[...] = before[...]


def main_step(place, sens_own, sens_other, out_block, slots, before, probs_t, mixed_gain, value_gain):
    layout, pieces = [], []
    for k, sides in enumerate(slots):
        for side in range(2):
            start = 0
            for piece in sides[side]:
                layout.append((k + 1, side, start))
                pieces.append(piece)
                start += piece.shape[0]
    seq_len, half_width = sens_own.shape
    call = kernel_call(
        functools.partial(main_kernel, tuple(layout)),
        jax.ShapeDtypeStruct(value_gain.shape, BF16),
        [SMEM] + [VMEM] * (7 + len(pieces)),
        [pltpu.VMEM((2, seq_len, half_width), BF16), pltpu.VMEM(mixed_gain.shape, F32)],
        flops=10**9,
        nbytes=8 * 10**6,
        limit=32,
    )
    return call(
        place, sens_own, sens_other, out_block, *pieces, before, probs_t, mixed_gain, value_gain
    )


def turn_kernel(*refs):
    *pieces, turned = refs
    for k, piece in enumerate(pieces):
        rows = piece.shape[0]
        turned[:, k * rows : (k + 1) * rows] = piece[...].astype(F32).T.astype(BF16)


def turned_side_by_side(pieces):
    rows, width = pieces[0].shape
    shape = jax.ShapeDtypeStruct((width, rows * len(pieces)), BF16)
    return kernel_call(turn_kernel, shape, [VMEM] * len(pieces), nbytes=10**6)(*pieces)


def relevance_kernel(count, core, inputs_t, value_block, *refs):
    own, (other, relevance) = refs[:count], refs[count:]
    seq_len, width = own[0].shape
    mine = jnp.zeros((inputs_t.shape[0], width), F32)
    for k in range(count):
        tokens = inputs_t[:, k * seq_len : (k + 1) * seq_len]
        mine += jnp.dot(tokens, own[k][...], preferred_element_type=F32)
    theirs = jnp.dot(inputs_t[...], other[...], preferred_element_type=F32)
    at = pl.ds(pl.multiple_of(core[0] * width, 128), width)
    relevance[:, at] = value_block[:, at].astype(F32) * mine
    at = pl.ds(pl.multiple_of((1 - core[0]) * width, 128), width)
    relevance[:, at] = value_block[:, at].astype(F32) * theirs


def relevance_step(core, inputs_t, value_block, own, other):
    call = kernel_call(
        functools.partial(relevance_kernel, len(own)),
        jax.ShapeDtypeStruct(value_block.shape, F32),
        [SMEM] + [VMEM] * (3 + len(own)),
        flops=2 * 10**8,
        nbytes=2 * 10**6,
    )
    return call(core, inputs_t, value_block, *own, other)


def moved(shard, axes, target):
    sizes = [lax.axis_size(axis) for axis in axes]
    places = list(itertools.product(*[range(size) for size in sizes]))
    index = {place: i for i, place in enumerate(places)}
    pairs = [(index[place], index[target(*place)]) for place in places if target(*place) is not None]
    return lax.ppermute(shard, axes, pairs)


def along_dp(shard, by):
    peers = lax.axis_size("dp")
    return moved(shard, ("dp",), lambda i: ((i + by) % peers,)) if by else shard


def other_core(shard):
    return moved(shard, ("mp",), lambda c: (1 - c,))


def from_next_section(shard):
    return moved(shard, ("section",), lambda s: (s - 1,) if s > 0 else None)


def ordered(first_is_mine, mine, theirs, axis):
    return jnp.concatenate(
        [jnp.where(first_is_mine, mine, theirs), jnp.where(first_is_mine, theirs, mine)], axis
    )


def part_of(array, index, width, axis):
    return lax.dynamic_slice_in_dim(array, index * width, width, axis)


def once(array, *others):
    return lax.optimization_barrier((array,) + others)[0]


def early_move(shard, axes, target):
    last = lax.axis_size("section") - 1
    at = axes.index("section")
    return moved(shard, axes, lambda *place: target(*place) if place[at] < last else None)


def between(shard, pairs):
    return early_move(shard, ("dp", "section"), lambda i, s: (pairs[i], s) if i in pairs else None)


def swap_groups(shard):
    return early_move(shard, ("groups", "section"), lambda g, s: (1 - g, s))


MIDDLE = {1: 2, 2: 1}
OUTWARD = {1: 0, 2: 3}


def start_gather(mine, *others):
    peers = lax.axis_size("dp")
    pos = lax.axis_index("dp")
    if peers != 4:
        return [between(mine, {i: i ^ k for i in range(peers)}) for k in range(1, peers)], *others[-2:]
    cut = [mine.shape[0] * 3 // 5]
    pair = between(mine, {i: i ^ 1 for i in range(peers)})
    near = between(mine, MIDDLE)
    pair, near, *others = lax.optimization_barrier((pair, near, *others))
    crossed = between(pair, MIDDLE)
    relayed = between(near, OUTWARD)
    pair_swapped = swap_groups(pair)
    crossed, relayed, pair_swapped = lax.optimization_barrier((crossed, relayed, pair_swapped))
    second = [
        jnp.where((pos == 1) | (pos == 2), *both)
        for both in zip(jnp.split(crossed, cut), jnp.split(relayed, cut))
    ]
    return [pair, pair_swapped, second, jnp.split(near, cut)], *others[-2:]


def finish_gather(started):
    peers = lax.axis_size("dp")
    pos = lax.axis_index("dp")
    if peers != 4:
        return [([block], [swap_groups(block)]) for block in started]
    pair, pair_swapped, second, near = started
    third = [
        jnp.where((pos == 1) | (pos == 2), direct, between(far, OUTWARD))
        for direct, far in zip(near, second)
    ]
    return [
        ([pair], [pair_swapped]),
        (second, [swap_groups(piece) for piece in second]),
        (third, [swap_groups(piece) for piece in third]),
    ]


def spread_product(sens_branch, out_block):
    axes = ("dp", "section", "mp")
    peers, cores = lax.axis_size("dp"), lax.axis_size("mp")
    last = lax.axis_size("section") - 1
    pos, core = lax.axis_index("dp"), lax.axis_index("mp")
    seq_len = sens_branch.shape[0]
    width = out_block.shape[1]
    per_core = peers // cores
    arrived = []
    for k in range(peers):
        to = lax.rem(pos + k, peers)
        part = part_of(sens_branch, lax.rem(to, per_core), width, 1)
        if k:
            part = moved(
                part,
                axes,
                lambda i, s, c: ((i + k) % peers, s, c)
                if s == last and c == (i + k) % peers // per_core
                else None,
            )
        arrived.append(part)
    mine = jnp.concatenate(arrived, 0)
    theirs = moved(
        mine,
        axes,
        lambda i, s, c: (i, s, 1 - c) if s == last and c == i // per_core else None,
    )
    if width % 128 == 0:
        use_mine = (core == pos // per_core).astype(jnp.int32)[None]
        own, *sent = spread_products(use_mine, mine, theirs, out_block, seq_len)
    else:
        product = by_columns(jnp.where(core == pos // per_core, mine, theirs), out_block)
        own, *sent = jnp.split(product, peers, axis=0)
    backs = [
        moved(
            sent[k - 1].astype(BF16),
            axes,
            lambda i, s, c: ((i - k) % peers, s, c) if s == last else None,
        )
        for k in range(1, peers)
    ]
    return own, backs


def on_device(hidden_in, attn_out, queries, keys, value_weight, out_weight, lengths):
    inputs = hidden_in[0, 0]
    branch = attn_out[0, 0]
    query_rows = queries[0, 0]
    key_rows = keys[0, 0]
    value_rows = value_weight[0]
    out_block = out_weight[0]
    seq_len, half_width = inputs.shape
    kv_width = key_rows.shape[1]
    sections = lax.axis_size("section")
    section_pos = lax.axis_index("section")
    group_pos = lax.axis_index("groups")
    peers = lax.axis_size("dp")
    dp_pos = lax.axis_index("dp")
    core_pos = lax.axis_index("mp")
    head_rows, block_width = out_block.shape
    is_last = section_pos == sections - 1

    totals = inputs.astype(F32) + branch.astype(F32)
    valid_rows = (lax.iota(jnp.int32, seq_len) < lengths[0]).astype(F32)
    current = (totals * valid_rows[:, None]).astype(BF16)

    def kept_of(entering):
        return inputs.astype(F32) * (entering.astype(F32) / stabilize(totals))

    def core_exchange(mine, take):
        return moved(
            mine, ("section", "mp"), lambda s, c: (s, 1 - c) if take(s == sections - 1) else None
        )

    def values_of(take):
        value_part = jnp.dot(inputs, value_rows, preferred_element_type=F32)
        part_mine = part_of(value_part, core_pos, kv_width, 1)
        part_other = part_of(value_part, 1 - core_pos, kv_width, 1)
        return part_mine + core_exchange(part_other.astype(BF16), take).astype(F32)

    def last_section():
        values_f = values_of(lambda last: last)
        rest = attend(lengths, query_rows, key_rows, values_f)
        sens_branch = sensitivity(lengths, inputs, branch)
        own, backs = spread_product(sens_branch, out_block)
        leaves, tree = jax.tree.flatten(early_shapes[-1])
        filler = lengths[0].astype(BF16)
        unused = [jnp.full(leaf.shape, filler + k, BF16) for k, leaf in enumerate(leaves)]
        own, *unused = lax.optimization_barrier((own, *unused))
        if peers > 4:
            for back in backs:
                own = own + back.astype(F32)
            backs = []
        found = sum_heads(own, backs, *rest)
        other = core_exchange(found, lambda last: last)
        place = jnp.stack([core_pos, lengths[0]])
        outgoing = last_outgoing(place, inputs, branch, found, other, value_rows)
        return values_f, found, outgoing, jax.tree.unflatten(tree, unused)

    def early_section():
        mine = part_of(out_block, group_pos, head_rows // 2, 0)
        values_f = values_of(lambda last: not last)
        found = jnp.full((seq_len, kv_width), lengths[0].astype(BF16))
        outgoing = jnp.full((seq_len, half_width), lengths[0].astype(BF16))
        started, found, outgoing = start_gather(mine, values_f, found, outgoing)
        return values_f, found, outgoing, started

    early_shapes = jax.eval_shape(early_section)
    values_f, sens_values, outgoing, started = lax.cond(is_last, last_section, early_section)
    arrived = from_next_section(outgoing)
    slots = finish_gather(started)
    rest = attend(lengths, query_rows, key_rows, values_f)

    def inputs_of_all(*others):
        rows = once(inputs, *others)
        pieces = [
            along_dp(part_of(rows, lax.rem(dp_pos + k, peers), block_rows, 1), k)
            for k in range(peers)
        ]
        if block_rows % 8 == 0 and peers <= 8:
            return turned_side_by_side(pieces)
        return jnp.concatenate(pieces, 0).T

    block_rows = half_width // peers
    value_block = part_of(value_rows, dp_pos, block_rows, 0)
    for turn in range(1, sections):
        active = section_pos == sections - 1 - turn
        current = jnp.where(active, arrived, current)
        sens_branch = sensitivity(lengths, inputs, branch, arrived)
        sens_other = core_exchange(sens_branch, lambda last: not last)
        if block_width % 128 == 0:
            place = jnp.stack([dp_pos, core_pos, group_pos, active.astype(jnp.int32)])
            if turn == 1:
                behind = [slots[-2][1], slots[-1][0], slots[-1][1][1:]]
                inputs_t = inputs_of_all(sens_other, *jax.tree.leaves(behind))
                sens_other, inputs_t, value_block, *_ = lax.optimization_barrier(
                    (sens_other, inputs_t, value_block)
                )
            found = main_step(
                place, sens_branch, sens_other, out_block, slots, sens_values, *rest
            )
        else:
            if turn == 1:
                inputs_t = inputs_of_all(sens_other)
            share = head_rows // 2
            own_rows = part_of(out_block, group_pos, share, 0)
            other_rows = part_of(out_block, 1 - group_pos, share, 0)
            sens_full = ordered(core_pos == 0, sens_branch, sens_other, 1)
            halves = [jnp.zeros((seq_len, share), F32) for _ in range(2)]
            for k, blocks in enumerate([([own_rows], [other_rows])] + slots):
                part = part_of(sens_full, dp_pos ^ k, block_width, 1)
                for side in range(2):
                    halves[side] += jnp.concatenate(
                        [by_columns(part, piece) for piece in blocks[side]], 1
                    )
            found = sum_heads(ordered(group_pos == 0, halves[0], halves[1], 1), [], *rest)
            found = jnp.where(active, found, sens_values)
        sens_values = found
        if turn + 1 < sections:
            sens_all = ordered(
                core_pos == 0, found, core_exchange(found, lambda last: not last), 1
            )
            back_inputs = by_columns(sens_all, value_rows)
            outgoing = kept_of(current) + inputs.astype(F32) * back_inputs
            arrived = from_next_section(outgoing.astype(BF16))

    heat_part = jnp.sum(kept_of(current), axis=1)
    heat_part += jnp.sum(sens_values.astype(F32) * values_f, axis=1)
    heat_rows = (heat_part + other_core(heat_part)) / DW

    own_sens = [along_dp(sens_values, k) for k in range(peers)]
    *own_sens, heat_rows = lax.optimization_barrier((*own_sens, heat_rows))
    other_sens = other_core(jnp.concatenate(own_sens, 0))
    if block_rows % 8 == 0 and peers <= 8:
        relevance_rows = relevance_step(
            core_pos[None], inputs_t, value_block, own_sens, other_sens
        )
    else:
        all_sens = ordered(core_pos == 0, jnp.concatenate(own_sens, 0), other_sens, 1)
        relevance_rows = value_block.astype(F32) * jnp.dot(
            inputs_t, all_sens, preferred_element_type=F32
        )
    return (heat_rows[None, None, :], relevance_rows[None])


def solution(mesh):
    placed = (
        P("section", ("groups", "dp"), None, "mp"),
        P("section", ("groups", "dp"), None, "mp"),
        P("section", ("groups", "dp"), None, "mp"),
        P("section", ("groups", "dp"), None, "mp"),
        P("section", "mp", None),
        P("section", "mp", "dp"),
        P(("groups", "dp")),
    )
    return jax.shard_map(
        on_device,
        mesh=mesh,
        in_specs=placed,
        out_specs=(
            P("section", ("groups", "dp"), None),
            P(("groups", "section"), ("mp", "dp"), None),
        ),
        check_vma=False,
    )
```

```python
import functools
import itertools
import math

import jax
import jax.numpy as jnp
from jax import lax
from jax.experimental import pallas as pl
from jax.experimental.pallas import tpu as pltpu
from jax.sharding import PartitionSpec as P

DW = 2560
HD = 128
QH = 20
KVH = 4
EPS = 0.25
F32 = jnp.float32
BF16 = jnp.bfloat16


def stabilize(entries):
    return jnp.where(entries >= 0, entries + EPS, entries - EPS)


VMEM = pl.BlockSpec(memory_space=pltpu.VMEM)
SMEM = pl.BlockSpec(memory_space=pltpu.SMEM)


def by_columns(left, right):
    return lax.dot_general(left, right, (((1,), (1,)), ((), ())), preferred_element_type=F32)


def kernel_call(body, shapes, in_specs, scratch=(), flops=0, nbytes=0, limit=24):
    return pl.pallas_call(
        body,
        out_shape=shapes,
        in_specs=in_specs,
        out_specs=jax.tree.map(lambda _: VMEM, shapes),
        scratch_shapes=scratch,
        compiler_params=pltpu.CompilerParams(vmem_limit_bytes=limit * 2**20),
        cost_estimate=pl.CostEstimate(flops=flops, bytes_accessed=nbytes, transcendentals=0),
    )


def attention_kernel(length, queries, keys, values, probs_t, mixed_gain, value_gain):
    seq_len = queries.shape[0]
    kv_heads = keys.shape[1] // HD
    group_size = queries.shape[1] // HD // kv_heads
    row = lax.broadcasted_iota(jnp.int32, (seq_len, seq_len), 0)
    column = lax.broadcasted_iota(jnp.int32, (seq_len, seq_len), 1)
    allowed = (column <= row) & (column < length[0])
    values_bf = values[...].astype(BF16)
    values_r = values_bf.astype(F32)
    value_gain[...] = values_r / stabilize(values_r)
    for g in range(kv_heads):
        key_head = keys[:, g * HD : (g + 1) * HD]
        value_head = values_bf[:, g * HD : (g + 1) * HD]
        for h in range(g * group_size, (g + 1) * group_size):
            scores = by_columns(queries[:, h * HD : (h + 1) * HD], key_head) / math.sqrt(HD)
            scores = jnp.where(allowed, scores, -1000000000.0)
            weights = jnp.exp(scores - jnp.max(scores, axis=1, keepdims=True))
            probs = weights / jnp.sum(weights, axis=1, keepdims=True)
            probs_t[h] = probs.T.astype(BF16)
            mixed = jnp.dot(probs.astype(BF16), value_head, preferred_element_type=F32)
            mixed_gain[:, h * HD : (h + 1) * HD] = mixed / stabilize(mixed)


def attend(length, queries, keys, values):
    seq_len, width = queries.shape
    shapes = (
        jax.ShapeDtypeStruct((width // HD, seq_len, seq_len), BF16),
        jax.ShapeDtypeStruct((seq_len, width), F32),
        jax.ShapeDtypeStruct(values.shape, F32),
    )
    call = kernel_call(
        attention_kernel, shapes, [SMEM, VMEM, VMEM, VMEM], flops=10**8, nbytes=3 * 10**6
    )
    return call(length, queries, keys, values)


def head_step(back_mixed, probs_t, mixed_gain, value_gain, found):
    heads = probs_t.shape[0]
    kv_heads = value_gain.shape[1] // HD
    group_size = heads // kv_heads
    for g in range(kv_heads):
        total = jnp.zeros((probs_t.shape[1], HD), F32)
        for h in range(g * group_size, (g + 1) * group_size):
            at = slice(h * HD, (h + 1) * HD)
            sens_mixed = (mixed_gain[:, at] * back_mixed[:, at]).astype(BF16)
            total += jnp.dot(probs_t[h], sens_mixed, preferred_element_type=F32)
        at = slice(g * HD, (g + 1) * HD)
        found[:, at] = (value_gain[:, at] * total).astype(BF16)


def sum_heads_kernel(count, product, *refs):
    backs, (probs_t, mixed_gain, value_gain, found, total) = refs[:count], refs[count:]
    back_mixed = product[...]
    for back in backs:
        back_mixed += back[...].astype(F32)
    total[...] = back_mixed
    head_step(total, probs_t, mixed_gain, value_gain, found)


def sum_heads(product, backs, probs_t, mixed_gain, value_gain):
    call = kernel_call(
        functools.partial(sum_heads_kernel, len(backs)),
        jax.ShapeDtypeStruct(value_gain.shape, BF16),
        [VMEM] * (4 + len(backs)),
        [pltpu.VMEM(product.shape, F32)],
        flops=5 * 10**7,
        nbytes=3 * 10**6,
    )
    return call(product, *backs, probs_t, mixed_gain, value_gain)


def product_kernel(use_mine, mine, theirs, block, own, *backs):
    seq_len = own.shape[0]

    def multiply(operand):
        product = by_columns(operand[...], block[...])
        own[...] = product[:seq_len]
        for k, back in enumerate(backs):
            back[...] = product[(k + 1) * seq_len : (k + 2) * seq_len].astype(BF16)

    @pl.when(use_mine[0] == 1)
    def _():
        multiply(mine)

    @pl.when(use_mine[0] == 0)
    def _():
        multiply(theirs)


def spread_products(use_mine, mine, theirs, block, seq_len):
    count = mine.shape[0] // seq_len
    width = block.shape[0]
    shapes = (jax.ShapeDtypeStruct((seq_len, width), F32),) + tuple(
        jax.ShapeDtypeStruct((seq_len, width), BF16) for _ in range(count - 1)
    )
    call = kernel_call(
        product_kernel, shapes, [SMEM, VMEM, VMEM, VMEM], flops=10**9, nbytes=5 * 10**6, limit=32
    )
    return call(use_mine, mine, theirs, block)


def sensitivity_kernel(length, inputs, branch, *refs):
    current, sens = refs if len(refs) == 2 else (None, refs[0])
    inputs_f = inputs[...].astype(F32)
    branch_f = branch[...].astype(F32)
    totals = inputs_f + branch_f
    if current is None:
        row = lax.broadcasted_iota(jnp.int32, totals.shape, 0)
        entering = jnp.where(row < length[0], totals, 0.0).astype(BF16).astype(F32)
    else:
        entering = current[...].astype(F32)
    sens[...] = (branch_f * (entering / stabilize(totals)) / stabilize(branch_f)).astype(BF16)


def sensitivity(length, inputs, branch, *current):
    call = kernel_call(
        sensitivity_kernel,
        jax.ShapeDtypeStruct(inputs.shape, BF16),
        [SMEM] + [VMEM] * (2 + len(current)),
        flops=10**7,
        nbytes=10**6,
    )
    return call(length, inputs, branch, *current)


def outgoing_kernel(place, inputs, branch, sens_own, sens_other, value_rows, outgoing):
    core, length = place[0], place[1]
    width = sens_own.shape[1]
    inputs_f = inputs[...].astype(F32)
    totals = inputs_f + branch[...].astype(F32)
    row = lax.broadcasted_iota(jnp.int32, totals.shape, 0)
    entering = jnp.where(row < length, totals, 0.0).astype(BF16).astype(F32)
    own = value_rows[:, pl.ds(pl.multiple_of(core * width, 128), width)]
    other = value_rows[:, pl.ds(pl.multiple_of((1 - core) * width, 128), width)]
    back_inputs = by_columns(sens_own[...], own) + by_columns(sens_other[...], other)
    kept = inputs_f * (entering / stabilize(totals))
    outgoing[...] = (kept + inputs_f * back_inputs).astype(BF16)


def last_outgoing(place, inputs, branch, sens_own, sens_other, value_rows):
    call = kernel_call(
        outgoing_kernel,
        jax.ShapeDtypeStruct(inputs.shape, BF16),
        [SMEM] + [VMEM] * 5,
        flops=2 * 10**8,
        nbytes=2 * 10**6,
    )
    return call(place, inputs, branch, sens_own, sens_other, value_rows)


def pair_attention_kernel(place, kept, got, probs_out, gain_t, value_gain, values):
    seq_len = kept.shape[0] - 8
    width = kept.shape[1] - 2 * HD
    heads = width // HD
    row = lax.broadcasted_iota(jnp.int32, (seq_len, seq_len), 0)
    column = lax.broadcasted_iota(jnp.int32, (seq_len, seq_len), 1)

    @pl.when(place[3] == 1)
    def _():
        for half, b in ((kept, place[4]), (got, 1 - place[4])):
            tokens = pl.ds(pl.multiple_of(b * seq_len, 128), seq_len)
            length = jnp.max(half[seq_len:, :HD].astype(F32), axis=0, keepdims=True)
            allowed = (column <= row) & (column.astype(F32) < length)
            value_head = half[:seq_len, width + HD :]
            value_f = value_head.astype(F32)
            values[tokens] = value_f
            value_gain[tokens] = value_f / stabilize(value_f)
            stacked = [half[:seq_len, h * HD : (h + 1) * HD] for h in range(heads)]
            scores = by_columns(
                jnp.concatenate(stacked, 0), half[:seq_len, width : width + HD]
            ) / math.sqrt(HD)
            scores = jnp.where(jnp.concatenate([allowed] * heads, 0), scores, -1000000000.0)
            weights = jnp.exp(scores - jnp.max(scores, axis=1, keepdims=True))
            probs = (weights / jnp.sum(weights, axis=1, keepdims=True)).astype(BF16)
            mixed = jnp.dot(probs, value_head, preferred_element_type=F32)
            gain = mixed / stabilize(mixed)
            for h in range(heads):
                at = slice(h * seq_len, (h + 1) * seq_len)
                probs_out[b, h] = probs[at]
                gain_t[h * HD : (h + 1) * HD, tokens] = gain[at].T


def pair_attend(place, kept, got):
    seq_len, width = kept.shape[0] - 8, kept.shape[1] - 2 * HD
    shapes = (
        jax.ShapeDtypeStruct((2, width // HD, seq_len, seq_len), BF16),
        jax.ShapeDtypeStruct((width, 2 * seq_len), F32),
        jax.ShapeDtypeStruct((2 * seq_len, HD), F32),
        jax.ShapeDtypeStruct((2 * seq_len, HD), F32),
    )
    return kernel_call(
        pair_attention_kernel, shapes, [SMEM, VMEM, VMEM], flops=10**8, nbytes=3 * 10**6
    )(place, kept, got)


def main_kernel(count, place, *refs):
    sens, out_block, (before, kept_sum, probs, gain_t, value_gain, values) = refs[:4], refs[4], refs[5:11]
    own_pieces, other_pieces = refs[11 : 11 + count], refs[11 + count : 11 + 2 * count]
    found, halves, total = refs[11 + 2 * count :]
    pos, core, group, active, side = [place[i] for i in range(5)]
    seq_len, half_width = sens[0].shape
    width = out_block.shape[1]
    per_core = half_width // width
    quarter = own_pieces[0].shape[0]

    @pl.when(active == 0)
    def _():
        found[...] = before[...]

    @pl.when(active == 1)
    def _():
        for j, half in ((0, core), (1, 1 - core)):
            for i, sequence in ((0, side), (1, 1 - side)):
                rows = pl.ds(pl.multiple_of(sequence * seq_len, 128), seq_len)
                halves[half, rows, :] = sens[2 * j + i][...]

        def part(k):
            owner = lax.rem(pos - k + count + 1, count + 1)
            start = pl.multiple_of(lax.rem(owner, per_core) * width, 128)
            return halves[owner // per_core, :, pl.ds(start, width)]

        rows = pl.ds(pl.multiple_of(side * 2 * quarter, 16), 2 * quarter)
        total[...] = by_columns(out_block[rows, :], part(0))
        for k in range(count):
            operand = part(k + 1)
            for at, piece in ((group, own_pieces[k]), (1 - group, other_pieces[k])):
                rows = pl.ds(pl.multiple_of(at * quarter, 8), quarter)
                total[rows, :] += by_columns(piece[...], operand)
        heats = []
        for b in range(2):
            tokens = slice(b * seq_len, (b + 1) * seq_len)
            back_values = jnp.zeros((HD, seq_len), F32)
            for h in range(probs.shape[1]):
                at = slice(h * HD, (h + 1) * HD)
                sens_mixed = (gain_t[at, tokens] * total[at, tokens]).astype(BF16)
                back_values += jnp.dot(sens_mixed, probs[b, h], preferred_element_type=F32)
            sens_values = (value_gain[tokens] * back_values.T).astype(BF16)
            found[tokens] = sens_values
            heats.append(by_token(sens_values.astype(F32) * values[tokens]))
        mine = jnp.where(side == 0, heats[0], heats[1]) + kept_sum[...]
        found[2 * seq_len :] = heat_rows_of(mine, jnp.where(side == 0, heats[1], heats[0]))


def by_token(array):
    groups = [array[:, at : at + 128] for at in range(0, array.shape[1], 128)]
    return jnp.sum(sum(groups).T, axis=0, keepdims=True)


def heat_rows_of(mine, theirs):
    rows = []
    for heat in (mine, theirs):
        high = heat.astype(BF16).astype(F32)
        rows += [high, heat - high]
    rows.append(jnp.zeros((12, mine.shape[1]), F32))
    return jnp.concatenate(rows, 0).astype(BF16)


def pack_kernel(place, found, got, values, kept_sum, packed):
    side = place[4]
    seq_len = found.shape[0]

    @pl.when(place[3] == 1)
    def _():
        mine, theirs = (
            jnp.where(side == 0, array[:, :HD], array[:, HD:]) for array in (found, got)
        )
        packed[:seq_len] = jnp.where(side == 0, mine, theirs)
        packed[seq_len : 2 * seq_len] = jnp.where(side == 0, theirs, mine)
        heat = by_token(found[...].astype(F32) * values[...]) + kept_sum[...]
        packed[2 * seq_len :] = heat_rows_of(heat, jnp.zeros_like(heat))


def pack_last(place, found, got, values, kept_sum):
    seq_len = found.shape[0]
    shape = jax.ShapeDtypeStruct((2 * seq_len + 16, HD), BF16)
    return kernel_call(pack_kernel, shape, [SMEM] + [VMEM] * 4, nbytes=10**6)(
        place, found, got, values, kept_sum
    )


def main_step(place, sens, out_block, quarters, before, kept_sum, rest):
    count = len(quarters[0])
    seq_len, half_width = sens[0].shape
    operands = [*sens, out_block, before, kept_sum, *rest, *quarters[0], *quarters[1]]
    call = kernel_call(
        functools.partial(main_kernel, count),
        jax.ShapeDtypeStruct(before.shape, BF16),
        [SMEM] + [VMEM] * len(operands),
        [pltpu.VMEM((2, 2 * seq_len, half_width), BF16), pltpu.VMEM(rest[1].shape, F32)],
        flops=10**9,
        nbytes=6 * 10**6,
        limit=32,
    )
    return call(place, *operands)


def main_plain(place, sens, out_block, quarters, before, kept_sum, rest):
    pos, core, group, active, side = [place[i] for i in range(5)]
    seq_len = sens[0].shape[0]
    width = out_block.shape[1]
    mine, theirs = (ordered(side == 0, sens[2 * j], sens[2 * j + 1], 0) for j in range(2))
    sens_full = ordered(core == 0, mine, theirs, 1)
    count = len(quarters[0])
    quarter = quarters[0][0].shape[0]
    totals = [0.0, 0.0]
    for k in range(count + 1):
        operand = part_of(sens_full, lax.rem(pos - k + count + 1, count + 1), width, 1)
        for half in range(2):
            if k:
                piece = quarters[half][k - 1]
            else:
                at = 2 * side + (group if half == 0 else 1 - group)
                piece = part_of(out_block, at, quarter, 0)
            totals[half] += by_columns(piece, operand)
    total = ordered(group == 0, totals[0], totals[1], 0)
    probs, gain_t, value_gain, values = rest
    sens_mixed = (gain_t * total).astype(BF16).reshape(-1, HD, 2, seq_len)
    back_values = jnp.einsum("hdbt,bhts->bsd", sens_mixed, probs, preferred_element_type=F32)
    found = (value_gain * back_values.reshape(2 * seq_len, HD)).astype(BF16)
    heats = jnp.sum((found.astype(F32) * values).reshape(2, 1, seq_len, HD), axis=3)
    mine = jnp.where(side == 0, heats[0], heats[1]) + kept_sum
    rows = heat_rows_of(mine, jnp.where(side == 0, heats[1], heats[0]))
    return jnp.where(active == 1, jnp.concatenate([found, rows], 0), before)


def turn_kernel(place, *refs):
    *pieces, turned = refs
    count = len(pieces)
    for k, piece in enumerate(pieces):
        rows = piece.shape[0]
        at = pl.multiple_of(lax.rem(place[0] - k + count, count) * rows, 128)
        turned[:, pl.ds(at, rows)] = piece[...].astype(F32).T.astype(BF16)


def turned_side_by_side(place, pieces):
    rows, width = pieces[0].shape
    shape = jax.ShapeDtypeStruct((width, rows * len(pieces)), BF16)
    specs = [SMEM] + [VMEM] * len(pieces)
    return kernel_call(turn_kernel, shape, specs, nbytes=10**6)(place, *pieces)


def heat_of(own, other, place, count):
    partner = lax.rem(2 * place[4] - 1 + count, count)
    size = own[0].shape[0]
    heat = 0.0
    for source in (own, [other[k * size : (k + 1) * size] for k in range(count)]):
        rows = [source[k][size - 16 :].astype(F32) for k in range(count)]
        heat += rows[0][0:1] + rows[0][1:2]
        for k in {1 % count, count - 1}:
            heat += jnp.where(partner == k, rows[k][2:3] + rows[k][3:4], 0.0)
    return heat / DW


def relevance_kernel(count, place, inputs_t, value_rows, *refs):
    own, (other, relevance, heat) = refs[:count], refs[count:]
    pos, core = place[0], place[1]
    size = own[0].shape[0]
    rows = size - 16
    relevance[...] = jnp.zeros_like(relevance)
    for k in range(count):
        source = lax.rem(pos - k + count, count)
        tokens = inputs_t[:, pl.ds(pl.multiple_of(source // 2 * rows, 128), rows)]
        for c, sens in ((core, own[k][:rows]), (1 - core, other[k * size : k * size + rows])):
            head = 2 * c + lax.rem(source, 2)
            at = pl.ds(pl.multiple_of(head * HD, 128), HD)
            relevance[:, at] += jnp.dot(tokens, sens, preferred_element_type=F32)
    rows = relevance.shape[0]
    value_block = value_rows[pl.ds(pl.multiple_of(pos * rows, 16), rows), :]
    relevance[...] *= value_block.astype(F32)
    heat[...] = heat_of(own, other, place, count)


def relevance_step(place, inputs_t, value_rows, own, other):
    shapes = (
        jax.ShapeDtypeStruct((inputs_t.shape[0], value_rows.shape[1]), F32),
        jax.ShapeDtypeStruct((1, (own[0].shape[0] - 16) // 2), F32),
    )
    call = kernel_call(
        functools.partial(relevance_kernel, len(own)),
        shapes,
        [SMEM] + [VMEM] * (3 + len(own)),
        flops=2 * 10**8,
        nbytes=2 * 10**6,
    )
    return call(place, inputs_t, value_rows, *own, other)


def relevance_plain(place, inputs_t, value_rows, own, other):
    pos, core = place[0], place[1]
    count, size = len(own), own[0].shape[0]
    rows = size - 16
    seq_len = rows // 2
    heat = heat_of(own, other, place, count)
    other = [other[k * size : k * size + rows] for k in range(count)]
    own = [piece[:rows] for piece in own]
    even = lax.rem(pos, 2) == 0
    by_core = []
    for sens in (own, other):
        same = jnp.concatenate([sens[k] for k in range(0, count, 2)], 0)
        cross = jnp.concatenate(
            [jnp.where(even, sens[(k - 1) % count], sens[k + 1]) for k in range(0, count, 2)], 0
        )
        by_core.append(ordered(even, same, cross, 1))
    inputs = inputs_t.reshape(-1, count, seq_len)
    tokens = []
    for k in range(0, count, 2):
        tokens.append(jnp.where(even, inputs[:, k], inputs[:, k + 1]))
        tokens.append(jnp.where(even, inputs[:, (k - 1) % count], inputs[:, k]))
    all_sens = ordered(core == 0, by_core[0], by_core[1], 1)
    summed = jnp.dot(jnp.concatenate(tokens, 1), all_sens, preferred_element_type=F32)
    return part_of(value_rows, pos, inputs_t.shape[0], 0).astype(F32) * summed, heat


def moved(shard, axes, target):
    sizes = [lax.axis_size(axis) for axis in axes]
    places = list(itertools.product(*[range(size) for size in sizes]))
    index = {place: i for i, place in enumerate(places)}
    pairs = [(index[place], index[target(*place)]) for place in places if target(*place) is not None]
    return lax.ppermute(shard, axes, pairs)


def along_dp(shard, by):
    peers = lax.axis_size("dp")
    return moved(shard, ("dp",), lambda i: ((i + by) % peers,)) if by else shard


def other_core(shard):
    return moved(shard, ("mp",), lambda c: (1 - c,))


def from_next_section(shard):
    return moved(shard, ("section",), lambda s: (s - 1,) if s > 0 else None)


def ordered(first_is_mine, mine, theirs, axis):
    return jnp.concatenate(
        [jnp.where(first_is_mine, mine, theirs), jnp.where(first_is_mine, theirs, mine)], axis
    )


def part_of(array, index, width, axis):
    return lax.dynamic_slice_in_dim(array, index * width, width, axis)


def once(array, *others):
    return lax.optimization_barrier((array,) + others)[0]


def early_move(shard, axes, target):
    last = lax.axis_size("section") - 1
    at = axes.index("section")
    return moved(shard, axes, lambda *place: target(*place) if place[at] < last else None)


def early_pair(shard):
    return early_move(shard, ("dp", "section"), lambda i, s: (i ^ 1, s))


def early_core(shard):
    return early_move(shard, ("section", "mp"), lambda s, c: (s, 1 - c))


def spread_product(sens_branch, out_block):
    axes = ("dp", "section", "mp")
    peers, cores = lax.axis_size("dp"), lax.axis_size("mp")
    last = lax.axis_size("section") - 1
    pos, core = lax.axis_index("dp"), lax.axis_index("mp")
    seq_len = sens_branch.shape[0]
    width = out_block.shape[1]
    per_core = peers // cores
    arrived = []
    for k in range(peers):
        to = lax.rem(pos + k, peers)
        part = part_of(sens_branch, lax.rem(to, per_core), width, 1)
        if k:
            part = moved(
                part,
                axes,
                lambda i, s, c: ((i + k) % peers, s, c)
                if s == last and c == (i + k) % peers // per_core
                else None,
            )
        arrived.append(part)
    mine = jnp.concatenate(arrived, 0)
    theirs = moved(
        mine,
        axes,
        lambda i, s, c: (i, s, 1 - c) if s == last and c == i // per_core else None,
    )
    if width % 128 == 0:
        use_mine = (core == pos // per_core).astype(jnp.int32)[None]
        own, *sent = spread_products(use_mine, mine, theirs, out_block, seq_len)
    else:
        product = by_columns(jnp.where(core == pos // per_core, mine, theirs), out_block)
        own, *sent = jnp.split(product, peers, axis=0)
    backs = [
        moved(
            sent[k - 1].astype(BF16),
            axes,
            lambda i, s, c: ((i - k) % peers, s, c) if s == last else None,
        )
        for k in range(1, peers)
    ]
    return own, backs


def on_device(hidden_in, attn_out, queries, keys, value_weight, out_weight, lengths):
    inputs = hidden_in[0, 0]
    branch = attn_out[0, 0]
    query_rows = queries[0, 0]
    key_rows = keys[0, 0]
    value_rows = value_weight[0]
    out_block = out_weight[0]
    seq_len, half_width = inputs.shape
    kv_width = key_rows.shape[1]
    head_width = query_rows.shape[1] // 2
    quarter = head_width // 2
    sections = lax.axis_size("section")
    section_pos = lax.axis_index("section")
    group_pos = lax.axis_index("groups")
    peers = lax.axis_size("dp")
    dp_pos = lax.axis_index("dp")
    core_pos = lax.axis_index("mp")
    block_rows = half_width // peers
    side = lax.rem(dp_pos, 2)
    even = side == 0
    is_last = section_pos == sections - 1
    in_tiles = out_block.shape[1] % 128 == 0 and peers <= 8

    def place(active):
        flags = [dp_pos, core_pos, group_pos, active, side]
        return jnp.stack([jnp.asarray(flag, jnp.int32) for flag in flags])

    def core_exchange(mine, take):
        return moved(
            mine, ("section", "mp"), lambda s, c: (s, 1 - c) if take(s == sections - 1) else None
        )

    def values_of(take):
        value_part = jnp.dot(inputs, value_rows, preferred_element_type=F32)
        part_mine = part_of(value_part, core_pos, kv_width, 1)
        part_other = part_of(value_part, 1 - core_pos, kv_width, 1)
        return part_mine + core_exchange(part_other.astype(BF16), take).astype(F32)

    where_last = jnp.stack([core_pos, lengths[0]])

    def last_section():
        values_f = values_of(lambda last: last)
        rest = attend(lengths, query_rows, key_rows, values_f)
        sens_branch = sensitivity(lengths, inputs, branch)
        own, backs = spread_product(sens_branch, out_block)
        leaves, tree = jax.tree.flatten(early_shapes[-1])
        filler = lengths[0].astype(BF16)
        unused = [jnp.full(leaf.shape, filler + k, BF16) for k, leaf in enumerate(leaves)]
        own, *unused = lax.optimization_barrier((own, *unused))
        if peers > 8:
            for back in backs:
                own = own + back.astype(F32)
            backs = []
        found = sum_heads(own, backs, *rest)
        other = core_exchange(found, lambda last: last)
        outgoing = last_outgoing(where_last, inputs, branch, found, other, value_rows)
        return values_f, found, outgoing, jax.tree.unflatten(tree, unused)

    def early_section():
        own_quarters = []
        for k in range(1, peers):
            rows = part_of(out_block, 2 * lax.rem(dp_pos + k, 2) + group_pos, quarter, 0)
            own_quarters.append(
                early_move(rows, ("dp", "section"), lambda i, s: ((i + k) % peers, s))
            )
        other_quarters = [
            early_move(rows, ("groups", "section"), lambda g, s: (1 - g, s))
            for rows in own_quarters
        ]
        values_f = values_of(lambda last: not last)

        def half_of(which):
            parts = [
                part_of(query_rows, which, head_width, 1),
                part_of(key_rows, which, HD, 1),
                part_of(values_f, which, HD, 1).astype(BF16),
            ]
            packed = jnp.concatenate(parts, 1)
            mark = jnp.full((8, packed.shape[1]), lengths[0].astype(BF16))
            return jnp.concatenate([packed, mark], 0)

        found = jnp.full((seq_len, kv_width), lengths[0].astype(BF16))
        outgoing = jnp.full((seq_len, half_width), lengths[0].astype(BF16))
        kept_half, sent_half, found, outgoing, *_ = lax.optimization_barrier(
            (half_of(side), half_of(1 - side), found, outgoing, *own_quarters)
            + (other_quarters[0], other_quarters[-1])
        )
        halves = (kept_half, early_pair(sent_half))
        return values_f, found, outgoing, (own_quarters, other_quarters, halves)

    early_shapes = jax.eval_shape(early_section)
    values_f, found, outgoing, prepared = lax.cond(is_last, last_section, early_section)
    own_quarters, other_quarters, (kept_half, got_half) = prepared
    arrived = from_next_section(outgoing)

    rows = once(inputs, outgoing)
    pieces = [
        along_dp(part_of(rows, lax.rem(dp_pos + k, peers), block_rows, 1), k) for k in range(peers)
    ]
    sens_mine = sensitivity(lengths, inputs, branch, arrived)
    sens_partner = early_pair(sens_mine)

    kept_half, got_half, found, arrived, *pieces = lax.optimization_barrier(
        (kept_half, got_half, found, arrived, *pieces, sens_mine)
    )[:-1]
    rest = pair_attend(place(~is_last), kept_half, got_half)
    if in_tiles:
        inputs_t = turned_side_by_side(place(0), pieces)
    else:
        inputs_t = jnp.concatenate(pieces, 0).T

    totals = inputs.astype(F32) + branch.astype(F32)
    valid_rows = (lax.iota(jnp.int32, seq_len) < lengths[0]).astype(F32)
    current = (totals * valid_rows[:, None]).astype(BF16)

    def kept_of(entering):
        return inputs.astype(F32) * (entering.astype(F32) / stabilize(totals))

    got = moved(found, ("dp", "section"), lambda i, s: (i ^ 1, s) if s == sections - 1 else None)
    last_kept = jnp.sum(kept_of(current), axis=1)[None]
    sens_values = pack_last(place(is_last), found, got, values_f, last_kept)

    for turn in range(1, sections):
        active = section_pos == sections - 1 - turn
        current = jnp.where(active, arrived, current)
        kept_sum = jnp.sum(kept_of(arrived), axis=1)[None]
        if turn > 1:
            sens_mine = sensitivity(lengths, inputs, branch, arrived)
            sens_partner = early_pair(sens_mine)
        else:
            sens_partner, *ready = lax.optimization_barrier(
                (sens_partner, sens_values, kept_sum, inputs_t, *rest)
            )
            sens_values, kept_sum, inputs_t, *rest = ready
        sens = [sens_mine, sens_partner, early_core(sens_mine), early_core(sens_partner)]
        step = main_step if in_tiles else main_plain
        sens_values = step(
            place(active),
            sens,
            out_block,
            (own_quarters, other_quarters),
            sens_values,
            kept_sum,
            rest,
        )
        if turn + 1 < sections:
            mine_now, theirs_now = (part_of(sens_values, w, seq_len, 0) for w in (side, 1 - side))
            found_now = ordered(even, mine_now, early_pair(theirs_now), 1)
            sens_all = ordered(core_pos == 0, found_now, early_core(found_now), 1)
            back_inputs = by_columns(sens_all, value_rows)
            outgoing = kept_of(current) + inputs.astype(F32) * back_inputs
            arrived = from_next_section(outgoing.astype(BF16))

    own_sens = [along_dp(sens_values, k) for k in range(peers)]
    other_sens = other_core(jnp.concatenate(own_sens, 0))
    step = relevance_step if in_tiles else relevance_plain
    relevance_rows, heat_rows = step(place(0), inputs_t, value_rows, own_sens, other_sens)
    return (heat_rows[None], relevance_rows[None])


def solution(mesh):
    placed = (
        P("section", ("groups", "dp"), None, "mp"),
        P("section", ("groups", "dp"), None, "mp"),
        P("section", ("groups", "dp"), None, "mp"),
        P("section", ("groups", "dp"), None, "mp"),
        P("section", "mp", None),
        P("section", "mp", "dp"),
        P(("groups", "dp")),
    )
    return jax.shard_map(
        on_device,
        mesh=mesh,
        in_specs=placed,
        out_specs=(
            P("section", ("groups", "dp"), None),
            P(("groups", "section"), ("mp", "dp"), None),
        ),
        check_vma=False,
    )
```

```python
import functools
import itertools
import math

import jax
import jax.numpy as jnp
from jax import lax
from jax.experimental import pallas as pl
from jax.experimental.pallas import tpu as pltpu
from jax.sharding import PartitionSpec as P

DW = 2560
HD = 128
QH = 20
KVH = 4
EPS = 0.25
F32 = jnp.float32
BF16 = jnp.bfloat16


def stabilize(entries):
    return jnp.where(entries >= 0, entries + EPS, entries - EPS)


VMEM = pl.BlockSpec(memory_space=pltpu.VMEM)
SMEM = pl.BlockSpec(memory_space=pltpu.SMEM)


def by_columns(left, right):
    return lax.dot_general(left, right, (((1,), (1,)), ((), ())), preferred_element_type=F32)


def kernel_call(body, shapes, in_specs, scratch=(), flops=0, nbytes=0, limit=24):
    return pl.pallas_call(
        body,
        out_shape=shapes,
        in_specs=in_specs,
        out_specs=jax.tree.map(lambda _: VMEM, shapes),
        scratch_shapes=scratch,
        compiler_params=pltpu.CompilerParams(vmem_limit_bytes=limit * 2**20),
        cost_estimate=pl.CostEstimate(flops=flops, bytes_accessed=nbytes, transcendentals=0),
    )


def attention_kernel(length, queries, keys, values, probs_t, mixed_gain, value_gain):
    seq_len = queries.shape[0]
    kv_heads = keys.shape[1] // HD
    group_size = queries.shape[1] // HD // kv_heads
    row = lax.broadcasted_iota(jnp.int32, (seq_len, seq_len), 0)
    column = lax.broadcasted_iota(jnp.int32, (seq_len, seq_len), 1)
    allowed = (column <= row) & (column < length[0])
    values_bf = values[...].astype(BF16)
    values_r = values_bf.astype(F32)
    value_gain[...] = values_r / stabilize(values_r)
    for g in range(kv_heads):
        key_head = keys[:, g * HD : (g + 1) * HD]
        value_head = values_bf[:, g * HD : (g + 1) * HD]
        for h in range(g * group_size, (g + 1) * group_size):
            scores = by_columns(queries[:, h * HD : (h + 1) * HD], key_head) / math.sqrt(HD)
            scores = jnp.where(allowed, scores, -1000000000.0)
            weights = jnp.exp(scores - jnp.max(scores, axis=1, keepdims=True))
            probs = weights / jnp.sum(weights, axis=1, keepdims=True)
            probs_t[h] = probs.T.astype(BF16)
            mixed = jnp.dot(probs.astype(BF16), value_head, preferred_element_type=F32)
            mixed_gain[:, h * HD : (h + 1) * HD] = mixed / stabilize(mixed)


def attend(length, queries, keys, values):
    seq_len, width = queries.shape
    shapes = (
        jax.ShapeDtypeStruct((width // HD, seq_len, seq_len), BF16),
        jax.ShapeDtypeStruct((seq_len, width), F32),
        jax.ShapeDtypeStruct(values.shape, F32),
    )
    call = kernel_call(
        attention_kernel, shapes, [SMEM, VMEM, VMEM, VMEM], flops=10**5, nbytes=10**4
    )
    return call(length, queries, keys, values)


def head_step(back_mixed, probs_t, mixed_gain, value_gain, found):
    heads = probs_t.shape[0]
    kv_heads = value_gain.shape[1] // HD
    group_size = heads // kv_heads
    for g in range(kv_heads):
        total = jnp.zeros((probs_t.shape[1], HD), F32)
        for h in range(g * group_size, (g + 1) * group_size):
            at = slice(h * HD, (h + 1) * HD)
            sens_mixed = (mixed_gain[:, at] * back_mixed[:, at]).astype(BF16)
            total += jnp.dot(probs_t[h], sens_mixed, preferred_element_type=F32)
        at = slice(g * HD, (g + 1) * HD)
        found[:, at] = (value_gain[:, at] * total).astype(BF16)


def sum_heads_kernel(count, product, *refs):
    backs, (probs_t, mixed_gain, value_gain, found, total) = refs[:count], refs[count:]
    back_mixed = product[...]
    for back in backs:
        back_mixed += back[...].astype(F32)
    total[...] = back_mixed
    head_step(total, probs_t, mixed_gain, value_gain, found)


def sum_heads(product, backs, probs_t, mixed_gain, value_gain):
    call = kernel_call(
        functools.partial(sum_heads_kernel, len(backs)),
        jax.ShapeDtypeStruct(value_gain.shape, BF16),
        [VMEM] * (4 + len(backs)),
        [pltpu.VMEM(product.shape, F32)],
        flops=5 * 10**7,
        nbytes=3 * 10**6,
    )
    return call(product, *backs, probs_t, mixed_gain, value_gain)


def product_kernel(use_mine, mine, theirs, block, own, *backs):
    seq_len = own.shape[0]

    def multiply(operand):
        product = by_columns(operand[...], block[...])
        own[...] = product[:seq_len]
        for k, back in enumerate(backs):
            back[...] = product[(k + 1) * seq_len : (k + 2) * seq_len].astype(BF16)

    @pl.when(use_mine[0] == 1)
    def _():
        multiply(mine)

    @pl.when(use_mine[0] == 0)
    def _():
        multiply(theirs)


def spread_products(use_mine, mine, theirs, block, seq_len):
    count = mine.shape[0] // seq_len
    width = block.shape[0]
    shapes = (jax.ShapeDtypeStruct((seq_len, width), F32),) + tuple(
        jax.ShapeDtypeStruct((seq_len, width), BF16) for _ in range(count - 1)
    )
    call = kernel_call(
        product_kernel, shapes, [SMEM, VMEM, VMEM, VMEM], flops=10**9, nbytes=5 * 10**6, limit=32
    )
    return call(use_mine, mine, theirs, block)


def sensitivity_kernel(length, inputs, branch, *refs):
    current, sens = refs if len(refs) == 2 else (None, refs[0])
    inputs_f = inputs[...].astype(F32)
    branch_f = branch[...].astype(F32)
    totals = inputs_f + branch_f
    if current is None:
        row = lax.broadcasted_iota(jnp.int32, totals.shape, 0)
        entering = jnp.where(row < length[0], totals, 0.0).astype(BF16).astype(F32)
    else:
        entering = current[...].astype(F32)
    sens[...] = (branch_f * (entering / stabilize(totals)) / stabilize(branch_f)).astype(BF16)


def sensitivity(length, inputs, branch, *current):
    call = kernel_call(
        sensitivity_kernel,
        jax.ShapeDtypeStruct(inputs.shape, BF16),
        [SMEM] + [VMEM] * (2 + len(current)),
        flops=10**7,
        nbytes=10**6,
    )
    return call(length, inputs, branch, *current)


def gain_kernel(inputs, branch, gain):
    branch_f = branch[...].astype(F32)
    totals = inputs[...].astype(F32) + branch_f
    gain[...] = (branch_f / stabilize(totals) / stabilize(branch_f)).astype(BF16)


def branch_gain(inputs, branch):
    shape = jax.ShapeDtypeStruct(inputs.shape, BF16)
    return kernel_call(gain_kernel, shape, [VMEM, VMEM], flops=10**7, nbytes=10**6)(inputs, branch)


def pair_sensitivity_kernel(inputs, branch, gain, current, partner, sens, kept_sum):
    seq_len = inputs.shape[0]
    inputs_f = inputs[...].astype(F32)
    branch_f = branch[...].astype(F32)
    sens_total = current[...].astype(F32) / stabilize(inputs_f + branch_f)
    sens[:seq_len] = (branch_f * sens_total / stabilize(branch_f)).astype(BF16)
    sens[seq_len:] = (partner[...].astype(F32) * gain[...].astype(F32)).astype(BF16)
    kept_sum[...] = by_token(inputs_f * sens_total)


def pair_sensitivity(inputs, branch, gain, current, partner):
    seq_len, width = inputs.shape
    shapes = (
        jax.ShapeDtypeStruct((2 * seq_len, width), BF16),
        jax.ShapeDtypeStruct((1, seq_len), F32),
    )
    call = kernel_call(
        pair_sensitivity_kernel, shapes, [VMEM] * 5, flops=10**7, nbytes=2 * 10**6
    )
    return call(inputs, branch, gain, current, partner)


def outgoing_kernel(place, inputs, branch, sens_own, sens_other, value_rows, outgoing):
    core, length = place[0], place[1]
    width = sens_own.shape[1]
    inputs_f = inputs[...].astype(F32)
    totals = inputs_f + branch[...].astype(F32)
    row = lax.broadcasted_iota(jnp.int32, totals.shape, 0)
    entering = jnp.where(row < length, totals, 0.0).astype(BF16).astype(F32)
    own = value_rows[:, pl.ds(pl.multiple_of(core * width, 128), width)]
    other = value_rows[:, pl.ds(pl.multiple_of((1 - core) * width, 128), width)]
    back_inputs = by_columns(sens_own[...], own) + by_columns(sens_other[...], other)
    kept = inputs_f * (entering / stabilize(totals))
    outgoing[...] = (kept + inputs_f * back_inputs).astype(BF16)


def last_outgoing(place, inputs, branch, sens_own, sens_other, value_rows):
    call = kernel_call(
        outgoing_kernel,
        jax.ShapeDtypeStruct(inputs.shape, BF16),
        [SMEM] + [VMEM] * 5,
        flops=2 * 10**8,
        nbytes=2 * 10**6,
    )
    return call(place, inputs, branch, sens_own, sens_other, value_rows)


def pair_attention_kernel(place, kept, got, probs_out, gain_t, value_gain, values):
    seq_len = kept.shape[0] - 8
    width = kept.shape[1] - 2 * HD
    heads = width // HD
    row = lax.broadcasted_iota(jnp.int32, (seq_len, seq_len), 0)
    column = lax.broadcasted_iota(jnp.int32, (seq_len, seq_len), 1)

    @pl.when(place[3] == 1)
    def _():
        for half, b in ((kept, place[4]), (got, 1 - place[4])):
            tokens = pl.ds(pl.multiple_of(b * seq_len, 128), seq_len)
            length = jnp.max(half[seq_len:, :HD].astype(F32), axis=0, keepdims=True)
            allowed = (column <= row) & (column.astype(F32) < length)
            value_head = half[:seq_len, width + HD : width + 2 * HD]
            value_f = value_head.astype(F32)
            values[tokens] = value_f
            value_gain[tokens] = value_f / stabilize(value_f)
            stacked = [half[:seq_len, h * HD : (h + 1) * HD] for h in range(heads)]
            scores = by_columns(
                jnp.concatenate(stacked, 0), half[:seq_len, width : width + HD]
            ) / math.sqrt(HD)
            scores = jnp.where(jnp.concatenate([allowed] * heads, 0), scores, -1000000000.0)
            weights = jnp.exp(scores - jnp.max(scores, axis=1, keepdims=True))
            probs = (weights / jnp.sum(weights, axis=1, keepdims=True)).astype(BF16)
            mixed = jnp.dot(probs, value_head, preferred_element_type=F32)
            gain = mixed / stabilize(mixed)
            for h in range(heads):
                at = slice(h * seq_len, (h + 1) * seq_len)
                probs_out[b, h] = probs[at]
                gain_t[h * HD : (h + 1) * HD, tokens] = gain[at].T


def pair_attend(place, kept, got):
    seq_len, width = kept.shape[0] - 8, kept.shape[1] - 2 * HD
    shapes = (
        jax.ShapeDtypeStruct((2, width // HD, seq_len, seq_len), BF16),
        jax.ShapeDtypeStruct((width, 2 * seq_len), F32),
        jax.ShapeDtypeStruct((2 * seq_len, HD), F32),
        jax.ShapeDtypeStruct((2 * seq_len, HD), F32),
    )
    return kernel_call(
        pair_attention_kernel, shapes, [SMEM, VMEM, VMEM], flops=10**8, nbytes=3 * 10**6
    )(place, kept, got)


def main_kernel(count, place, *refs):
    sens, out_block, (before, kept_sum, probs, gain_t, value_gain, values) = refs[:2], refs[2], refs[3:9]
    own_pieces, other_pieces = refs[9 : 9 + count], refs[9 + count : 9 + 2 * count]
    found, halves, total = refs[9 + 2 * count :]
    pos, core, group, active, side = [place[i] for i in range(5)]
    seq_len, half_width = sens[0].shape[0] // 2, sens[0].shape[1]
    width = out_block.shape[1]
    per_core = half_width // width
    quarter = own_pieces[0].shape[0]

    @pl.when(active == 0)
    def _():
        found[...] = before[...]

    @pl.when(active == 1)
    def _():
        for j, half in ((0, core), (1, 1 - core)):
            for i, sequence in ((0, side), (1, 1 - side)):
                rows = pl.ds(pl.multiple_of(sequence * seq_len, 128), seq_len)
                halves[half, rows, :] = sens[j][i * seq_len : (i + 1) * seq_len]

        def part(k):
            owner = lax.rem(pos - k + count + 1, count + 1)
            start = pl.multiple_of(lax.rem(owner, per_core) * width, 128)
            return halves[owner // per_core, :, pl.ds(start, width)]

        rows = pl.ds(pl.multiple_of(side * 2 * quarter, 16), 2 * quarter)
        total[...] = by_columns(out_block[rows, :], part(0))
        for k in range(count):
            operand = part(k + 1)
            for at, piece in ((group, own_pieces[k]), (1 - group, other_pieces[k])):
                rows = pl.ds(pl.multiple_of(at * quarter, 8), quarter)
                total[rows, :] += by_columns(piece[...], operand)
        heats = []
        for b in range(2):
            tokens = slice(b * seq_len, (b + 1) * seq_len)
            back_values = jnp.zeros((HD, seq_len), F32)
            for h in range(probs.shape[1]):
                at = slice(h * HD, (h + 1) * HD)
                sens_mixed = (gain_t[at, tokens] * total[at, tokens]).astype(BF16)
                back_values += jnp.dot(sens_mixed, probs[b, h], preferred_element_type=F32)
            sens_values = (value_gain[tokens] * back_values.T).astype(BF16)
            found[tokens] = sens_values
            heats.append(by_token(sens_values.astype(F32) * values[tokens]))
        mine = jnp.where(side == 0, heats[0], heats[1]) + kept_sum[...]
        found[2 * seq_len :] = heat_rows_of(mine, jnp.where(side == 0, heats[1], heats[0]))


def by_token(array):
    groups = [array[:, at : at + 128] for at in range(0, array.shape[1], 128)]
    return jnp.sum(sum(groups).T, axis=0, keepdims=True)


def heat_rows_of(mine, theirs):
    rows = []
    for heat in (mine, theirs):
        high = heat.astype(BF16).astype(F32)
        rows += [high, heat - high]
    rows.append(jnp.zeros((12, mine.shape[1]), F32))
    return jnp.concatenate(rows, 0).astype(BF16)


def pack_kernel(place, found, got, values, kept_sum, packed):
    side = place[4]
    seq_len = found.shape[0]

    @pl.when(place[3] == 1)
    def _():
        mine, theirs = (
            jnp.where(side == 0, array[:, :HD], array[:, HD:]) for array in (found, got)
        )
        packed[:seq_len] = jnp.where(side == 0, mine, theirs)
        packed[seq_len : 2 * seq_len] = jnp.where(side == 0, theirs, mine)
        heat = by_token(found[...].astype(F32) * values[...]) + kept_sum[...]
        packed[2 * seq_len :] = heat_rows_of(heat, jnp.zeros_like(heat))


def pack_last(place, found, got, values, kept_sum):
    seq_len = found.shape[0]
    shape = jax.ShapeDtypeStruct((2 * seq_len + 16, HD), BF16)
    return kernel_call(pack_kernel, shape, [SMEM] + [VMEM] * 4, nbytes=10**6)(
        place, found, got, values, kept_sum
    )


def main_step(place, sens, out_block, quarters, before, kept_sum, rest):
    count = len(quarters[0])
    seq_len, half_width = sens[0].shape[0] // 2, sens[0].shape[1]
    operands = [*sens, out_block, before, kept_sum, *rest, *quarters[0], *quarters[1]]
    call = kernel_call(
        functools.partial(main_kernel, count),
        jax.ShapeDtypeStruct(before.shape, BF16),
        [SMEM] + [VMEM] * len(operands),
        [pltpu.VMEM((2, 2 * seq_len, half_width), BF16), pltpu.VMEM(rest[1].shape, F32)],
        flops=10**9,
        nbytes=6 * 10**6,
        limit=32,
    )
    return call(place, *operands)


def main_plain(place, sens, out_block, quarters, before, kept_sum, rest):
    pos, core, group, active, side = [place[i] for i in range(5)]
    seq_len = sens[0].shape[0] // 2
    width = out_block.shape[1]
    mine, theirs = (ordered(side == 0, half[:seq_len], half[seq_len:], 0) for half in sens)
    sens_full = ordered(core == 0, mine, theirs, 1)
    count = len(quarters[0])
    quarter = quarters[0][0].shape[0]
    totals = [0.0, 0.0]
    for k in range(count + 1):
        operand = part_of(sens_full, lax.rem(pos - k + count + 1, count + 1), width, 1)
        for half in range(2):
            if k:
                piece = quarters[half][k - 1]
            else:
                at = 2 * side + (group if half == 0 else 1 - group)
                piece = part_of(out_block, at, quarter, 0)
            totals[half] += by_columns(piece, operand)
    total = ordered(group == 0, totals[0], totals[1], 0)
    probs, gain_t, value_gain, values = rest
    sens_mixed = (gain_t * total).astype(BF16).reshape(-1, HD, 2, seq_len)
    back_values = jnp.einsum("hdbt,bhts->bsd", sens_mixed, probs, preferred_element_type=F32)
    found = (value_gain * back_values.reshape(2 * seq_len, HD)).astype(BF16)
    heats = jnp.sum((found.astype(F32) * values).reshape(2, 1, seq_len, HD), axis=3)
    mine = jnp.where(side == 0, heats[0], heats[1]) + kept_sum
    rows = heat_rows_of(mine, jnp.where(side == 0, heats[1], heats[0]))
    return jnp.where(active == 1, jnp.concatenate([found, rows], 0), before)


def turn_kernel(place, *refs):
    *pieces, turned = refs
    count = len(pieces)
    for k, piece in enumerate(pieces):
        rows = piece.shape[0]
        at = pl.multiple_of(lax.rem(place[0] - k + count, count) * rows, 128)
        turned[:, pl.ds(at, rows)] = piece[...].astype(F32).T.astype(BF16)


def turned_side_by_side(place, pieces):
    rows, width = pieces[0].shape
    shape = jax.ShapeDtypeStruct((width, rows * len(pieces)), BF16)
    specs = [SMEM] + [VMEM] * len(pieces)
    return kernel_call(turn_kernel, shape, specs, nbytes=10**6)(place, *pieces)


def heat_of(own, other, place, count):
    partner = lax.rem(2 * place[4] - 1 + count, count)
    size = own[0].shape[0]
    heat = 0.0
    for source in (own, [other[k * size : (k + 1) * size] for k in range(count)]):
        rows = [source[k][size - 16 :].astype(F32) for k in range(count)]
        heat += rows[0][0:1] + rows[0][1:2]
        for k in {1 % count, count - 1}:
            heat += jnp.where(partner == k, rows[k][2:3] + rows[k][3:4], 0.0)
    return heat / DW


def relevance_kernel(count, place, inputs_t, value_rows, *refs):
    own, (other, relevance, heat, sens) = refs[:count], refs[count:]
    pos, core = place[0], place[1]
    size = own[0].shape[0]
    rows = size - 16
    for k in range(count):
        source = lax.rem(pos - k + count, count)
        tokens = pl.ds(pl.multiple_of(source // 2 * rows, 128), rows)
        for c, piece in ((core, own[k][:rows]), (1 - core, other[k * size : k * size + rows])):
            head = 2 * c + lax.rem(source, 2)
            sens[tokens, pl.ds(pl.multiple_of(head * HD, 128), HD)] = piece
    rows = relevance.shape[0]
    value_block = value_rows[pl.ds(pl.multiple_of(pos * rows, 16), rows), :]
    summed = jnp.dot(inputs_t[...], sens[...], preferred_element_type=F32)
    relevance[...] = value_block.astype(F32) * summed
    heat[...] = heat_of(own, other, place, count)


def relevance_step(place, inputs_t, value_rows, own, other):
    shapes = (
        jax.ShapeDtypeStruct((inputs_t.shape[0], value_rows.shape[1]), F32),
        jax.ShapeDtypeStruct((1, (own[0].shape[0] - 16) // 2), F32),
    )
    call = kernel_call(
        functools.partial(relevance_kernel, len(own)),
        shapes,
        [SMEM] + [VMEM] * (3 + len(own)),
        [pltpu.VMEM((inputs_t.shape[1], value_rows.shape[1]), BF16)],
        flops=2 * 10**8,
        nbytes=2 * 10**6,
    )
    return call(place, inputs_t, value_rows, *own, other)


def relevance_plain(place, inputs_t, value_rows, own, other):
    pos, core = place[0], place[1]
    count, size = len(own), own[0].shape[0]
    rows = size - 16
    seq_len = rows // 2
    heat = heat_of(own, other, place, count)
    other = [other[k * size : k * size + rows] for k in range(count)]
    own = [piece[:rows] for piece in own]
    even = lax.rem(pos, 2) == 0
    by_core = []
    for sens in (own, other):
        same = jnp.concatenate([sens[k] for k in range(0, count, 2)], 0)
        cross = jnp.concatenate(
            [jnp.where(even, sens[(k - 1) % count], sens[k + 1]) for k in range(0, count, 2)], 0
        )
        by_core.append(ordered(even, same, cross, 1))
    inputs = inputs_t.reshape(-1, count, seq_len)
    tokens = []
    for k in range(0, count, 2):
        tokens.append(jnp.where(even, inputs[:, k], inputs[:, k + 1]))
        tokens.append(jnp.where(even, inputs[:, (k - 1) % count], inputs[:, k]))
    all_sens = ordered(core == 0, by_core[0], by_core[1], 1)
    summed = jnp.dot(jnp.concatenate(tokens, 1), all_sens, preferred_element_type=F32)
    return part_of(value_rows, pos, inputs_t.shape[0], 0).astype(F32) * summed, heat


def moved(shard, axes, target):
    sizes = [lax.axis_size(axis) for axis in axes]
    places = list(itertools.product(*[range(size) for size in sizes]))
    index = {place: i for i, place in enumerate(places)}
    pairs = [(index[place], index[target(*place)]) for place in places if target(*place) is not None]
    return lax.ppermute(shard, axes, pairs)


def along_dp(shard, by):
    peers = lax.axis_size("dp")
    return moved(shard, ("dp",), lambda i: ((i + by) % peers,)) if by else shard


def other_core(shard):
    return moved(shard, ("mp",), lambda c: (1 - c,))


def from_next_section(shard, flip_pair=0):
    return moved(
        shard, ("dp", "section"), lambda i, s: (i ^ flip_pair, s - 1) if s > 0 else None
    )


def ordered(first_is_mine, mine, theirs, axis):
    return jnp.concatenate(
        [jnp.where(first_is_mine, mine, theirs), jnp.where(first_is_mine, theirs, mine)], axis
    )


def part_of(array, index, width, axis):
    return lax.dynamic_slice_in_dim(array, index * width, width, axis)


def once(array, *others):
    return lax.optimization_barrier((array,) + others)[0]


def early_move(shard, axes, target):
    last = lax.axis_size("section") - 1
    at = axes.index("section")
    return moved(shard, axes, lambda *place: target(*place) if place[at] < last else None)


def early_pair(shard):
    return early_move(shard, ("dp", "section"), lambda i, s: (i ^ 1, s))


def early_core(shard):
    return early_move(shard, ("section", "mp"), lambda s, c: (s, 1 - c))


def spread_product(sens_branch, out_block):
    axes = ("dp", "section", "mp")
    peers, cores = lax.axis_size("dp"), lax.axis_size("mp")
    last = lax.axis_size("section") - 1
    pos, core = lax.axis_index("dp"), lax.axis_index("mp")
    seq_len = sens_branch.shape[0]
    width = out_block.shape[1]
    per_core = peers // cores
    arrived = []
    for k in range(peers):
        to = lax.rem(pos + k, peers)
        part = part_of(sens_branch, lax.rem(to, per_core), width, 1)
        if k:
            part = moved(
                part,
                axes,
                lambda i, s, c: ((i + k) % peers, s, c)
                if s == last and c == (i + k) % peers // per_core
                else None,
            )
        arrived.append(part)
    mine = jnp.concatenate(arrived, 0)
    theirs = moved(
        mine,
        axes,
        lambda i, s, c: (i, s, 1 - c) if s == last and c == i // per_core else None,
    )
    if width % 128 == 0:
        use_mine = (core == pos // per_core).astype(jnp.int32)[None]
        own, *sent = spread_products(use_mine, mine, theirs, out_block, seq_len)
    else:
        product = by_columns(jnp.where(core == pos // per_core, mine, theirs), out_block)
        own, *sent = jnp.split(product, peers, axis=0)
    backs = [
        moved(
            sent[k - 1].astype(BF16),
            axes,
            lambda i, s, c: ((i - k) % peers, s, c) if s == last else None,
        )
        for k in range(1, peers)
    ]
    return own, backs


def on_device(hidden_in, attn_out, queries, keys, value_weight, out_weight, lengths):
    inputs = hidden_in[0, 0]
    branch = attn_out[0, 0]
    query_rows = queries[0, 0]
    key_rows = keys[0, 0]
    value_rows = value_weight[0]
    out_block = out_weight[0]
    seq_len, half_width = inputs.shape
    kv_width = key_rows.shape[1]
    head_width = query_rows.shape[1] // 2
    quarter = head_width // 2
    sections = lax.axis_size("section")
    section_pos = lax.axis_index("section")
    group_pos = lax.axis_index("groups")
    peers = lax.axis_size("dp")
    dp_pos = lax.axis_index("dp")
    core_pos = lax.axis_index("mp")
    block_rows = half_width // peers
    side = lax.rem(dp_pos, 2)
    even = side == 0
    is_last = section_pos == sections - 1
    in_tiles = out_block.shape[1] % 128 == 0 and peers <= 8

    def place(active):
        flags = [dp_pos, core_pos, group_pos, active, side]
        return jnp.stack([jnp.asarray(flag, jnp.int32) for flag in flags])

    def core_exchange(mine, take):
        return moved(
            mine, ("section", "mp"), lambda s, c: (s, 1 - c) if take(s == sections - 1) else None
        )

    def values_of(take, rows):
        value_part = jnp.dot(rows, value_rows, preferred_element_type=F32)
        part_mine = part_of(value_part, core_pos, kv_width, 1)
        part_other = part_of(value_part, 1 - core_pos, kv_width, 1)
        return part_mine + core_exchange(part_other.astype(BF16), take).astype(F32)

    def last_section():
        sens_branch = sensitivity(lengths, inputs, branch)
        own, backs = spread_product(sens_branch, out_block)
        values_f = values_of(lambda last: last, once(inputs, own))
        rest = attend(lengths, query_rows, key_rows, values_f)
        leaves, tree = jax.tree.flatten(early_shapes[-1])
        filler = lengths[0].astype(BF16)
        unused = [jnp.full(leaf.shape, filler + k, BF16) for k, leaf in enumerate(leaves)]
        where_last = jnp.stack([core_pos, lengths[0]])
        own, where_last, *unused = lax.optimization_barrier((own, where_last, *unused))
        if peers > 8:
            for back in backs:
                own = own + back.astype(F32)
            backs = []
        found = sum_heads(own, backs, *rest)
        other = core_exchange(found, lambda last: last)
        outgoing = last_outgoing(where_last, inputs, branch, found, other, value_rows)
        return values_f, found, outgoing, jax.tree.unflatten(tree, unused)

    def early_section():
        own_quarters = []
        for k in range(1, peers):
            rows = part_of(out_block, 2 * lax.rem(dp_pos + k, 2) + group_pos, quarter, 0)
            own_quarters.append(
                early_move(rows, ("dp", "section"), lambda i, s: ((i + k) % peers, s))
            )
        other_quarters = [
            early_move(rows, ("groups", "section"), lambda g, s: (1 - g, s))
            for rows in own_quarters
        ]
        values_f = values_of(lambda last: not last, inputs)

        def half_of(which):
            parts = [
                part_of(query_rows, which, head_width, 1),
                part_of(key_rows, which, HD, 1),
                part_of(values_f, which, HD, 1).astype(BF16),
            ]
            packed = jnp.concatenate(parts, 1)
            mark = jnp.full((8, packed.shape[1]), lengths[0].astype(BF16))
            return jnp.concatenate([packed, mark], 0)

        found = jnp.full((seq_len, kv_width), lengths[0].astype(BF16))
        outgoing = jnp.full((seq_len, half_width), lengths[0].astype(BF16))
        partner_gain = early_pair(branch_gain(inputs, branch))
        sent_half = half_of(1 - side)
        sent_half = once(sent_half, *own_quarters, other_quarters[0], other_quarters[-1])
        got_half = early_pair(sent_half)
        kept_half, found, outgoing = half_of(side), *lax.optimization_barrier((found, outgoing, values_f))[:2]
        return values_f, found, outgoing, (
            own_quarters,
            other_quarters,
            (kept_half, got_half, partner_gain),
        )

    early_shapes = jax.eval_shape(early_section)
    values_f, found, outgoing, prepared = lax.cond(is_last, last_section, early_section)
    own_quarters, other_quarters, (kept_half, got_half, partner_gain) = prepared
    arrived = from_next_section(outgoing)
    partner_arrived = from_next_section(outgoing, 1)

    rows = once(inputs, outgoing)
    pieces = [
        along_dp(part_of(rows, lax.rem(dp_pos + k, peers), block_rows, 1), k) for k in range(peers)
    ]
    rest = pair_attend(place(~is_last), kept_half, got_half)
    if in_tiles:
        inputs_t = turned_side_by_side(place(0), pieces)
    else:
        inputs_t = jnp.concatenate(pieces, 0).T

    totals = inputs.astype(F32) + branch.astype(F32)
    valid_rows = (lax.iota(jnp.int32, seq_len) < lengths[0]).astype(F32)
    current = (totals * valid_rows[:, None]).astype(BF16)

    def kept_of(entering):
        return inputs.astype(F32) * (entering.astype(F32) / stabilize(totals))

    got = moved(found, ("dp", "section"), lambda i, s: (i ^ 1, s) if s == sections - 1 else None)
    last_kept = jnp.sum(kept_of(current), axis=1)[None]
    sens_values = pack_last(place(is_last), found, got, values_f, last_kept)

    for turn in range(1, sections):
        active = section_pos == sections - 1 - turn
        current = jnp.where(active, arrived, current)
        if turn == 1:
            arrived, partner_arrived, sens_values, inputs_t, *rest = lax.optimization_barrier(
                (arrived, partner_arrived, sens_values, inputs_t, *rest)
            )
        sens_own, kept_sum = pair_sensitivity(
            inputs, branch, partner_gain, arrived, partner_arrived
        )
        sens = [sens_own, early_core(sens_own)]
        step = main_step if in_tiles else main_plain
        sens_values = step(
            place(active),
            sens,
            out_block,
            (own_quarters, other_quarters),
            sens_values,
            kept_sum,
            rest,
        )
        if turn + 1 < sections:
            mine_now, theirs_now = (part_of(sens_values, w, seq_len, 0) for w in (side, 1 - side))
            found_now = ordered(even, mine_now, early_pair(theirs_now), 1)
            sens_all = ordered(core_pos == 0, found_now, early_core(found_now), 1)
            back_inputs = by_columns(sens_all, value_rows)
            outgoing = kept_of(current) + inputs.astype(F32) * back_inputs
            arrived = from_next_section(outgoing.astype(BF16))
            partner_arrived = from_next_section(outgoing.astype(BF16), 1)

    own_sens = [along_dp(sens_values, k) for k in range(peers)]
    other_sens = other_core(jnp.concatenate(own_sens, 0))
    step = relevance_step if in_tiles else relevance_plain
    relevance_rows, heat_rows = step(place(0), inputs_t, value_rows, own_sens, other_sens)
    return (heat_rows[None], relevance_rows[None])


def solution(mesh):
    placed = (
        P("section", ("groups", "dp"), None, "mp"),
        P("section", ("groups", "dp"), None, "mp"),
        P("section", ("groups", "dp"), None, "mp"),
        P("section", ("groups", "dp"), None, "mp"),
        P("section", "mp", None),
        P("section", "mp", "dp"),
        P(("groups", "dp")),
    )
    return jax.shard_map(
        on_device,
        mesh=mesh,
        in_specs=placed,
        out_specs=(
            P("section", ("groups", "dp"), None),
            P(("groups", "section"), ("mp", "dp"), None),
        ),
        check_vma=False,
    )
```

```python
import functools
import itertools
import math

import jax
import jax.numpy as jnp
from jax import lax
from jax.experimental import pallas as pl
from jax.experimental.pallas import tpu as pltpu
from jax.sharding import PartitionSpec as P

DW = 2560
HD = 128
QH = 20
KVH = 4
EPS = 0.25
F32 = jnp.float32
BF16 = jnp.bfloat16


def stabilize(entries):
    return jnp.where(entries >= 0, entries + EPS, entries - EPS)


VMEM = pl.BlockSpec(memory_space=pltpu.VMEM)
SMEM = pl.BlockSpec(memory_space=pltpu.SMEM)


def by_columns(left, right):
    return lax.dot_general(left, right, (((1,), (1,)), ((), ())), preferred_element_type=F32)


def kernel_call(body, shapes, in_specs, scratch=(), flops=0, nbytes=0, limit=24):
    return pl.pallas_call(
        body,
        out_shape=shapes,
        in_specs=in_specs,
        out_specs=jax.tree.map(lambda _: VMEM, shapes),
        scratch_shapes=scratch,
        compiler_params=pltpu.CompilerParams(vmem_limit_bytes=limit * 2**20),
        cost_estimate=pl.CostEstimate(flops=flops, bytes_accessed=nbytes, transcendentals=0),
    )


def attention_kernel(length, queries, keys, values, probs_t, mixed_gain, value_gain):
    seq_len = queries.shape[0]
    kv_heads = keys.shape[1] // HD
    group_size = queries.shape[1] // HD // kv_heads
    row = lax.broadcasted_iota(jnp.int32, (seq_len, seq_len), 0)
    column = lax.broadcasted_iota(jnp.int32, (seq_len, seq_len), 1)
    allowed = (column <= row) & (column < length[0])
    values_bf = values[...].astype(BF16)
    values_r = values_bf.astype(F32)
    value_gain[...] = values_r / stabilize(values_r)
    for g in range(kv_heads):
        key_head = keys[:, g * HD : (g + 1) * HD]
        value_head = values_bf[:, g * HD : (g + 1) * HD]
        for h in range(g * group_size, (g + 1) * group_size):
            scores = by_columns(queries[:, h * HD : (h + 1) * HD], key_head) / math.sqrt(HD)
            scores = jnp.where(allowed, scores, -1000000000.0)
            weights = jnp.exp(scores - jnp.max(scores, axis=1, keepdims=True))
            probs = weights / jnp.sum(weights, axis=1, keepdims=True)
            probs_t[h] = probs.T.astype(BF16)
            mixed = jnp.dot(probs.astype(BF16), value_head, preferred_element_type=F32)
            mixed_gain[:, h * HD : (h + 1) * HD] = mixed / stabilize(mixed)


def attend(length, queries, keys, values):
    seq_len, width = queries.shape
    shapes = (
        jax.ShapeDtypeStruct((width // HD, seq_len, seq_len), BF16),
        jax.ShapeDtypeStruct((seq_len, width), F32),
        jax.ShapeDtypeStruct(values.shape, F32),
    )
    call = kernel_call(
        attention_kernel, shapes, [SMEM, VMEM, VMEM, VMEM], flops=10**5, nbytes=10**4
    )
    return call(length, queries, keys, values)


def head_step(back_mixed, probs_t, mixed_gain, value_gain, found):
    heads = probs_t.shape[0]
    kv_heads = value_gain.shape[1] // HD
    group_size = heads // kv_heads
    for g in range(kv_heads):
        total = jnp.zeros((probs_t.shape[1], HD), F32)
        for h in range(g * group_size, (g + 1) * group_size):
            at = slice(h * HD, (h + 1) * HD)
            sens_mixed = (mixed_gain[:, at] * back_mixed[:, at]).astype(BF16)
            total += jnp.dot(probs_t[h], sens_mixed, preferred_element_type=F32)
        at = slice(g * HD, (g + 1) * HD)
        found[:, at] = (value_gain[:, at] * total).astype(BF16)


def sum_heads_kernel(count, product, *refs):
    backs, (probs_t, mixed_gain, value_gain, found, total) = refs[:count], refs[count:]
    back_mixed = product[...]
    for back in backs:
        back_mixed += back[...].astype(F32)
    total[...] = back_mixed
    head_step(total, probs_t, mixed_gain, value_gain, found)


def sum_heads(product, backs, probs_t, mixed_gain, value_gain):
    call = kernel_call(
        functools.partial(sum_heads_kernel, len(backs)),
        jax.ShapeDtypeStruct(value_gain.shape, BF16),
        [VMEM] * (4 + len(backs)),
        [pltpu.VMEM(product.shape, F32)],
        flops=5 * 10**7,
        nbytes=3 * 10**6,
    )
    return call(product, *backs, probs_t, mixed_gain, value_gain)


def product_kernel(use_mine, mine, theirs, block, own, *backs):
    seq_len = own.shape[0]

    def multiply(operand):
        product = by_columns(operand[...], block[...])
        own[...] = product[:seq_len]
        for k, back in enumerate(backs):
            back[...] = product[(k + 1) * seq_len : (k + 2) * seq_len].astype(BF16)

    @pl.when(use_mine[0] == 1)
    def _():
        multiply(mine)

    @pl.when(use_mine[0] == 0)
    def _():
        multiply(theirs)


def spread_products(use_mine, mine, theirs, block, seq_len):
    count = mine.shape[0] // seq_len
    width = block.shape[0]
    shapes = (jax.ShapeDtypeStruct((seq_len, width), F32),) + tuple(
        jax.ShapeDtypeStruct((seq_len, width), BF16) for _ in range(count - 1)
    )
    call = kernel_call(
        product_kernel, shapes, [SMEM, VMEM, VMEM, VMEM], flops=10**9, nbytes=5 * 10**6, limit=32
    )
    return call(use_mine, mine, theirs, block)


def sensitivity_kernel(length, inputs, branch, *refs):
    current, sens = refs if len(refs) == 2 else (None, refs[0])
    inputs_f = inputs[...].astype(F32)
    branch_f = branch[...].astype(F32)
    totals = inputs_f + branch_f
    if current is None:
        row = lax.broadcasted_iota(jnp.int32, totals.shape, 0)
        entering = jnp.where(row < length[0], totals, 0.0).astype(BF16).astype(F32)
    else:
        entering = current[...].astype(F32)
    sens[...] = (branch_f * (entering / stabilize(totals)) / stabilize(branch_f)).astype(BF16)


def sensitivity(length, inputs, branch, *current):
    call = kernel_call(
        sensitivity_kernel,
        jax.ShapeDtypeStruct(inputs.shape, BF16),
        [SMEM] + [VMEM] * (2 + len(current)),
        flops=10**7,
        nbytes=10**6,
    )
    return call(length, inputs, branch, *current)


def gain_kernel(inputs, branch, gain):
    branch_f = branch[...].astype(F32)
    totals = inputs[...].astype(F32) + branch_f
    gain[...] = (branch_f / stabilize(totals) / stabilize(branch_f)).astype(BF16)


def branch_gain(inputs, branch):
    shape = jax.ShapeDtypeStruct(inputs.shape, BF16)
    return kernel_call(gain_kernel, shape, [VMEM, VMEM], flops=10**7, nbytes=10**6)(inputs, branch)


def pair_sensitivity_kernel(inputs, branch, gain, current, partner, sens, kept_sum):
    seq_len = inputs.shape[0]
    inputs_f = inputs[...].astype(F32)
    branch_f = branch[...].astype(F32)
    sens_total = current[...].astype(F32) / stabilize(inputs_f + branch_f)
    sens[:seq_len] = (branch_f * sens_total / stabilize(branch_f)).astype(BF16)
    sens[seq_len:] = (partner[...].astype(F32) * gain[...].astype(F32)).astype(BF16)
    kept_sum[...] = by_token(inputs_f * sens_total)


def pair_sensitivity(inputs, branch, gain, current, partner):
    seq_len, width = inputs.shape
    shapes = (
        jax.ShapeDtypeStruct((2 * seq_len, width), BF16),
        jax.ShapeDtypeStruct((1, seq_len), F32),
    )
    call = kernel_call(
        pair_sensitivity_kernel, shapes, [VMEM] * 5, flops=10**7, nbytes=2 * 10**6
    )
    return call(inputs, branch, gain, current, partner)


def outgoing_kernel(place, inputs, branch, sens_own, sens_other, value_rows, outgoing):
    core, length = place[0], place[1]
    width = sens_own.shape[1]
    inputs_f = inputs[...].astype(F32)
    totals = inputs_f + branch[...].astype(F32)
    row = lax.broadcasted_iota(jnp.int32, totals.shape, 0)
    entering = jnp.where(row < length, totals, 0.0).astype(BF16).astype(F32)
    own = value_rows[:, pl.ds(pl.multiple_of(core * width, 128), width)]
    other = value_rows[:, pl.ds(pl.multiple_of((1 - core) * width, 128), width)]
    back_inputs = by_columns(sens_own[...], own) + by_columns(sens_other[...], other)
    kept = inputs_f * (entering / stabilize(totals))
    outgoing[...] = (kept + inputs_f * back_inputs).astype(BF16)


def last_outgoing(place, inputs, branch, sens_own, sens_other, value_rows):
    call = kernel_call(
        outgoing_kernel,
        jax.ShapeDtypeStruct(inputs.shape, BF16),
        [SMEM] + [VMEM] * 5,
        flops=2 * 10**8,
        nbytes=2 * 10**6,
    )
    return call(place, inputs, branch, sens_own, sens_other, value_rows)


def pair_attention_kernel(place, kept, got, probs_out, gain_t, value_gain, values):
    seq_len = kept.shape[0] - 8
    width = kept.shape[1] - 2 * HD
    heads = width // HD
    row = lax.broadcasted_iota(jnp.int32, (seq_len, seq_len), 0)
    column = lax.broadcasted_iota(jnp.int32, (seq_len, seq_len), 1)

    @pl.when(place[3] == 1)
    def _():
        for half, b in ((kept, place[4]), (got, 1 - place[4])):
            tokens = pl.ds(pl.multiple_of(b * seq_len, 128), seq_len)
            length = jnp.max(half[seq_len:, :HD].astype(F32), axis=0, keepdims=True)
            allowed = (column <= row) & (column.astype(F32) < length)
            value_head = half[:seq_len, width + HD : width + 2 * HD]
            value_f = value_head.astype(F32)
            values[tokens] = value_f
            value_gain[tokens] = value_f / stabilize(value_f)
            stacked = [half[:seq_len, h * HD : (h + 1) * HD] for h in range(heads)]
            scores = by_columns(
                jnp.concatenate(stacked, 0), half[:seq_len, width : width + HD]
            ) / math.sqrt(HD)
            scores = jnp.where(jnp.concatenate([allowed] * heads, 0), scores, -1000000000.0)
            weights = jnp.exp(scores - jnp.max(scores, axis=1, keepdims=True))
            probs = (weights / jnp.sum(weights, axis=1, keepdims=True)).astype(BF16)
            mixed = jnp.dot(probs, value_head, preferred_element_type=F32)
            gain = mixed / stabilize(mixed)
            for h in range(heads):
                at = slice(h * seq_len, (h + 1) * seq_len)
                probs_out[b, h] = probs[at]
                gain_t[h * HD : (h + 1) * HD, tokens] = gain[at].T


def pair_attend(place, kept, got):
    seq_len, width = kept.shape[0] - 8, kept.shape[1] - 2 * HD
    shapes = (
        jax.ShapeDtypeStruct((2, width // HD, seq_len, seq_len), BF16),
        jax.ShapeDtypeStruct((width, 2 * seq_len), F32),
        jax.ShapeDtypeStruct((2 * seq_len, HD), F32),
        jax.ShapeDtypeStruct((2 * seq_len, HD), F32),
    )
    return kernel_call(
        pair_attention_kernel, shapes, [SMEM, VMEM, VMEM], flops=10**8, nbytes=3 * 10**6
    )(place, kept, got)


def main_kernel(count, place, *refs):
    sens, out_block, (before, kept_sum, probs, gain_t, value_gain, values) = refs[:2], refs[2], refs[3:9]
    own_pieces, other_pieces = refs[9 : 9 + count], refs[9 + count : 9 + 2 * count]
    found, halves, total = refs[9 + 2 * count :]
    pos, core, group, active, side = [place[i] for i in range(5)]
    seq_len, half_width = sens[0].shape[0] // 2, sens[0].shape[1]
    width = out_block.shape[1]
    per_core = half_width // width
    quarter = own_pieces[0].shape[0]

    @pl.when(active == 0)
    def _():
        found[...] = before[...]

    @pl.when(active == 1)
    def _():
        for j, half in ((0, core), (1, 1 - core)):
            for i, sequence in ((0, side), (1, 1 - side)):
                rows = pl.ds(pl.multiple_of(sequence * seq_len, 128), seq_len)
                halves[half, rows, :] = sens[j][i * seq_len : (i + 1) * seq_len]

        def part(k):
            owner = lax.rem(pos - k + count + 1, count + 1)
            start = pl.multiple_of(lax.rem(owner, per_core) * width, 128)
            return halves[owner // per_core, :, pl.ds(start, width)]

        rows = pl.ds(pl.multiple_of(side * 2 * quarter, 16), 2 * quarter)
        total[...] = by_columns(out_block[rows, :], part(0))
        for k in range(count):
            operand = part(k + 1)
            for at, piece in ((group, own_pieces[k]), (1 - group, other_pieces[k])):
                rows = pl.ds(pl.multiple_of(at * quarter, 8), quarter)
                total[rows, :] += by_columns(piece[...], operand)
        heats = []
        for b in range(2):
            tokens = slice(b * seq_len, (b + 1) * seq_len)
            back_values = jnp.zeros((HD, seq_len), F32)
            for h in range(probs.shape[1]):
                at = slice(h * HD, (h + 1) * HD)
                sens_mixed = (gain_t[at, tokens] * total[at, tokens]).astype(BF16)
                back_values += jnp.dot(sens_mixed, probs[b, h], preferred_element_type=F32)
            sens_values = (value_gain[tokens] * back_values.T).astype(BF16)
            found[tokens] = sens_values
            heats.append(by_token(sens_values.astype(F32) * values[tokens]))
        mine = jnp.where(side == 0, heats[0], heats[1]) + kept_sum[...]
        found[2 * seq_len :] = heat_rows_of(mine, jnp.where(side == 0, heats[1], heats[0]))


def by_token(array):
    groups = [array[:, at : at + 128] for at in range(0, array.shape[1], 128)]
    return jnp.sum(sum(groups).T, axis=0, keepdims=True)


def heat_rows_of(mine, theirs):
    rows = []
    for heat in (mine, theirs):
        high = heat.astype(BF16).astype(F32)
        rows += [high, heat - high]
    rows.append(jnp.zeros((12, mine.shape[1]), F32))
    return jnp.concatenate(rows, 0).astype(BF16)


def pack_kernel(place, found, got, values, kept_sum, packed):
    side = place[4]
    seq_len = found.shape[0]

    @pl.when(place[3] == 1)
    def _():
        mine, theirs = (
            jnp.where(side == 0, array[:, :HD], array[:, HD:]) for array in (found, got)
        )
        packed[:seq_len] = jnp.where(side == 0, mine, theirs)
        packed[seq_len : 2 * seq_len] = jnp.where(side == 0, theirs, mine)
        heat = by_token(found[...].astype(F32) * values[...]) + kept_sum[...]
        packed[2 * seq_len :] = heat_rows_of(heat, jnp.zeros_like(heat))


def pack_last(place, found, got, values, kept_sum):
    seq_len = found.shape[0]
    shape = jax.ShapeDtypeStruct((2 * seq_len + 16, HD), BF16)
    return kernel_call(pack_kernel, shape, [SMEM] + [VMEM] * 4, nbytes=10**6)(
        place, found, got, values, kept_sum
    )


def main_step(place, sens, out_block, quarters, before, kept_sum, rest):
    count = len(quarters[0])
    seq_len, half_width = sens[0].shape[0] // 2, sens[0].shape[1]
    operands = [*sens, out_block, before, kept_sum, *rest, *quarters[0], *quarters[1]]
    call = kernel_call(
        functools.partial(main_kernel, count),
        jax.ShapeDtypeStruct(before.shape, BF16),
        [SMEM] + [VMEM] * len(operands),
        [pltpu.VMEM((2, 2 * seq_len, half_width), BF16), pltpu.VMEM(rest[1].shape, F32)],
        flops=10**9,
        nbytes=6 * 10**6,
        limit=32,
    )
    return call(place, *operands)


def main_plain(place, sens, out_block, quarters, before, kept_sum, rest):
    pos, core, group, active, side = [place[i] for i in range(5)]
    seq_len = sens[0].shape[0] // 2
    width = out_block.shape[1]
    mine, theirs = (ordered(side == 0, half[:seq_len], half[seq_len:], 0) for half in sens)
    sens_full = ordered(core == 0, mine, theirs, 1)
    count = len(quarters[0])
    quarter = quarters[0][0].shape[0]
    totals = [0.0, 0.0]
    for k in range(count + 1):
        operand = part_of(sens_full, lax.rem(pos - k + count + 1, count + 1), width, 1)
        for half in range(2):
            if k:
                piece = quarters[half][k - 1]
            else:
                at = 2 * side + (group if half == 0 else 1 - group)
                piece = part_of(out_block, at, quarter, 0)
            totals[half] += by_columns(piece, operand)
    total = ordered(group == 0, totals[0], totals[1], 0)
    probs, gain_t, value_gain, values = rest
    sens_mixed = (gain_t * total).astype(BF16).reshape(-1, HD, 2, seq_len)
    back_values = jnp.einsum("hdbt,bhts->bsd", sens_mixed, probs, preferred_element_type=F32)
    found = (value_gain * back_values.reshape(2 * seq_len, HD)).astype(BF16)
    heats = jnp.sum((found.astype(F32) * values).reshape(2, 1, seq_len, HD), axis=3)
    mine = jnp.where(side == 0, heats[0], heats[1]) + kept_sum
    rows = heat_rows_of(mine, jnp.where(side == 0, heats[1], heats[0]))
    return jnp.where(active == 1, jnp.concatenate([found, rows], 0), before)


def turn_kernel(place, *refs):
    *pieces, turned = refs
    count = len(pieces)
    for k, piece in enumerate(pieces):
        rows = piece.shape[0]
        at = pl.multiple_of(lax.rem(place[0] - k + count, count) * rows, 128)
        turned[:, pl.ds(at, rows)] = piece[...].astype(F32).T.astype(BF16)


def turned_side_by_side(place, pieces):
    rows, width = pieces[0].shape
    shape = jax.ShapeDtypeStruct((width, rows * len(pieces)), BF16)
    specs = [SMEM] + [VMEM] * len(pieces)
    return kernel_call(turn_kernel, shape, specs, nbytes=10**6)(place, *pieces)


def heat_of(own, other, place, count):
    partner = lax.rem(2 * place[4] - 1 + count, count)
    size = own[0].shape[0]
    sums = []
    for source in (own, [other[k * size : (k + 1) * size] for k in range(count)]):
        rows = [source[k][size - 16 :].astype(F32) for k in range(count)]
        heat = rows[0][0:1] + rows[0][1:2]
        for k in sorted({1 % count, count - 1}):
            heat += jnp.where(partner == k, rows[k][2:3] + rows[k][3:4], 0.0)
        sums.append(heat)
    heat = sums[0] + sums[1]
    return heat / DW


def relevance_kernel(count, place, inputs_t, value_rows, *refs):
    own, (other, relevance, heat, sens) = refs[:count], refs[count:]
    pos, core = place[0], place[1]
    size = own[0].shape[0]
    rows = size - 16
    for k in range(count):
        source = lax.rem(pos - k + count, count)
        tokens = pl.ds(pl.multiple_of(source // 2 * rows, 128), rows)
        for c, piece in ((core, own[k][:rows]), (1 - core, other[k * size : k * size + rows])):
            head = 2 * c + lax.rem(source, 2)
            sens[tokens, pl.ds(pl.multiple_of(head * HD, 128), HD)] = piece
    rows = relevance.shape[0]
    value_block = value_rows[pl.ds(pl.multiple_of(pos * rows, 16), rows), :]
    summed = jnp.dot(inputs_t[...], sens[...], preferred_element_type=F32)
    relevance[...] = value_block.astype(F32) * summed
    heat[...] = heat_of(own, other, place, count)


def relevance_step(place, inputs_t, value_rows, own, other):
    shapes = (
        jax.ShapeDtypeStruct((inputs_t.shape[0], value_rows.shape[1]), F32),
        jax.ShapeDtypeStruct((1, (own[0].shape[0] - 16) // 2), F32),
    )
    call = kernel_call(
        functools.partial(relevance_kernel, len(own)),
        shapes,
        [SMEM] + [VMEM] * (3 + len(own)),
        [pltpu.VMEM((inputs_t.shape[1], value_rows.shape[1]), BF16)],
        flops=2 * 10**8,
        nbytes=2 * 10**6,
    )
    return call(place, inputs_t, value_rows, *own, other)


def relevance_plain(place, inputs_t, value_rows, own, other):
    pos, core = place[0], place[1]
    count, size = len(own), own[0].shape[0]
    rows = size - 16
    seq_len = rows // 2
    heat = heat_of(own, other, place, count)
    other = [other[k * size : k * size + rows] for k in range(count)]
    own = [piece[:rows] for piece in own]
    even = lax.rem(pos, 2) == 0
    by_core = []
    for sens in (own, other):
        same = jnp.concatenate([sens[k] for k in range(0, count, 2)], 0)
        cross = jnp.concatenate(
            [jnp.where(even, sens[(k - 1) % count], sens[k + 1]) for k in range(0, count, 2)], 0
        )
        by_core.append(ordered(even, same, cross, 1))
    inputs = inputs_t.reshape(-1, count, seq_len)
    tokens = []
    for k in range(0, count, 2):
        tokens.append(jnp.where(even, inputs[:, k], inputs[:, k + 1]))
        tokens.append(jnp.where(even, inputs[:, (k - 1) % count], inputs[:, k]))
    all_sens = ordered(core == 0, by_core[0], by_core[1], 1)
    summed = jnp.dot(jnp.concatenate(tokens, 1), all_sens, preferred_element_type=F32)
    return part_of(value_rows, pos, inputs_t.shape[0], 0).astype(F32) * summed, heat


def moved(shard, axes, target):
    sizes = [lax.axis_size(axis) for axis in axes]
    places = list(itertools.product(*[range(size) for size in sizes]))
    index = {place: i for i, place in enumerate(places)}
    pairs = [(index[place], index[target(*place)]) for place in places if target(*place) is not None]
    return lax.ppermute(shard, axes, pairs)


def along_dp(shard, by):
    peers = lax.axis_size("dp")
    return moved(shard, ("dp",), lambda i: ((i + by) % peers,)) if by else shard


def other_core(shard):
    return moved(shard, ("mp",), lambda c: (1 - c,))


def from_next_section(shard, flip_pair=0):
    return moved(
        shard, ("dp", "section"), lambda i, s: (i ^ flip_pair, s - 1) if s > 0 else None
    )


def ordered(first_is_mine, mine, theirs, axis):
    return jnp.concatenate(
        [jnp.where(first_is_mine, mine, theirs), jnp.where(first_is_mine, theirs, mine)], axis
    )


def part_of(array, index, width, axis):
    return lax.dynamic_slice_in_dim(array, index * width, width, axis)


def once(array, *others):
    return lax.optimization_barrier((array,) + others)[0]


def early_move(shard, axes, target):
    last = lax.axis_size("section") - 1
    at = axes.index("section")
    return moved(shard, axes, lambda *place: target(*place) if place[at] < last else None)


def early_pair(shard):
    return early_move(shard, ("dp", "section"), lambda i, s: (i ^ 1, s))


def early_core(shard):
    return early_move(shard, ("section", "mp"), lambda s, c: (s, 1 - c))


def spread_product(sens_branch, out_block):
    axes = ("dp", "section", "mp")
    peers, cores = lax.axis_size("dp"), lax.axis_size("mp")
    last = lax.axis_size("section") - 1
    pos, core = lax.axis_index("dp"), lax.axis_index("mp")
    seq_len = sens_branch.shape[0]
    width = out_block.shape[1]
    per_core = peers // cores
    arrived = []
    for k in range(peers):
        to = lax.rem(pos + k, peers)
        part = part_of(sens_branch, lax.rem(to, per_core), width, 1)
        if k:
            part = moved(
                part,
                axes,
                lambda i, s, c: ((i + k) % peers, s, c)
                if s == last and c == (i + k) % peers // per_core
                else None,
            )
        arrived.append(part)
    mine = jnp.concatenate(arrived, 0)
    theirs = moved(
        mine,
        axes,
        lambda i, s, c: (i, s, 1 - c) if s == last and c == i // per_core else None,
    )
    if width % 128 == 0:
        use_mine = (core == pos // per_core).astype(jnp.int32)[None]
        own, *sent = spread_products(use_mine, mine, theirs, out_block, seq_len)
    else:
        product = by_columns(jnp.where(core == pos // per_core, mine, theirs), out_block)
        own, *sent = jnp.split(product, peers, axis=0)
    backs = [
        moved(
            sent[k - 1].astype(BF16),
            axes,
            lambda i, s, c: ((i - k) % peers, s, c) if s == last else None,
        )
        for k in range(1, peers)
    ]
    return own, backs


def on_device(hidden_in, attn_out, queries, keys, value_weight, out_weight, lengths):
    inputs = hidden_in[0, 0]
    branch = attn_out[0, 0]
    query_rows = queries[0, 0]
    key_rows = keys[0, 0]
    value_rows = value_weight[0]
    out_block = out_weight[0]
    seq_len, half_width = inputs.shape
    kv_width = key_rows.shape[1]
    head_width = query_rows.shape[1] // 2
    quarter = head_width // 2
    sections = lax.axis_size("section")
    section_pos = lax.axis_index("section")
    group_pos = lax.axis_index("groups")
    peers = lax.axis_size("dp")
    dp_pos = lax.axis_index("dp")
    core_pos = lax.axis_index("mp")
    block_rows = half_width // peers
    side = lax.rem(dp_pos, 2)
    even = side == 0
    is_last = section_pos == sections - 1
    in_tiles = out_block.shape[1] % 128 == 0 and peers <= 8

    def place(active):
        flags = [dp_pos, core_pos, group_pos, active, side]
        return jnp.stack([jnp.asarray(flag, jnp.int32) for flag in flags])

    def core_exchange(mine, take):
        return moved(
            mine, ("section", "mp"), lambda s, c: (s, 1 - c) if take(s == sections - 1) else None
        )

    def values_of(take, rows):
        value_part = jnp.dot(rows, value_rows, preferred_element_type=F32)
        part_mine = part_of(value_part, core_pos, kv_width, 1)
        part_other = part_of(value_part, 1 - core_pos, kv_width, 1)
        return part_mine + core_exchange(part_other.astype(BF16), take).astype(F32)

    def last_section():
        sens_branch = sensitivity(lengths, inputs, branch)
        own, backs = spread_product(sens_branch, out_block)
        values_f = values_of(lambda last: last, once(inputs, own))
        rest = attend(lengths, query_rows, key_rows, values_f)
        leaves, tree = jax.tree.flatten(early_shapes[-1])
        filler = lengths[0].astype(BF16)
        unused = [jnp.full(leaf.shape, filler + k, BF16) for k, leaf in enumerate(leaves)]
        where_last = jnp.stack([core_pos, lengths[0]])
        own, where_last, *unused = lax.optimization_barrier((own, where_last, *unused))
        if peers > 8:
            for back in backs:
                own = own + back.astype(F32)
            backs = []
        found = sum_heads(own, backs, *rest)
        other = core_exchange(found, lambda last: last)
        outgoing = last_outgoing(where_last, inputs, branch, found, other, value_rows)
        return values_f, found, outgoing, jax.tree.unflatten(tree, unused)

    def early_section():
        own_quarters = []
        for k in range(1, peers):
            rows = part_of(out_block, 2 * lax.rem(dp_pos + k, 2) + group_pos, quarter, 0)
            own_quarters.append(
                early_move(rows, ("dp", "section"), lambda i, s: ((i + k) % peers, s))
            )
        other_quarters = [
            early_move(rows, ("groups", "section"), lambda g, s: (1 - g, s))
            for rows in own_quarters
        ]
        values_f = values_of(lambda last: not last, inputs)

        def half_of(which):
            parts = [
                part_of(query_rows, which, head_width, 1),
                part_of(key_rows, which, HD, 1),
                part_of(values_f, which, HD, 1).astype(BF16),
            ]
            packed = jnp.concatenate(parts, 1)
            mark = jnp.full((8, packed.shape[1]), lengths[0].astype(BF16))
            return jnp.concatenate([packed, mark], 0)

        found = jnp.full((seq_len, kv_width), lengths[0].astype(BF16))
        outgoing = jnp.full((seq_len, half_width), lengths[0].astype(BF16))
        partner_gain = early_pair(branch_gain(inputs, branch))
        sent_half = half_of(1 - side)
        sent_half = once(sent_half, *own_quarters, other_quarters[0], other_quarters[-1])
        got_half = early_pair(sent_half)
        kept_half, found, outgoing = half_of(side), *lax.optimization_barrier((found, outgoing, values_f))[:2]
        return values_f, found, outgoing, (
            own_quarters,
            other_quarters,
            (kept_half, got_half, partner_gain),
        )

    early_shapes = jax.eval_shape(early_section)
    values_f, found, outgoing, prepared = lax.cond(is_last, last_section, early_section)
    own_quarters, other_quarters, (kept_half, got_half, partner_gain) = prepared
    arrived = from_next_section(outgoing)
    partner_arrived = from_next_section(outgoing, 1)

    rows = once(inputs, outgoing)
    pieces = [
        along_dp(part_of(rows, lax.rem(dp_pos + k, peers), block_rows, 1), k) for k in range(peers)
    ]
    rest = pair_attend(place(~is_last), kept_half, got_half)
    if in_tiles:
        inputs_t = turned_side_by_side(place(0), pieces)
    else:
        inputs_t = jnp.concatenate(pieces, 0).T

    totals = inputs.astype(F32) + branch.astype(F32)
    valid_rows = (lax.iota(jnp.int32, seq_len) < lengths[0]).astype(F32)
    current = (totals * valid_rows[:, None]).astype(BF16)

    def kept_of(entering):
        return inputs.astype(F32) * (entering.astype(F32) / stabilize(totals))

    got = moved(found, ("dp", "section"), lambda i, s: (i ^ 1, s) if s == sections - 1 else None)
    last_kept = jnp.sum(kept_of(current), axis=1)[None]
    sens_values = pack_last(place(is_last), found, got, values_f, last_kept)

    for turn in range(1, sections):
        active = section_pos == sections - 1 - turn
        current = jnp.where(active, arrived, current)
        if turn == 1:
            arrived, partner_arrived, sens_values, inputs_t, *rest = lax.optimization_barrier(
                (arrived, partner_arrived, sens_values, inputs_t, *rest)
            )
        sens_own, kept_sum = pair_sensitivity(
            inputs, branch, partner_gain, arrived, partner_arrived
        )
        sens = [sens_own, early_core(sens_own)]
        step = main_step if in_tiles else main_plain
        sens_values = step(
            place(active),
            sens,
            out_block,
            (own_quarters, other_quarters),
            sens_values,
            kept_sum,
            rest,
        )
        if turn + 1 < sections:
            mine_now, theirs_now = (part_of(sens_values, w, seq_len, 0) for w in (side, 1 - side))
            found_now = ordered(even, mine_now, early_pair(theirs_now), 1)
            sens_all = ordered(core_pos == 0, found_now, early_core(found_now), 1)
            back_inputs = by_columns(sens_all, value_rows)
            outgoing = kept_of(current) + inputs.astype(F32) * back_inputs
            arrived = from_next_section(outgoing.astype(BF16))
            partner_arrived = from_next_section(outgoing.astype(BF16), 1)

    own_sens = [along_dp(sens_values, k) for k in range(peers)]
    other_sens = other_core(jnp.concatenate(own_sens, 0))
    step = relevance_step if in_tiles else relevance_plain
    relevance_rows, heat_rows = step(place(0), inputs_t, value_rows, own_sens, other_sens)
    return (heat_rows[None], relevance_rows[None])


def solution(mesh):
    placed = (
        P("section", ("groups", "dp"), None, "mp"),
        P("section", ("groups", "dp"), None, "mp"),
        P("section", ("groups", "dp"), None, "mp"),
        P("section", ("groups", "dp"), None, "mp"),
        P("section", "mp", None),
        P("section", "mp", "dp"),
        P(("groups", "dp")),
    )
    return jax.shard_map(
        on_device,
        mesh=mesh,
        in_specs=placed,
        out_specs=(
            P("section", ("groups", "dp"), None),
            P(("groups", "section"), ("mp", "dp"), None),
        ),
        check_vma=False,
    )
```

```python
import functools
import itertools
import math

import jax
import jax.numpy as jnp
from jax import lax
from jax.experimental import pallas as pl
from jax.experimental.pallas import tpu as pltpu
from jax.sharding import PartitionSpec as P

DW = 2560
HD = 128
QH = 20
KVH = 4
EPS = 0.25
F32 = jnp.float32
BF16 = jnp.bfloat16


def stabilize(entries):
    return jnp.where(entries >= 0, entries + EPS, entries - EPS)


VMEM = pl.BlockSpec(memory_space=pltpu.VMEM)
SMEM = pl.BlockSpec(memory_space=pltpu.SMEM)


def by_columns(left, right):
    return lax.dot_general(left, right, (((1,), (1,)), ((), ())), preferred_element_type=F32)


def kernel_call(body, shapes, in_specs, scratch=(), flops=0, nbytes=0, limit=24):
    return pl.pallas_call(
        body,
        out_shape=shapes,
        in_specs=in_specs,
        out_specs=jax.tree.map(lambda _: VMEM, shapes),
        scratch_shapes=scratch,
        compiler_params=pltpu.CompilerParams(vmem_limit_bytes=limit * 2**20),
        cost_estimate=pl.CostEstimate(flops=flops, bytes_accessed=nbytes, transcendentals=0),
    )


def attention_kernel(length, queries, keys, values, probs_t, mixed_gain, value_gain):
    seq_len = queries.shape[0]
    kv_heads = keys.shape[1] // HD
    group_size = queries.shape[1] // HD // kv_heads
    row = lax.broadcasted_iota(jnp.int32, (seq_len, seq_len), 0)
    column = lax.broadcasted_iota(jnp.int32, (seq_len, seq_len), 1)
    allowed = (column <= row) & (column < length[0])
    values_bf = values[...].astype(BF16)
    values_r = values_bf.astype(F32)
    value_gain[...] = values_r / stabilize(values_r)
    for g in range(kv_heads):
        key_head = keys[:, g * HD : (g + 1) * HD]
        value_head = values_bf[:, g * HD : (g + 1) * HD]
        for h in range(g * group_size, (g + 1) * group_size):
            scores = by_columns(queries[:, h * HD : (h + 1) * HD], key_head) / math.sqrt(HD)
            scores = jnp.where(allowed, scores, -1000000000.0)
            weights = jnp.exp(scores - jnp.max(scores, axis=1, keepdims=True))
            probs = weights / jnp.sum(weights, axis=1, keepdims=True)
            probs_t[h] = probs.T.astype(BF16)
            mixed = jnp.dot(probs.astype(BF16), value_head, preferred_element_type=F32)
            mixed_gain[:, h * HD : (h + 1) * HD] = mixed / stabilize(mixed)


def attend(length, queries, keys, values):
    seq_len, width = queries.shape
    shapes = (
        jax.ShapeDtypeStruct((width // HD, seq_len, seq_len), BF16),
        jax.ShapeDtypeStruct((seq_len, width), F32),
        jax.ShapeDtypeStruct(values.shape, F32),
    )
    call = kernel_call(
        attention_kernel, shapes, [SMEM, VMEM, VMEM, VMEM], flops=10**5, nbytes=10**4
    )
    return call(length, queries, keys, values)


def head_step(back_mixed, probs_t, mixed_gain, value_gain, found):
    heads = probs_t.shape[0]
    kv_heads = value_gain.shape[1] // HD
    group_size = heads // kv_heads
    for g in range(kv_heads):
        total = jnp.zeros((probs_t.shape[1], HD), F32)
        for h in range(g * group_size, (g + 1) * group_size):
            at = slice(h * HD, (h + 1) * HD)
            sens_mixed = (mixed_gain[:, at] * back_mixed[:, at]).astype(BF16)
            total += jnp.dot(probs_t[h], sens_mixed, preferred_element_type=F32)
        at = slice(g * HD, (g + 1) * HD)
        found[:, at] = (value_gain[:, at] * total).astype(BF16)


def sum_heads_kernel(count, product, *refs):
    backs, (probs_t, mixed_gain, value_gain, found, total) = refs[:count], refs[count:]
    back_mixed = product[...]
    for back in backs:
        back_mixed += back[...].astype(F32)
    total[...] = back_mixed
    head_step(total, probs_t, mixed_gain, value_gain, found)


def sum_heads(product, backs, probs_t, mixed_gain, value_gain):
    call = kernel_call(
        functools.partial(sum_heads_kernel, len(backs)),
        jax.ShapeDtypeStruct(value_gain.shape, BF16),
        [VMEM] * (4 + len(backs)),
        [pltpu.VMEM(product.shape, F32)],
        flops=5 * 10**7,
        nbytes=3 * 10**6,
    )
    return call(product, *backs, probs_t, mixed_gain, value_gain)


def product_kernel(use_mine, mine, theirs, block, own, *backs):
    seq_len = own.shape[0]

    def multiply(operand):
        product = by_columns(operand[...], block[...])
        own[...] = product[:seq_len]
        for k, back in enumerate(backs):
            back[...] = product[(k + 1) * seq_len : (k + 2) * seq_len].astype(BF16)

    @pl.when(use_mine[0] == 1)
    def _():
        multiply(mine)

    @pl.when(use_mine[0] == 0)
    def _():
        multiply(theirs)


def spread_products(use_mine, mine, theirs, block, seq_len):
    count = mine.shape[0] // seq_len
    width = block.shape[0]
    shapes = (jax.ShapeDtypeStruct((seq_len, width), F32),) + tuple(
        jax.ShapeDtypeStruct((seq_len, width), BF16) for _ in range(count - 1)
    )
    call = kernel_call(
        product_kernel, shapes, [SMEM, VMEM, VMEM, VMEM], flops=10**9, nbytes=5 * 10**6, limit=32
    )
    return call(use_mine, mine, theirs, block)


def sensitivity_kernel(length, inputs, branch, *refs):
    current, sens = refs if len(refs) == 2 else (None, refs[0])
    inputs_f = inputs[...].astype(F32)
    branch_f = branch[...].astype(F32)
    totals = inputs_f + branch_f
    if current is None:
        row = lax.broadcasted_iota(jnp.int32, totals.shape, 0)
        entering = jnp.where(row < length[0], totals, 0.0).astype(BF16).astype(F32)
    else:
        entering = current[...].astype(F32)
    sens[...] = (branch_f * (entering / stabilize(totals)) / stabilize(branch_f)).astype(BF16)


def sensitivity(length, inputs, branch, *current):
    call = kernel_call(
        sensitivity_kernel,
        jax.ShapeDtypeStruct(inputs.shape, BF16),
        [SMEM] + [VMEM] * (2 + len(current)),
        flops=10**7,
        nbytes=10**6,
    )
    return call(length, inputs, branch, *current)


def gain_kernel(inputs, branch, gain):
    branch_f = branch[...].astype(F32)
    totals = inputs[...].astype(F32) + branch_f
    gain[...] = (branch_f / stabilize(totals) / stabilize(branch_f)).astype(BF16)


def branch_gain(inputs, branch):
    shape = jax.ShapeDtypeStruct(inputs.shape, BF16)
    return kernel_call(gain_kernel, shape, [VMEM, VMEM], flops=10**7, nbytes=10**6)(inputs, branch)


def pair_sensitivity_kernel(own_gain, gain, current, partner, sens):
    seq_len = current.shape[0]
    sens[:seq_len] = (current[...].astype(F32) * own_gain[...].astype(F32)).astype(BF16)
    sens[seq_len:] = (partner[...].astype(F32) * gain[...].astype(F32)).astype(BF16)


def pair_sensitivity(own_gain, gain, current, partner):
    seq_len, width = current.shape
    shape = jax.ShapeDtypeStruct((2 * seq_len, width), BF16)
    call = kernel_call(
        pair_sensitivity_kernel, shape, [VMEM] * 4, flops=10**7, nbytes=2 * 10**6
    )
    return call(own_gain, gain, current, partner)


def kept_kernel(inputs, branch, current, kept_sum):
    inputs_f = inputs[...].astype(F32)
    totals = inputs_f + branch[...].astype(F32)
    kept_sum[...] = by_token(inputs_f * (current[...].astype(F32) / stabilize(totals)))


def sum_of_kept(inputs, branch, current):
    shape = jax.ShapeDtypeStruct((1, inputs.shape[0]), F32)
    return kernel_call(kept_kernel, shape, [VMEM] * 3, flops=10**5, nbytes=10**4)(
        inputs, branch, current
    )


def outgoing_kernel(place, inputs, branch, sens_own, sens_other, value_rows, outgoing):
    core, length = place[0], place[1]
    width = sens_own.shape[1]
    inputs_f = inputs[...].astype(F32)
    totals = inputs_f + branch[...].astype(F32)
    row = lax.broadcasted_iota(jnp.int32, totals.shape, 0)
    entering = jnp.where(row < length, totals, 0.0).astype(BF16).astype(F32)
    own = value_rows[:, pl.ds(pl.multiple_of(core * width, 128), width)]
    other = value_rows[:, pl.ds(pl.multiple_of((1 - core) * width, 128), width)]
    back_inputs = by_columns(sens_own[...], own) + by_columns(sens_other[...], other)
    kept = inputs_f * (entering / stabilize(totals))
    outgoing[...] = (kept + inputs_f * back_inputs).astype(BF16)


def last_outgoing(place, inputs, branch, sens_own, sens_other, value_rows):
    call = kernel_call(
        outgoing_kernel,
        jax.ShapeDtypeStruct(inputs.shape, BF16),
        [SMEM] + [VMEM] * 5,
        flops=2 * 10**8,
        nbytes=2 * 10**6,
    )
    return call(place, inputs, branch, sens_own, sens_other, value_rows)


def pair_attention_kernel(place, kept, got, probs_out, gain_t, value_gain, values):
    seq_len = kept.shape[0] - 8
    width = kept.shape[1] - 2 * HD
    heads = width // HD
    row = lax.broadcasted_iota(jnp.int32, (seq_len, seq_len), 0)
    column = lax.broadcasted_iota(jnp.int32, (seq_len, seq_len), 1)

    @pl.when(place[3] == 1)
    def _():
        for half, b in ((kept, place[4]), (got, 1 - place[4])):
            tokens = pl.ds(pl.multiple_of(b * seq_len, 128), seq_len)
            length = jnp.max(half[seq_len:, :HD].astype(F32), axis=0, keepdims=True)
            allowed = (column <= row) & (column.astype(F32) < length)
            value_head = half[:seq_len, width + HD : width + 2 * HD]
            value_f = value_head.astype(F32)
            values[tokens] = value_f
            value_gain[tokens] = value_f / stabilize(value_f)
            stacked = [half[:seq_len, h * HD : (h + 1) * HD] for h in range(heads)]
            scores = by_columns(
                jnp.concatenate(stacked, 0), half[:seq_len, width : width + HD]
            ) / math.sqrt(HD)
            scores = jnp.where(jnp.concatenate([allowed] * heads, 0), scores, -1000000000.0)
            weights = jnp.exp(scores - jnp.max(scores, axis=1, keepdims=True))
            probs = (weights / jnp.sum(weights, axis=1, keepdims=True)).astype(BF16)
            mixed = jnp.dot(probs, value_head, preferred_element_type=F32)
            gain = mixed / stabilize(mixed)
            for h in range(heads):
                at = slice(h * seq_len, (h + 1) * seq_len)
                probs_out[b, h] = probs[at]
                gain_t[h * HD : (h + 1) * HD, tokens] = gain[at].T


def pair_attend(place, kept, got):
    seq_len, width = kept.shape[0] - 8, kept.shape[1] - 2 * HD
    shapes = (
        jax.ShapeDtypeStruct((2, width // HD, seq_len, seq_len), BF16),
        jax.ShapeDtypeStruct((width, 2 * seq_len), F32),
        jax.ShapeDtypeStruct((2 * seq_len, HD), F32),
        jax.ShapeDtypeStruct((2 * seq_len, HD), F32),
    )
    return kernel_call(
        pair_attention_kernel, shapes, [SMEM, VMEM, VMEM], flops=10**8, nbytes=3 * 10**6
    )(place, kept, got)


def main_kernel(count, place, *refs):
    sens, out_block, (before, kept_sum, probs, gain_t, value_gain, values) = refs[:2], refs[2], refs[3:9]
    own_pieces, other_pieces = refs[9 : 9 + count], refs[9 + count : 9 + 2 * count]
    found, halves, total = refs[9 + 2 * count :]
    pos, core, group, active, side = [place[i] for i in range(5)]
    seq_len, half_width = sens[0].shape[0] // 2, sens[0].shape[1]
    width = out_block.shape[1]
    per_core = half_width // width
    quarter = own_pieces[0].shape[0]

    @pl.when(active == 0)
    def _():
        found[...] = before[...]

    @pl.when(active == 1)
    def _():
        for j, half in ((0, core), (1, 1 - core)):
            for i, sequence in ((0, side), (1, 1 - side)):
                rows = pl.ds(pl.multiple_of(sequence * seq_len, 128), seq_len)
                halves[half, rows, :] = sens[j][i * seq_len : (i + 1) * seq_len]

        def part(k):
            owner = lax.rem(pos - k + count + 1, count + 1)
            start = pl.multiple_of(lax.rem(owner, per_core) * width, 128)
            return halves[owner // per_core, :, pl.ds(start, width)]

        rows = pl.ds(pl.multiple_of(side * 2 * quarter, 16), 2 * quarter)
        total[...] = by_columns(out_block[rows, :], part(0))
        for k in range(count):
            operand = part(k + 1)
            for at, piece in ((group, own_pieces[k]), (1 - group, other_pieces[k])):
                rows = pl.ds(pl.multiple_of(at * quarter, 8), quarter)
                total[rows, :] += by_columns(piece[...], operand)
        heats = []
        for b in range(2):
            tokens = slice(b * seq_len, (b + 1) * seq_len)
            back_values = jnp.zeros((HD, seq_len), F32)
            for h in range(probs.shape[1]):
                at = slice(h * HD, (h + 1) * HD)
                sens_mixed = (gain_t[at, tokens] * total[at, tokens]).astype(BF16)
                back_values += jnp.dot(sens_mixed, probs[b, h], preferred_element_type=F32)
            sens_values = (value_gain[tokens] * back_values.T).astype(BF16)
            found[tokens] = sens_values
            heats.append(by_token(sens_values.astype(F32) * values[tokens]))
        mine = jnp.where(side == 0, heats[0], heats[1]) + kept_sum[...]
        found[2 * seq_len :] = heat_rows_of(mine, jnp.where(side == 0, heats[1], heats[0]))


def by_token(array):
    groups = [array[:, at : at + 128] for at in range(0, array.shape[1], 128)]
    return jnp.sum(sum(groups).T, axis=0, keepdims=True)


def heat_rows_of(mine, theirs):
    rows = []
    for heat in (mine, theirs):
        high = heat.astype(BF16).astype(F32)
        rows += [high, heat - high]
    rows.append(jnp.zeros((12, mine.shape[1]), F32))
    return jnp.concatenate(rows, 0).astype(BF16)


def pack_kernel(place, found, got, values, kept_sum, packed):
    side = place[4]
    seq_len = found.shape[0]

    @pl.when(place[3] == 1)
    def _():
        mine, theirs = (
            jnp.where(side == 0, array[:, :HD], array[:, HD:]) for array in (found, got)
        )
        packed[:seq_len] = jnp.where(side == 0, mine, theirs)
        packed[seq_len : 2 * seq_len] = jnp.where(side == 0, theirs, mine)
        heat = by_token(found[...].astype(F32) * values[...]) + kept_sum[...]
        packed[2 * seq_len :] = heat_rows_of(heat, jnp.zeros_like(heat))


def pack_last(place, found, got, values, kept_sum):
    seq_len = found.shape[0]
    shape = jax.ShapeDtypeStruct((2 * seq_len + 16, HD), BF16)
    return kernel_call(pack_kernel, shape, [SMEM] + [VMEM] * 4, nbytes=10**6)(
        place, found, got, values, kept_sum
    )


def main_step(place, sens, out_block, quarters, before, kept_sum, rest):
    count = len(quarters[0])
    seq_len, half_width = sens[0].shape[0] // 2, sens[0].shape[1]
    operands = [*sens, out_block, before, kept_sum, *rest, *quarters[0], *quarters[1]]
    call = kernel_call(
        functools.partial(main_kernel, count),
        jax.ShapeDtypeStruct(before.shape, BF16),
        [SMEM] + [VMEM] * len(operands),
        [pltpu.VMEM((2, 2 * seq_len, half_width), BF16), pltpu.VMEM(rest[1].shape, F32)],
        flops=10**9,
        nbytes=6 * 10**6,
        limit=32,
    )
    return call(place, *operands)


def main_plain(place, sens, out_block, quarters, before, kept_sum, rest):
    pos, core, group, active, side = [place[i] for i in range(5)]
    seq_len = sens[0].shape[0] // 2
    width = out_block.shape[1]
    mine, theirs = (ordered(side == 0, half[:seq_len], half[seq_len:], 0) for half in sens)
    sens_full = ordered(core == 0, mine, theirs, 1)
    count = len(quarters[0])
    quarter = quarters[0][0].shape[0]
    totals = [0.0, 0.0]
    for k in range(count + 1):
        operand = part_of(sens_full, lax.rem(pos - k + count + 1, count + 1), width, 1)
        for half in range(2):
            if k:
                piece = quarters[half][k - 1]
            else:
                at = 2 * side + (group if half == 0 else 1 - group)
                piece = part_of(out_block, at, quarter, 0)
            totals[half] += by_columns(piece, operand)
    total = ordered(group == 0, totals[0], totals[1], 0)
    probs, gain_t, value_gain, values = rest
    sens_mixed = (gain_t * total).astype(BF16).reshape(-1, HD, 2, seq_len)
    back_values = jnp.einsum("hdbt,bhts->bsd", sens_mixed, probs, preferred_element_type=F32)
    found = (value_gain * back_values.reshape(2 * seq_len, HD)).astype(BF16)
    heats = jnp.sum((found.astype(F32) * values).reshape(2, 1, seq_len, HD), axis=3)
    mine = jnp.where(side == 0, heats[0], heats[1]) + kept_sum
    rows = heat_rows_of(mine, jnp.where(side == 0, heats[1], heats[0]))
    return jnp.where(active == 1, jnp.concatenate([found, rows], 0), before)


def turn_kernel(place, *refs):
    *pieces, turned = refs
    count = len(pieces)
    for k, piece in enumerate(pieces):
        rows = piece.shape[0]
        at = pl.multiple_of(lax.rem(place[0] - k + count, count) * rows, 128)
        turned[:, pl.ds(at, rows)] = piece[...].astype(F32).T.astype(BF16)


def turned_side_by_side(place, pieces):
    rows, width = pieces[0].shape
    shape = jax.ShapeDtypeStruct((width, rows * len(pieces)), BF16)
    specs = [SMEM] + [VMEM] * len(pieces)
    return kernel_call(turn_kernel, shape, specs, nbytes=10**6)(place, *pieces)


def heat_of(own, other, place, count):
    partner = lax.rem(2 * place[4] - 1 + count, count)
    size = own[0].shape[0]
    sums = []
    for source in (own, [other[k * size : (k + 1) * size] for k in range(count)]):
        rows = [source[k][size - 16 :].astype(F32) for k in range(count)]
        heat = rows[0][0:1] + rows[0][1:2]
        for k in sorted({1 % count, count - 1}):
            heat += jnp.where(partner == k, rows[k][2:3] + rows[k][3:4], 0.0)
        sums.append(heat)
    heat = sums[0] + sums[1]
    return heat / DW


def relevance_kernel(count, place, inputs_t, value_rows, *refs):
    own, (other, relevance, heat, sens) = refs[:count], refs[count:]
    pos, core = place[0], place[1]
    size = own[0].shape[0]
    rows = size - 16
    for k in range(count):
        source = lax.rem(pos - k + count, count)
        tokens = pl.ds(pl.multiple_of(source // 2 * rows, 128), rows)
        for c, piece in ((core, own[k][:rows]), (1 - core, other[k * size : k * size + rows])):
            head = 2 * c + lax.rem(source, 2)
            sens[tokens, pl.ds(pl.multiple_of(head * HD, 128), HD)] = piece
    rows = relevance.shape[0]
    value_block = value_rows[pl.ds(pl.multiple_of(pos * rows, 16), rows), :]
    summed = jnp.dot(inputs_t[...], sens[...], preferred_element_type=F32)
    relevance[...] = value_block.astype(F32) * summed
    heat[...] = heat_of(own, other, place, count)


def relevance_step(place, inputs_t, value_rows, own, other):
    shapes = (
        jax.ShapeDtypeStruct((inputs_t.shape[0], value_rows.shape[1]), F32),
        jax.ShapeDtypeStruct((1, (own[0].shape[0] - 16) // 2), F32),
    )
    call = kernel_call(
        functools.partial(relevance_kernel, len(own)),
        shapes,
        [SMEM] + [VMEM] * (3 + len(own)),
        [pltpu.VMEM((inputs_t.shape[1], value_rows.shape[1]), BF16)],
        flops=2 * 10**8,
        nbytes=2 * 10**6,
    )
    return call(place, inputs_t, value_rows, *own, other)


def relevance_plain(place, inputs_t, value_rows, own, other):
    pos, core = place[0], place[1]
    count, size = len(own), own[0].shape[0]
    rows = size - 16
    seq_len = rows // 2
    heat = heat_of(own, other, place, count)
    other = [other[k * size : k * size + rows] for k in range(count)]
    own = [piece[:rows] for piece in own]
    even = lax.rem(pos, 2) == 0
    by_core = []
    for sens in (own, other):
        same = jnp.concatenate([sens[k] for k in range(0, count, 2)], 0)
        cross = jnp.concatenate(
            [jnp.where(even, sens[(k - 1) % count], sens[k + 1]) for k in range(0, count, 2)], 0
        )
        by_core.append(ordered(even, same, cross, 1))
    inputs = inputs_t.reshape(-1, count, seq_len)
    tokens = []
    for k in range(0, count, 2):
        tokens.append(jnp.where(even, inputs[:, k], inputs[:, k + 1]))
        tokens.append(jnp.where(even, inputs[:, (k - 1) % count], inputs[:, k]))
    all_sens = ordered(core == 0, by_core[0], by_core[1], 1)
    summed = jnp.dot(jnp.concatenate(tokens, 1), all_sens, preferred_element_type=F32)
    return part_of(value_rows, pos, inputs_t.shape[0], 0).astype(F32) * summed, heat


def moved(shard, axes, target):
    sizes = [lax.axis_size(axis) for axis in axes]
    places = list(itertools.product(*[range(size) for size in sizes]))
    index = {place: i for i, place in enumerate(places)}
    pairs = [(index[place], index[target(*place)]) for place in places if target(*place) is not None]
    return lax.ppermute(shard, axes, pairs)


def along_dp(shard, by):
    peers = lax.axis_size("dp")
    return moved(shard, ("dp",), lambda i: ((i + by) % peers,)) if by else shard


def other_core(shard):
    return moved(shard, ("mp",), lambda c: (1 - c,))


def from_next_section(shard, flip_pair=0):
    return moved(
        shard, ("dp", "section"), lambda i, s: (i ^ flip_pair, s - 1) if s > 0 else None
    )


def ordered(first_is_mine, mine, theirs, axis):
    return jnp.concatenate(
        [jnp.where(first_is_mine, mine, theirs), jnp.where(first_is_mine, theirs, mine)], axis
    )


def part_of(array, index, width, axis):
    return lax.dynamic_slice_in_dim(array, index * width, width, axis)


def once(array, *others):
    return lax.optimization_barrier((array,) + others)[0]


def early_move(shard, axes, target):
    last = lax.axis_size("section") - 1
    at = axes.index("section")
    return moved(shard, axes, lambda *place: target(*place) if place[at] < last else None)


def early_pair(shard):
    return early_move(shard, ("dp", "section"), lambda i, s: (i ^ 1, s))


def early_core(shard):
    return early_move(shard, ("section", "mp"), lambda s, c: (s, 1 - c))


def spread_product(sens_branch, out_block):
    axes = ("dp", "section", "mp")
    peers, cores = lax.axis_size("dp"), lax.axis_size("mp")
    last = lax.axis_size("section") - 1
    pos, core = lax.axis_index("dp"), lax.axis_index("mp")
    seq_len = sens_branch.shape[0]
    width = out_block.shape[1]
    per_core = peers // cores
    arrived = []
    for k in range(peers):
        to = lax.rem(pos + k, peers)
        part = part_of(sens_branch, lax.rem(to, per_core), width, 1)
        if k:
            part = moved(
                part,
                axes,
                lambda i, s, c: ((i + k) % peers, s, c)
                if s == last and c == (i + k) % peers // per_core
                else None,
            )
        arrived.append(part)
    mine = jnp.concatenate(arrived, 0)
    theirs = moved(
        mine,
        axes,
        lambda i, s, c: (i, s, 1 - c) if s == last and c == i // per_core else None,
    )
    if width % 128 == 0:
        use_mine = (core == pos // per_core).astype(jnp.int32)[None]
        own, *sent = spread_products(use_mine, mine, theirs, out_block, seq_len)
    else:
        product = by_columns(jnp.where(core == pos // per_core, mine, theirs), out_block)
        own, *sent = jnp.split(product, peers, axis=0)
    backs = [
        moved(
            sent[k - 1].astype(BF16),
            axes,
            lambda i, s, c: ((i - k) % peers, s, c) if s == last else None,
        )
        for k in range(1, peers)
    ]
    return own, backs


def on_device(hidden_in, attn_out, queries, keys, value_weight, out_weight, lengths):
    inputs = hidden_in[0, 0]
    branch = attn_out[0, 0]
    query_rows = queries[0, 0]
    key_rows = keys[0, 0]
    value_rows = value_weight[0]
    out_block = out_weight[0]
    seq_len, half_width = inputs.shape
    kv_width = key_rows.shape[1]
    head_width = query_rows.shape[1] // 2
    quarter = head_width // 2
    sections = lax.axis_size("section")
    section_pos = lax.axis_index("section")
    group_pos = lax.axis_index("groups")
    peers = lax.axis_size("dp")
    dp_pos = lax.axis_index("dp")
    core_pos = lax.axis_index("mp")
    block_rows = half_width // peers
    side = lax.rem(dp_pos, 2)
    even = side == 0
    is_last = section_pos == sections - 1
    in_tiles = out_block.shape[1] % 128 == 0 and peers <= 8

    def place(active):
        flags = [dp_pos, core_pos, group_pos, active, side]
        return jnp.stack([jnp.asarray(flag, jnp.int32) for flag in flags])

    def core_exchange(mine, take):
        return moved(
            mine, ("section", "mp"), lambda s, c: (s, 1 - c) if take(s == sections - 1) else None
        )

    def values_of(take, rows):
        value_part = jnp.dot(rows, value_rows, preferred_element_type=F32)
        part_mine = part_of(value_part, core_pos, kv_width, 1)
        part_other = part_of(value_part, 1 - core_pos, kv_width, 1)
        return part_mine + core_exchange(part_other.astype(BF16), take).astype(F32)

    def last_section():
        sens_branch = sensitivity(lengths, inputs, branch)
        own, backs = spread_product(sens_branch, out_block)
        values_f = values_of(lambda last: last, once(inputs, own))
        rest = attend(lengths, query_rows, key_rows, values_f)
        leaves, tree = jax.tree.flatten(early_shapes[-1])
        filler = lengths[0].astype(BF16)
        unused = [jnp.full(leaf.shape, filler + k, BF16) for k, leaf in enumerate(leaves)]
        where_last = jnp.stack([core_pos, lengths[0]])
        own, where_last, *unused = lax.optimization_barrier((own, where_last, *unused))
        if peers > 8:
            for back in backs:
                own = own + back.astype(F32)
            backs = []
        found = sum_heads(own, backs, *rest)
        other = core_exchange(found, lambda last: last)
        outgoing = last_outgoing(where_last, inputs, branch, found, other, value_rows)
        return values_f, found, outgoing, jax.tree.unflatten(tree, unused)

    def early_section():
        own_quarters = []
        for k in range(1, peers):
            rows = part_of(out_block, 2 * lax.rem(dp_pos + k, 2) + group_pos, quarter, 0)
            own_quarters.append(
                early_move(rows, ("dp", "section"), lambda i, s: ((i + k) % peers, s))
            )
        other_quarters = [
            early_move(rows, ("groups", "section"), lambda g, s: (1 - g, s))
            for rows in own_quarters
        ]
        values_f = values_of(lambda last: not last, inputs)

        def half_of(which):
            parts = [
                part_of(query_rows, which, head_width, 1),
                part_of(key_rows, which, HD, 1),
                part_of(values_f, which, HD, 1).astype(BF16),
            ]
            packed = jnp.concatenate(parts, 1)
            mark = jnp.full((8, packed.shape[1]), lengths[0].astype(BF16))
            return jnp.concatenate([packed, mark], 0)

        found = jnp.full((seq_len, kv_width), lengths[0].astype(BF16))
        outgoing = jnp.full((seq_len, half_width), lengths[0].astype(BF16))
        partner_gain = early_pair(branch_gain(inputs, branch))
        sent_half = half_of(1 - side)
        sent_half = once(sent_half, *own_quarters, other_quarters[0], other_quarters[-1])
        got_half = early_pair(sent_half)
        kept_half, found, outgoing = half_of(side), *lax.optimization_barrier((found, outgoing, values_f))[:2]
        return values_f, found, outgoing, (
            own_quarters,
            other_quarters,
            (kept_half, got_half, partner_gain),
        )

    early_shapes = jax.eval_shape(early_section)
    values_f, found, outgoing, prepared = lax.cond(is_last, last_section, early_section)
    own_quarters, other_quarters, (kept_half, got_half, partner_gain) = prepared
    arrived = from_next_section(outgoing)
    partner_arrived = from_next_section(outgoing, 1)

    rows = once(inputs, outgoing)
    pieces = [
        along_dp(part_of(rows, lax.rem(dp_pos + k, peers), block_rows, 1), k) for k in range(peers)
    ]
    rest = pair_attend(place(~is_last), kept_half, got_half)
    own_gain = branch_gain(inputs, branch)
    if in_tiles:
        inputs_t = turned_side_by_side(place(0), pieces)
    else:
        inputs_t = jnp.concatenate(pieces, 0).T

    totals = inputs.astype(F32) + branch.astype(F32)
    valid_rows = (lax.iota(jnp.int32, seq_len) < lengths[0]).astype(F32)
    current = (totals * valid_rows[:, None]).astype(BF16)

    def kept_of(entering):
        return inputs.astype(F32) * (entering.astype(F32) / stabilize(totals))

    got = moved(found, ("dp", "section"), lambda i, s: (i ^ 1, s) if s == sections - 1 else None)
    last_kept = jnp.sum(kept_of(current), axis=1)[None]
    sens_values = pack_last(place(is_last), found, got, values_f, last_kept)

    for turn in range(1, sections):
        active = section_pos == sections - 1 - turn
        current = jnp.where(active, arrived, current)
        if turn == 1:
            arrived, partner_arrived, inputs_t, own_gain, *rest = lax.optimization_barrier(
                (arrived, partner_arrived, inputs_t, own_gain, *rest)
            )
        sens_own = pair_sensitivity(own_gain, partner_gain, arrived, partner_arrived)
        kept_sum = sum_of_kept(inputs, branch, arrived)
        sens = [sens_own, early_core(sens_own)]
        step = main_step if in_tiles else main_plain
        sens_values = step(
            place(active),
            sens,
            out_block,
            (own_quarters, other_quarters),
            sens_values,
            kept_sum,
            rest,
        )
        if turn + 1 < sections:
            mine_now, theirs_now = (part_of(sens_values, w, seq_len, 0) for w in (side, 1 - side))
            found_now = ordered(even, mine_now, early_pair(theirs_now), 1)
            sens_all = ordered(core_pos == 0, found_now, early_core(found_now), 1)
            back_inputs = by_columns(sens_all, value_rows)
            outgoing = kept_of(current) + inputs.astype(F32) * back_inputs
            arrived = from_next_section(outgoing.astype(BF16))
            partner_arrived = from_next_section(outgoing.astype(BF16), 1)

    own_sens = [along_dp(sens_values, k) for k in range(peers)]
    other_sens = other_core(jnp.concatenate(own_sens, 0))
    step = relevance_step if in_tiles else relevance_plain
    relevance_rows, heat_rows = step(place(0), inputs_t, value_rows, own_sens, other_sens)
    return (heat_rows[None], relevance_rows[None])


def solution(mesh):
    placed = (
        P("section", ("groups", "dp"), None, "mp"),
        P("section", ("groups", "dp"), None, "mp"),
        P("section", ("groups", "dp"), None, "mp"),
        P("section", ("groups", "dp"), None, "mp"),
        P("section", "mp", None),
        P("section", "mp", "dp"),
        P(("groups", "dp")),
    )
    return jax.shard_map(
        on_device,
        mesh=mesh,
        in_specs=placed,
        out_specs=(
            P("section", ("groups", "dp"), None),
            P(("groups", "section"), ("mp", "dp"), None),
        ),
        check_vma=False,
    )
```

```python
import functools
import itertools
import math

import jax
import jax.numpy as jnp
from jax import lax
from jax.experimental import pallas as pl
from jax.experimental.pallas import tpu as pltpu
from jax.sharding import PartitionSpec as P

DW = 2560
HD = 128
QH = 20
KVH = 4
EPS = 0.25
F32 = jnp.float32
BF16 = jnp.bfloat16


def stabilize(entries):
    return jnp.where(entries >= 0, entries + EPS, entries - EPS)


VMEM = pl.BlockSpec(memory_space=pltpu.VMEM)
SMEM = pl.BlockSpec(memory_space=pltpu.SMEM)


def by_columns(left, right):
    return lax.dot_general(left, right, (((1,), (1,)), ((), ())), preferred_element_type=F32)


def kernel_call(body, shapes, in_specs, scratch=(), flops=0, nbytes=0, limit=24):
    return pl.pallas_call(
        body,
        out_shape=shapes,
        in_specs=in_specs,
        out_specs=jax.tree.map(lambda _: VMEM, shapes),
        scratch_shapes=scratch,
        compiler_params=pltpu.CompilerParams(vmem_limit_bytes=limit * 2**20),
        cost_estimate=pl.CostEstimate(flops=flops, bytes_accessed=nbytes, transcendentals=0),
    )


def attention_kernel(length, queries, keys, values, probs_t, mixed_gain, value_gain):
    seq_len = queries.shape[0]
    kv_heads = keys.shape[1] // HD
    group_size = queries.shape[1] // HD // kv_heads
    row = lax.broadcasted_iota(jnp.int32, (seq_len, seq_len), 0)
    column = lax.broadcasted_iota(jnp.int32, (seq_len, seq_len), 1)
    allowed = (column <= row) & (column < length[0])
    values_bf = values[...].astype(BF16)
    values_r = values_bf.astype(F32)
    value_gain[...] = values_r / stabilize(values_r)
    for g in range(kv_heads):
        key_head = keys[:, g * HD : (g + 1) * HD]
        value_head = values_bf[:, g * HD : (g + 1) * HD]
        for h in range(g * group_size, (g + 1) * group_size):
            scores = by_columns(queries[:, h * HD : (h + 1) * HD], key_head) / math.sqrt(HD)
            scores = jnp.where(allowed, scores, -1000000000.0)
            weights = jnp.exp(scores - jnp.max(scores, axis=1, keepdims=True))
            probs = weights / jnp.sum(weights, axis=1, keepdims=True)
            probs_t[h] = probs.T.astype(BF16)
            mixed = jnp.dot(probs.astype(BF16), value_head, preferred_element_type=F32)
            mixed_gain[:, h * HD : (h + 1) * HD] = mixed / stabilize(mixed)


def attend(length, queries, keys, values):
    seq_len, width = queries.shape
    shapes = (
        jax.ShapeDtypeStruct((width // HD, seq_len, seq_len), BF16),
        jax.ShapeDtypeStruct((seq_len, width), F32),
        jax.ShapeDtypeStruct(values.shape, F32),
    )
    call = kernel_call(
        attention_kernel, shapes, [SMEM, VMEM, VMEM, VMEM], flops=10**5, nbytes=10**4
    )
    return call(length, queries, keys, values)


def head_step(back_mixed, probs_t, mixed_gain, value_gain, found):
    heads = probs_t.shape[0]
    kv_heads = value_gain.shape[1] // HD
    group_size = heads // kv_heads
    for g in range(kv_heads):
        total = jnp.zeros((probs_t.shape[1], HD), F32)
        for h in range(g * group_size, (g + 1) * group_size):
            at = slice(h * HD, (h + 1) * HD)
            sens_mixed = (mixed_gain[:, at] * back_mixed[:, at]).astype(BF16)
            total += jnp.dot(probs_t[h], sens_mixed, preferred_element_type=F32)
        at = slice(g * HD, (g + 1) * HD)
        found[:, at] = (value_gain[:, at] * total).astype(BF16)


def sum_heads_kernel(count, product, *refs):
    backs, (probs_t, mixed_gain, value_gain, found, total) = refs[:count], refs[count:]
    back_mixed = product[...]
    for back in backs:
        back_mixed += back[...].astype(F32)
    total[...] = back_mixed
    head_step(total, probs_t, mixed_gain, value_gain, found)


def sum_heads(product, backs, probs_t, mixed_gain, value_gain):
    call = kernel_call(
        functools.partial(sum_heads_kernel, len(backs)),
        jax.ShapeDtypeStruct(value_gain.shape, BF16),
        [VMEM] * (4 + len(backs)),
        [pltpu.VMEM(product.shape, F32)],
        flops=5 * 10**7,
        nbytes=3 * 10**6,
    )
    return call(product, *backs, probs_t, mixed_gain, value_gain)


def product_kernel(use_mine, mine, theirs, block, own, *backs):
    seq_len = own.shape[0]

    def multiply(operand):
        product = by_columns(operand[...], block[...])
        own[...] = product[:seq_len]
        for k, back in enumerate(backs):
            back[...] = product[(k + 1) * seq_len : (k + 2) * seq_len].astype(BF16)

    @pl.when(use_mine[0] == 1)
    def _():
        multiply(mine)

    @pl.when(use_mine[0] == 0)
    def _():
        multiply(theirs)


def spread_products(use_mine, mine, theirs, block, seq_len):
    count = mine.shape[0] // seq_len
    width = block.shape[0]
    shapes = (jax.ShapeDtypeStruct((seq_len, width), F32),) + tuple(
        jax.ShapeDtypeStruct((seq_len, width), BF16) for _ in range(count - 1)
    )
    call = kernel_call(
        product_kernel, shapes, [SMEM, VMEM, VMEM, VMEM], flops=10**9, nbytes=5 * 10**6, limit=32
    )
    return call(use_mine, mine, theirs, block)


def sensitivity_kernel(length, inputs, branch, *refs):
    current, sens = refs if len(refs) == 2 else (None, refs[0])
    inputs_f = inputs[...].astype(F32)
    branch_f = branch[...].astype(F32)
    totals = inputs_f + branch_f
    if current is None:
        row = lax.broadcasted_iota(jnp.int32, totals.shape, 0)
        entering = jnp.where(row < length[0], totals, 0.0).astype(BF16).astype(F32)
    else:
        entering = current[...].astype(F32)
    sens[...] = (branch_f * (entering / stabilize(totals)) / stabilize(branch_f)).astype(BF16)


def sensitivity(length, inputs, branch, *current):
    call = kernel_call(
        sensitivity_kernel,
        jax.ShapeDtypeStruct(inputs.shape, BF16),
        [SMEM] + [VMEM] * (2 + len(current)),
        flops=10**7,
        nbytes=10**6,
    )
    return call(length, inputs, branch, *current)


def gain_kernel(inputs, branch, gain):
    branch_f = branch[...].astype(F32)
    totals = inputs[...].astype(F32) + branch_f
    gain[...] = (branch_f / stabilize(totals) / stabilize(branch_f)).astype(BF16)


def branch_gain(inputs, branch):
    shape = jax.ShapeDtypeStruct(inputs.shape, BF16)
    return kernel_call(gain_kernel, shape, [VMEM, VMEM], flops=10**7, nbytes=10**6)(inputs, branch)


def pair_sensitivity_kernel(own_gain, gain, current, partner, sens):
    seq_len = current.shape[0]
    sens[:seq_len] = (current[...].astype(F32) * own_gain[...].astype(F32)).astype(BF16)
    sens[seq_len:] = (partner[...].astype(F32) * gain[...].astype(F32)).astype(BF16)


def pair_sensitivity(own_gain, gain, current, partner):
    seq_len, width = current.shape
    shape = jax.ShapeDtypeStruct((2 * seq_len, width), BF16)
    call = kernel_call(
        pair_sensitivity_kernel, shape, [VMEM] * 4, flops=10**7, nbytes=2 * 10**6
    )
    return call(own_gain, gain, current, partner)


def kept_kernel(inputs, branch, current, kept_sum):
    inputs_f = inputs[...].astype(F32)
    totals = inputs_f + branch[...].astype(F32)
    kept_sum[...] = by_token(inputs_f * (current[...].astype(F32) / stabilize(totals)))


def sum_of_kept(inputs, branch, current):
    shape = jax.ShapeDtypeStruct((1, inputs.shape[0]), F32)
    return kernel_call(kept_kernel, shape, [VMEM] * 3, flops=10**5, nbytes=10**4)(
        inputs, branch, current
    )


def outgoing_kernel(place, inputs, branch, sens_own, sens_other, value_rows, outgoing):
    core, length = place[0], place[1]
    width = sens_own.shape[1]
    inputs_f = inputs[...].astype(F32)
    totals = inputs_f + branch[...].astype(F32)
    row = lax.broadcasted_iota(jnp.int32, totals.shape, 0)
    entering = jnp.where(row < length, totals, 0.0).astype(BF16).astype(F32)
    own = value_rows[:, pl.ds(pl.multiple_of(core * width, 128), width)]
    other = value_rows[:, pl.ds(pl.multiple_of((1 - core) * width, 128), width)]
    back_inputs = by_columns(sens_own[...], own) + by_columns(sens_other[...], other)
    kept = inputs_f * (entering / stabilize(totals))
    outgoing[...] = (kept + inputs_f * back_inputs).astype(BF16)


def last_outgoing(place, inputs, branch, sens_own, sens_other, value_rows):
    call = kernel_call(
        outgoing_kernel,
        jax.ShapeDtypeStruct(inputs.shape, BF16),
        [SMEM] + [VMEM] * 5,
        flops=2 * 10**8,
        nbytes=2 * 10**6,
    )
    return call(place, inputs, branch, sens_own, sens_other, value_rows)


def pair_attention_kernel(place, kept, got, probs_out, gain_t, value_gain, values):
    seq_len = kept.shape[0] - 8
    width = kept.shape[1] - 2 * HD
    heads = width // HD
    row = lax.broadcasted_iota(jnp.int32, (seq_len, seq_len), 0)
    column = lax.broadcasted_iota(jnp.int32, (seq_len, seq_len), 1)

    @pl.when(place[3] == 1)
    def _():
        for half, b in ((kept, place[4]), (got, 1 - place[4])):
            tokens = pl.ds(pl.multiple_of(b * seq_len, 128), seq_len)
            length = jnp.max(half[seq_len:, :HD].astype(F32), axis=0, keepdims=True)
            allowed = (column <= row) & (column.astype(F32) < length)
            value_head = half[:seq_len, width + HD : width + 2 * HD]
            value_f = value_head.astype(F32)
            values[tokens] = value_f
            value_gain[tokens] = value_f / stabilize(value_f)
            stacked = [half[:seq_len, h * HD : (h + 1) * HD] for h in range(heads)]
            scores = by_columns(
                jnp.concatenate(stacked, 0), half[:seq_len, width : width + HD]
            ) / math.sqrt(HD)
            scores = jnp.where(jnp.concatenate([allowed] * heads, 0), scores, -1000000000.0)
            weights = jnp.exp(scores - jnp.max(scores, axis=1, keepdims=True))
            probs = (weights / jnp.sum(weights, axis=1, keepdims=True)).astype(BF16)
            mixed = jnp.dot(probs, value_head, preferred_element_type=F32)
            gain = mixed / stabilize(mixed)
            for h in range(heads):
                at = slice(h * seq_len, (h + 1) * seq_len)
                probs_out[b, h] = probs[at]
                gain_t[h * HD : (h + 1) * HD, tokens] = gain[at].T


def pair_attend(place, kept, got):
    seq_len, width = kept.shape[0] - 8, kept.shape[1] - 2 * HD
    shapes = (
        jax.ShapeDtypeStruct((2, width // HD, seq_len, seq_len), BF16),
        jax.ShapeDtypeStruct((width, 2 * seq_len), F32),
        jax.ShapeDtypeStruct((2 * seq_len, HD), F32),
        jax.ShapeDtypeStruct((2 * seq_len, HD), F32),
    )
    return kernel_call(
        pair_attention_kernel, shapes, [SMEM, VMEM, VMEM], flops=10**8, nbytes=3 * 10**6
    )(place, kept, got)


def main_kernel(count, place, *refs):
    sens, out_block, (before, kept_sum, probs, gain_t, value_gain, values) = refs[:2], refs[2], refs[3:9]
    own_pieces, other_pieces = refs[9 : 9 + count], refs[9 + count : 9 + 2 * count]
    found, halves, total = refs[9 + 2 * count :]
    pos, core, group, active, side = [place[i] for i in range(5)]
    seq_len, half_width = sens[0].shape[0] // 2, sens[0].shape[1]
    width = out_block.shape[1]
    per_core = half_width // width
    quarter = own_pieces[0].shape[0]

    @pl.when(active == 0)
    def _():
        found[...] = before[...]

    @pl.when(active == 1)
    def _():
        for j, half in ((0, core), (1, 1 - core)):
            for i, sequence in ((0, side), (1, 1 - side)):
                rows = pl.ds(pl.multiple_of(sequence * seq_len, 128), seq_len)
                halves[half, rows, :] = sens[j][i * seq_len : (i + 1) * seq_len]

        def part(k):
            owner = lax.rem(pos - k + count + 1, count + 1)
            start = pl.multiple_of(lax.rem(owner, per_core) * width, 128)
            return halves[owner // per_core, :, pl.ds(start, width)]

        total[...] = by_columns(out_block[...], part(0))
        for k in range(count):
            operand = part(k + 1)
            for at, piece in ((group, own_pieces[k]), (1 - group, other_pieces[k])):
                rows = pl.ds(pl.multiple_of(at * quarter, 8), quarter)
                total[rows, :] += by_columns(piece[...], operand)
        heats = []
        for b in range(2):
            tokens = slice(b * seq_len, (b + 1) * seq_len)
            back_values = jnp.zeros((HD, seq_len), F32)
            for h in range(probs.shape[1]):
                at = slice(h * HD, (h + 1) * HD)
                sens_mixed = (gain_t[at, tokens] * total[at, tokens]).astype(BF16)
                back_values += jnp.dot(sens_mixed, probs[b, h], preferred_element_type=F32)
            sens_values = (value_gain[tokens] * back_values.T).astype(BF16)
            found[tokens] = sens_values
            heats.append(by_token(sens_values.astype(F32) * values[tokens]))
        mine = jnp.where(side == 0, heats[0], heats[1]) + kept_sum[...]
        found[2 * seq_len :] = heat_rows_of(mine, jnp.where(side == 0, heats[1], heats[0]))


def by_token(array):
    groups = [array[:, at : at + 128] for at in range(0, array.shape[1], 128)]
    return jnp.sum(sum(groups).T, axis=0, keepdims=True)


def heat_rows_of(mine, theirs):
    rows = []
    for heat in (mine, theirs):
        high = heat.astype(BF16).astype(F32)
        rows += [high, heat - high]
    rows.append(jnp.zeros((12, mine.shape[1]), F32))
    return jnp.concatenate(rows, 0).astype(BF16)


def pack_kernel(place, found, got, values, kept_sum, packed):
    side = place[4]
    seq_len = found.shape[0]

    @pl.when(place[3] == 1)
    def _():
        mine, theirs = (
            jnp.where(side == 0, array[:, :HD], array[:, HD:]) for array in (found, got)
        )
        packed[:seq_len] = jnp.where(side == 0, mine, theirs)
        packed[seq_len : 2 * seq_len] = jnp.where(side == 0, theirs, mine)
        heat = by_token(found[...].astype(F32) * values[...]) + kept_sum[...]
        packed[2 * seq_len :] = heat_rows_of(heat, jnp.zeros_like(heat))


def pack_last(place, found, got, values, kept_sum):
    seq_len = found.shape[0]
    shape = jax.ShapeDtypeStruct((2 * seq_len + 16, HD), BF16)
    return kernel_call(pack_kernel, shape, [SMEM] + [VMEM] * 4, nbytes=10**6)(
        place, found, got, values, kept_sum
    )


def main_step(place, sens, out_block, quarters, before, kept_sum, rest):
    count = len(quarters[0])
    seq_len, half_width = sens[0].shape[0] // 2, sens[0].shape[1]
    operands = [*sens, out_block, before, kept_sum, *rest, *quarters[0], *quarters[1]]
    call = kernel_call(
        functools.partial(main_kernel, count),
        jax.ShapeDtypeStruct(before.shape, BF16),
        [SMEM] + [VMEM] * len(operands),
        [pltpu.VMEM((2, 2 * seq_len, half_width), BF16), pltpu.VMEM(rest[1].shape, F32)],
        flops=10**9,
        nbytes=6 * 10**6,
        limit=32,
    )
    return call(place, *operands)


def main_plain(place, sens, out_block, quarters, before, kept_sum, rest):
    pos, core, group, active, side = [place[i] for i in range(5)]
    seq_len = sens[0].shape[0] // 2
    width = out_block.shape[1]
    mine, theirs = (ordered(side == 0, half[:seq_len], half[seq_len:], 0) for half in sens)
    sens_full = ordered(core == 0, mine, theirs, 1)
    count = len(quarters[0])
    quarter = quarters[0][0].shape[0]
    totals = [0.0, 0.0]
    for k in range(count + 1):
        operand = part_of(sens_full, lax.rem(pos - k + count + 1, count + 1), width, 1)
        for half in range(2):
            if k:
                piece = quarters[half][k - 1]
            else:
                piece = part_of(out_block, group if half == 0 else 1 - group, quarter, 0)
            totals[half] += by_columns(piece, operand)
    total = ordered(group == 0, totals[0], totals[1], 0)
    probs, gain_t, value_gain, values = rest
    sens_mixed = (gain_t * total).astype(BF16).reshape(-1, HD, 2, seq_len)
    back_values = jnp.einsum("hdbt,bhts->bsd", sens_mixed, probs, preferred_element_type=F32)
    found = (value_gain * back_values.reshape(2 * seq_len, HD)).astype(BF16)
    heats = jnp.sum((found.astype(F32) * values).reshape(2, 1, seq_len, HD), axis=3)
    mine = jnp.where(side == 0, heats[0], heats[1]) + kept_sum
    rows = heat_rows_of(mine, jnp.where(side == 0, heats[1], heats[0]))
    return jnp.where(active == 1, jnp.concatenate([found, rows], 0), before)


def turn_kernel(place, *refs):
    *pieces, turned = refs
    count = len(pieces)
    for k, piece in enumerate(pieces):
        rows = piece.shape[0]
        at = pl.multiple_of(lax.rem(place[0] - k + count, count) * rows, 128)
        turned[:, pl.ds(at, rows)] = piece[...].astype(F32).T.astype(BF16)


def turned_side_by_side(place, pieces):
    rows, width = pieces[0].shape
    shape = jax.ShapeDtypeStruct((width, rows * len(pieces)), BF16)
    specs = [SMEM] + [VMEM] * len(pieces)
    return kernel_call(turn_kernel, shape, specs, nbytes=10**6)(place, *pieces)


def heat_of(own, other, place, count):
    partner = lax.rem(2 * place[4] - 1 + count, count)
    size = own[0].shape[0]
    sums = []
    for source in (own, [other[k * size : (k + 1) * size] for k in range(count)]):
        rows = [source[k][size - 16 :].astype(F32) for k in range(count)]
        heat = rows[0][0:1] + rows[0][1:2]
        for k in sorted({1 % count, count - 1}):
            heat += jnp.where(partner == k, rows[k][2:3] + rows[k][3:4], 0.0)
        sums.append(heat)
    heat = sums[0] + sums[1]
    return heat / DW


def relevance_kernel(count, place, inputs_t, value_rows, *refs):
    own, (other, relevance, heat, sens) = refs[:count], refs[count:]
    pos, core = place[0], place[1]
    size = own[0].shape[0]
    rows = size - 16
    for k in range(count):
        source = lax.rem(pos - k + count, count)
        tokens = pl.ds(pl.multiple_of(source // 2 * rows, 128), rows)
        for c, piece in ((core, own[k][:rows]), (1 - core, other[k * size : k * size + rows])):
            head = 2 * c + lax.rem(source, 2)
            sens[tokens, pl.ds(pl.multiple_of(head * HD, 128), HD)] = piece
    rows = relevance.shape[0]
    value_block = value_rows[pl.ds(pl.multiple_of(pos * rows, 16), rows), :]
    summed = jnp.dot(inputs_t[...], sens[...], preferred_element_type=F32)
    relevance[...] = value_block.astype(F32) * summed
    heat[...] = heat_of(own, other, place, count)


def relevance_step(place, inputs_t, value_rows, own, other):
    shapes = (
        jax.ShapeDtypeStruct((inputs_t.shape[0], value_rows.shape[1]), F32),
        jax.ShapeDtypeStruct((1, (own[0].shape[0] - 16) // 2), F32),
    )
    call = kernel_call(
        functools.partial(relevance_kernel, len(own)),
        shapes,
        [SMEM] + [VMEM] * (3 + len(own)),
        [pltpu.VMEM((inputs_t.shape[1], value_rows.shape[1]), BF16)],
        flops=2 * 10**8,
        nbytes=2 * 10**6,
    )
    return call(place, inputs_t, value_rows, *own, other)


def relevance_plain(place, inputs_t, value_rows, own, other):
    pos, core = place[0], place[1]
    count, size = len(own), own[0].shape[0]
    rows = size - 16
    seq_len = rows // 2
    heat = heat_of(own, other, place, count)
    other = [other[k * size : k * size + rows] for k in range(count)]
    own = [piece[:rows] for piece in own]
    even = lax.rem(pos, 2) == 0
    by_core = []
    for sens in (own, other):
        same = jnp.concatenate([sens[k] for k in range(0, count, 2)], 0)
        cross = jnp.concatenate(
            [jnp.where(even, sens[(k - 1) % count], sens[k + 1]) for k in range(0, count, 2)], 0
        )
        by_core.append(ordered(even, same, cross, 1))
    inputs = inputs_t.reshape(-1, count, seq_len)
    tokens = []
    for k in range(0, count, 2):
        tokens.append(jnp.where(even, inputs[:, k], inputs[:, k + 1]))
        tokens.append(jnp.where(even, inputs[:, (k - 1) % count], inputs[:, k]))
    all_sens = ordered(core == 0, by_core[0], by_core[1], 1)
    summed = jnp.dot(jnp.concatenate(tokens, 1), all_sens, preferred_element_type=F32)
    return part_of(value_rows, pos, inputs_t.shape[0], 0).astype(F32) * summed, heat


def moved(shard, axes, target):
    sizes = [lax.axis_size(axis) for axis in axes]
    places = list(itertools.product(*[range(size) for size in sizes]))
    index = {place: i for i, place in enumerate(places)}
    pairs = [(index[place], index[target(*place)]) for place in places if target(*place) is not None]
    return lax.ppermute(shard, axes, pairs)


def along_dp(shard, by):
    peers = lax.axis_size("dp")
    return moved(shard, ("dp",), lambda i: ((i + by) % peers,)) if by else shard


def other_core(shard):
    return moved(shard, ("mp",), lambda c: (1 - c,))


def from_next_section(shard, flip_pair=0):
    return moved(
        shard, ("dp", "section"), lambda i, s: (i ^ flip_pair, s - 1) if s > 0 else None
    )


def ordered(first_is_mine, mine, theirs, axis):
    return jnp.concatenate(
        [jnp.where(first_is_mine, mine, theirs), jnp.where(first_is_mine, theirs, mine)], axis
    )


def part_of(array, index, width, axis):
    return lax.dynamic_slice_in_dim(array, index * width, width, axis)


def once(array, *others):
    return lax.optimization_barrier((array,) + others)[0]


def early_move(shard, axes, target):
    last = lax.axis_size("section") - 1
    at = axes.index("section")
    return moved(shard, axes, lambda *place: target(*place) if place[at] < last else None)


def early_pair(shard):
    return early_move(shard, ("dp", "section"), lambda i, s: (i ^ 1, s))


def early_core(shard):
    return early_move(shard, ("section", "mp"), lambda s, c: (s, 1 - c))


def spread_product(sens_branch, out_block):
    axes = ("dp", "section", "mp")
    peers, cores = lax.axis_size("dp"), lax.axis_size("mp")
    last = lax.axis_size("section") - 1
    pos, core = lax.axis_index("dp"), lax.axis_index("mp")
    seq_len = sens_branch.shape[0]
    width = out_block.shape[1]
    per_core = peers // cores
    arrived = []
    for k in range(peers):
        to = lax.rem(pos + k, peers)
        part = part_of(sens_branch, lax.rem(to, per_core), width, 1)
        if k:
            part = moved(
                part,
                axes,
                lambda i, s, c: ((i + k) % peers, s, c)
                if s == last and c == (i + k) % peers // per_core
                else None,
            )
        arrived.append(part)
    mine = jnp.concatenate(arrived, 0)
    theirs = moved(
        mine,
        axes,
        lambda i, s, c: (i, s, 1 - c) if s == last and c == i // per_core else None,
    )
    if width % 128 == 0:
        use_mine = (core == pos // per_core).astype(jnp.int32)[None]
        own, *sent = spread_products(use_mine, mine, theirs, out_block, seq_len)
    else:
        product = by_columns(jnp.where(core == pos // per_core, mine, theirs), out_block)
        own, *sent = jnp.split(product, peers, axis=0)
    backs = [
        moved(
            sent[k - 1].astype(BF16),
            axes,
            lambda i, s, c: ((i - k) % peers, s, c) if s == last else None,
        )
        for k in range(1, peers)
    ]
    return own, backs


def on_device(hidden_in, attn_out, queries, keys, value_weight, out_weight, lengths):
    inputs = hidden_in[0, 0]
    branch = attn_out[0, 0]
    query_rows = queries[0, 0]
    key_rows = keys[0, 0]
    value_rows = value_weight[0]
    out_block = out_weight[0]
    seq_len, half_width = inputs.shape
    kv_width = key_rows.shape[1]
    head_width = query_rows.shape[1] // 2
    quarter = head_width // 2
    sections = lax.axis_size("section")
    section_pos = lax.axis_index("section")
    group_pos = lax.axis_index("groups")
    peers = lax.axis_size("dp")
    dp_pos = lax.axis_index("dp")
    core_pos = lax.axis_index("mp")
    block_rows = half_width // peers
    side = lax.rem(dp_pos, 2)
    even = side == 0
    is_last = section_pos == sections - 1
    in_tiles = out_block.shape[1] % 128 == 0 and peers <= 8

    def place(active):
        flags = [dp_pos, core_pos, group_pos, active, side]
        return jnp.stack([jnp.asarray(flag, jnp.int32) for flag in flags])

    def core_exchange(mine, take):
        return moved(
            mine, ("section", "mp"), lambda s, c: (s, 1 - c) if take(s == sections - 1) else None
        )

    def values_of(take, rows):
        value_part = jnp.dot(rows, value_rows, preferred_element_type=F32)
        part_mine = part_of(value_part, core_pos, kv_width, 1)
        part_other = part_of(value_part, 1 - core_pos, kv_width, 1)
        return part_mine + core_exchange(part_other.astype(BF16), take).astype(F32)

    def last_section():
        sens_branch = sensitivity(lengths, inputs, branch)
        own, backs = spread_product(sens_branch, out_block)
        values_f = values_of(lambda last: last, once(inputs, own))
        rest = attend(lengths, query_rows, key_rows, values_f)
        leaves, tree = jax.tree.flatten(early_shapes[-1])
        filler = lengths[0].astype(BF16)
        unused = [jnp.full(leaf.shape, filler + k, BF16) for k, leaf in enumerate(leaves)]
        where_last = jnp.stack([core_pos, lengths[0]])
        own, where_last, *unused = lax.optimization_barrier((own, where_last, *unused))
        if peers > 8:
            for back in backs:
                own = own + back.astype(F32)
            backs = []
        found = sum_heads(own, backs, *rest)
        other = core_exchange(found, lambda last: last)
        outgoing = last_outgoing(where_last, inputs, branch, found, other, value_rows)
        return values_f, found, outgoing, jax.tree.unflatten(tree, unused)

    def early_section():
        own_quarters = []
        for k in range(1, peers):
            rows = part_of(out_block, 2 * lax.rem(dp_pos + k, 2) + group_pos, quarter, 0)
            own_quarters.append(
                early_move(rows, ("dp", "section"), lambda i, s: ((i + k) % peers, s))
            )
        other_quarters = [
            early_move(rows, ("groups", "section"), lambda g, s: (1 - g, s))
            for rows in own_quarters
        ]
        values_f = values_of(lambda last: not last, inputs)

        def half_of(which):
            parts = [
                part_of(query_rows, which, head_width, 1),
                part_of(key_rows, which, HD, 1),
                part_of(values_f, which, HD, 1).astype(BF16),
            ]
            packed = jnp.concatenate(parts, 1)
            mark = jnp.full((8, packed.shape[1]), lengths[0].astype(BF16))
            return jnp.concatenate([packed, mark], 0)

        found = jnp.full((seq_len, kv_width), lengths[0].astype(BF16))
        outgoing = jnp.full((seq_len, half_width), lengths[0].astype(BF16))
        partner_gain = early_pair(branch_gain(inputs, branch))
        sent_half = half_of(1 - side)
        sent_half = once(sent_half, *own_quarters, other_quarters[0], other_quarters[-1])
        got_half = early_pair(sent_half)
        kept_half, found, outgoing = half_of(side), *lax.optimization_barrier((found, outgoing, values_f))[:2]
        return values_f, found, outgoing, (
            own_quarters,
            other_quarters,
            (kept_half, got_half, partner_gain),
        )

    early_shapes = jax.eval_shape(early_section)
    values_f, found, outgoing, prepared = lax.cond(is_last, last_section, early_section)
    own_quarters, other_quarters, (kept_half, got_half, partner_gain) = prepared
    arrived = from_next_section(outgoing)
    partner_arrived = from_next_section(outgoing, 1)

    rows = once(inputs, outgoing)
    pieces = [
        along_dp(part_of(rows, lax.rem(dp_pos + k, peers), block_rows, 1), k) for k in range(peers)
    ]
    rest = pair_attend(place(~is_last), kept_half, got_half)
    own_gain = branch_gain(inputs, branch)
    own_block = part_of(out_block, side, head_width, 0)
    if in_tiles:
        inputs_t = turned_side_by_side(place(0), pieces)
    else:
        inputs_t = jnp.concatenate(pieces, 0).T

    totals = inputs.astype(F32) + branch.astype(F32)
    valid_rows = (lax.iota(jnp.int32, seq_len) < lengths[0]).astype(F32)
    current = (totals * valid_rows[:, None]).astype(BF16)

    def kept_of(entering):
        return inputs.astype(F32) * (entering.astype(F32) / stabilize(totals))

    got = moved(found, ("dp", "section"), lambda i, s: (i ^ 1, s) if s == sections - 1 else None)
    last_kept = jnp.sum(kept_of(current), axis=1)[None]
    sens_values = pack_last(place(is_last), found, got, values_f, last_kept)

    for turn in range(1, sections):
        active = section_pos == sections - 1 - turn
        current = jnp.where(active, arrived, current)
        if turn == 1:
            arrived, partner_arrived, inputs_t, own_gain, own_block, *rest = lax.optimization_barrier(
                (arrived, partner_arrived, inputs_t, own_gain, own_block, *rest)
            )
        sens_own = pair_sensitivity(own_gain, partner_gain, arrived, partner_arrived)
        kept_sum = sum_of_kept(inputs, branch, arrived)
        sens = [sens_own, early_core(sens_own)]
        step = main_step if in_tiles else main_plain
        sens_values = step(
            place(active),
            sens,
            own_block,
            (own_quarters, other_quarters),
            sens_values,
            kept_sum,
            rest,
        )
        if turn + 1 < sections:
            mine_now, theirs_now = (part_of(sens_values, w, seq_len, 0) for w in (side, 1 - side))
            found_now = ordered(even, mine_now, early_pair(theirs_now), 1)
            sens_all = ordered(core_pos == 0, found_now, early_core(found_now), 1)
            back_inputs = by_columns(sens_all, value_rows)
            outgoing = kept_of(current) + inputs.astype(F32) * back_inputs
            arrived = from_next_section(outgoing.astype(BF16))
            partner_arrived = from_next_section(outgoing.astype(BF16), 1)

    own_sens = [along_dp(sens_values, k) for k in range(peers)]
    other_sens = other_core(jnp.concatenate(own_sens, 0))
    step = relevance_step if in_tiles else relevance_plain
    relevance_rows, heat_rows = step(place(0), inputs_t, value_rows, own_sens, other_sens)
    return (heat_rows[None], relevance_rows[None])


def solution(mesh):
    placed = (
        P("section", ("groups", "dp"), None, "mp"),
        P("section", ("groups", "dp"), None, "mp"),
        P("section", ("groups", "dp"), None, "mp"),
        P("section", ("groups", "dp"), None, "mp"),
        P("section", "mp", None),
        P("section", "mp", "dp"),
        P(("groups", "dp")),
    )
    return jax.shard_map(
        on_device,
        mesh=mesh,
        in_specs=placed,
        out_specs=(
            P("section", ("groups", "dp"), None),
            P(("groups", "section"), ("mp", "dp"), None),
        ),
        check_vma=False,
    )
```
